32 devices in a mesh: dp: 16 (over z, y, x), ffn: 2 (over core).
Axes of the slice: x: 2, y: 2, z: 4, core: 2. Of those that a mesh axis runs over, the one named last changes fastest.
Arguments:
- states: bfloat16 [32768, 384], P('dp'), may hold values from -8 to 8
- teacher_states: bfloat16 [32768, 768], P('dp'), may hold values from -6 to 6
- lengths: int32 [32], P('dp'), may hold values from 128 to 1024
- domain_ids: int32 [32], P('dp'), may hold values from 0 to 7
- domain_weight: float32 [8], replicated, may hold values from 0.5 to 2
- teacher_qkv: bfloat16 [768, 3, 768], P(None, None, 'ffn'), may hold values from -0.21875 to 0.21875
- attn_a: float32 [384, 1536], P('dp'), may hold values from -0.8164966 to 0.8164966
- ffn_in: float32 [384, 1536], P('dp', 'ffn'), may hold values from -0.4082483 to 0.4082483
- ffn_out: float32 [384, 1536], P('dp', 'ffn'), may hold values from -0.15625 to 0.15625
- attn_b: float32 [384, 3, 384], P('dp', None, 'ffn'), may hold values from -0.3125 to 0.3125
- vec_d: float32 [384, 8], P('dp'), may hold values from -1.5 to 3
- mom1_attn_a: float32 [384, 1536], P('dp'), may hold values from -0.0004272461 to 0.0004272461
- mom1_ffn_in: float32 [384, 1536], P('dp', 'ffn'), may hold values from -0.0004272461 to 0.0004272461
- mom1_ffn_out: float32 [384, 1536], P('dp', 'ffn'), may hold values from -0.0004272461 to 0.0004272461
- mom1_attn_b: float32 [384, 3, 384], P('dp', None, 'ffn'), may hold values from -0.0004272461 to 0.0004272461
- mom1_vec_d: float32 [384, 8], P('dp'), may hold values from -0.001953125 to 0.001953125
- mom2_attn_a: float32 [384, 1536], P('dp'), may hold values from 2.257426e-10 to 3.6118817e-09
- mom2_ffn_in: float32 [384, 1536], P('dp', 'ffn'), may hold values from 2.257426e-10 to 3.6118817e-09
- mom2_ffn_out: float32 [384, 1536], P('dp', 'ffn'), may hold values from 2.257426e-10 to 3.6118817e-09
- mom2_attn_b: float32 [384, 3, 384], P('dp', None, 'ffn'), may hold values from 2.257426e-10 to 3.6118817e-09
- mom2_vec_d: float32 [384, 8], P('dp'), may hold values from 3.6118817e-09 to 5.643565e-08
Outputs:
- grad_norm: float32 [], replicated
- new_attn_a: float32 [384, 1536], P('dp')
- new_ffn_in: float32 [384, 1536], P('dp', 'ffn')
- new_ffn_out: float32 [384, 1536], P('dp', 'ffn')
- new_attn_b: float32 [384, 3, 384], P('dp', None, 'ffn')
- new_vec_d: float32 [384, 8], P('dp')
- out_mom1_attn_a: float32 [384, 1536], P('dp')
- out_mom1_ffn_in: float32 [384, 1536], P('dp', 'ffn')
- out_mom1_ffn_out: float32 [384, 1536], P('dp', 'ffn')
- out_mom1_attn_b: float32 [384, 3, 384], P('dp', None, 'ffn')
- out_mom1_vec_d: float32 [384, 8], P('dp')
- out_mom2_attn_a: float32 [384, 1536], P('dp')
- out_mom2_ffn_in: float32 [384, 1536], P('dp', 'ffn')
- out_mom2_ffn_out: float32 [384, 1536], P('dp', 'ffn')
- out_mom2_attn_b: float32 [384, 3, 384], P('dp', None, 'ffn')
- out_mom2_vec_d: float32 [384, 8], P('dp')
The draws below stay inside these ranges and needn't reach their ends.
All inputs are finite; a program needn't handle non-finite values.
Results may differ from the reference program's by a relative error of at most 0.0072.
Values may be sent and summed in bfloat16 or wider, within the bound.
No kernel may reach another device: no remote copies, remote signals or barrier semaphores. Data moves between devices by JAX's collectives and lax.ppermute only.
A program may use at most 320 MiB of HBM per device.

```python
import math
import jax
import jax.numpy as jnp
from jax import lax

D = 384
HEADS = 12
HEAD = 32
FF = 1536
TDIM = 768
THEAD = 64
LEN = 1024
DOMAINS = 8
STEP = 10
SEQS = 32
TOKENS = 32768
PARAMS = 2214912


def draw_states(key, part):
    key = jax.random.fold_in(key, 11)
    position = jnp.arange(D, dtype=jnp.float32) / (D - 1)
    values = jax.random.truncated_normal(key, -4.0, 4.0, (TOKENS, D), jnp.float32) * (0.6 + 1.2 * position)
    return values.astype(jnp.bfloat16)


def draw_attn_a(key, part):
    key = jax.random.fold_in(key, 12)
    columns = jnp.arange(4 * D)
    scaling = jnp.where(columns < 3 * D, 1.0, 4.0) * D ** (-0.5)
    return jax.random.truncated_normal(key, -4.0, 4.0, (D, 4 * D), jnp.float32) * scaling


def draw_ffn_in(key, part):
    key = jax.random.fold_in(key, 13)
    position = jnp.arange(FF, dtype=jnp.float32) / (FF - 1)
    scaling = (0.6 + 1.2 * position) * D ** (-0.5)
    return jax.random.truncated_normal(key, -4.0, 4.0, (D, FF), jnp.float32) * scaling


def draw_vec_d(key, part):
    key = jax.random.fold_in(key, 14)
    key_gain, key_shift = jax.random.split(key)
    position = jnp.arange(D, dtype=jnp.float32) / (D - 1)
    rising = 0.6 + 1.2 * position
    jitter = 0.1 * jax.random.truncated_normal(key_gain, -4.0, 4.0, (D, 8), jnp.float32)
    offsets = 0.3 * jax.random.truncated_normal(key_shift, -4.0, 4.0, (D, 8), jnp.float32)
    columns = jnp.arange(8)
    is_gain = (columns == 3) | (columns == 6)
    return jnp.where(is_gain[None, :], rising[:, None] * (1.0 + jitter), offsets)


def touch_ends(result, own_key, smallest, largest):
    dims = result.shape
    spot = [jax.random.randint(jax.random.fold_in(own_key, axis), (), 0, dims[axis]) for axis in range(len(dims))]
    result = result.at[tuple(spot)].set(smallest)
    longest = dims.index(max(dims))
    spot[longest] = (spot[longest] + 1) % dims[longest]
    return result.at[tuple(spot)].set(largest)


def shard_levels(rng, dims, pieces, least, high):
    factor_of = 1.0
    for dim, blocks in pieces:
        draws = jax.random.uniform(jax.random.fold_in(jax.random.fold_in(rng, 6), dim), (blocks,), jnp.float32, least / len(pieces), high / len(pieces))
        factor_of = factor_of * jnp.repeat(jnp.exp(draws), dims[dim] // blocks).reshape((-1,) + (1,) * (len(dims) - 1 - dim))
    return factor_of


def gaussian(key, dims, deviation, limit, cuts=(), kind=jnp.bfloat16):
    factor_of = shard_levels(key, dims, cuts, -0.22, 0.18) if cuts else 1.0
    entries = jax.random.normal(key, dims, jnp.float32) * deviation * factor_of
    return jnp.minimum(jnp.maximum(entries, -limit), limit).astype(kind)


def setup_inputs(seed: int = 0) -> dict:
    splits = jax.random.split(jax.random.key(seed), 22)
    states = draw_states(jax.random.fold_in(splits[21], 71), 0)
    teacher_states = gaussian(splits[1], (TOKENS, TDIM), 1.0, 6.0, ((0, 16),))
    lengths = touch_ends(jax.random.randint(splits[2], (SEQS,), LEN // 8, LEN + 1), jax.random.fold_in(splits[2], 1), LEN // 8, LEN).astype(jnp.int32)
    domain_ids = touch_ends(jax.random.randint(splits[3], (SEQS,), 0, DOMAINS), jax.random.fold_in(splits[3], 1), 0, DOMAINS - 1).astype(jnp.int32)
    domain_weight = jnp.clip(jnp.exp(jax.random.uniform(splits[4], (DOMAINS,), jnp.float32, math.log(0.5), math.log(2.0))), 0.5, 2.0)
    teacher_qkv = gaussian(splits[5], (TDIM, 3, TDIM), TDIM ** -0.5, 0.21875, ((2, 2),))
    attn_a = draw_attn_a(jax.random.fold_in(splits[21], 71), 0)
    ffn_in = draw_ffn_in(jax.random.fold_in(splits[21], 71), 0)
    ffn_out = gaussian(splits[8], (D, FF), FF ** -0.5, 0.15625, ((0, 16), (1, 2)), jnp.float32)
    attn_b = gaussian(splits[9], (D, 3, D), D ** -0.5, 0.3125, ((0, 16), (2, 2)), jnp.float32)
    vec_d = draw_vec_d(jax.random.fold_in(splits[21], 71), 0)
    mom1_attn_a = gaussian(splits[11], (D, 4 * D), ((83 * PARAMS) ** -0.5), 0.0004272461, ((0, 16),), jnp.float32)
    mom1_ffn_in = gaussian(splits[12], (D, FF), ((83 * PARAMS) ** -0.5), 0.0004272461, ((0, 16), (1, 2)), jnp.float32)
    mom1_ffn_out = gaussian(splits[13], (D, FF), ((83 * PARAMS) ** -0.5), 0.0004272461, ((0, 16), (1, 2)), jnp.float32)
    mom1_attn_b = gaussian(splits[14], (D, 3, D), ((83 * PARAMS) ** -0.5), 0.0004272461, ((0, 16), (2, 2)), jnp.float32)
    mom1_vec_d = gaussian(splits[15], (D, 8), ((5 * PARAMS) ** -0.5), 0.001953125, ((0, 16),), jnp.float32)
    mom2_attn_a = jnp.clip(jnp.exp(math.log(3.611881682630269e-09) - 2.7725887 * jax.random.uniform(splits[16], (D, 4 * D), jnp.float32) ** shard_levels(splits[16], (D, 4 * D), ((0, 16),), -0.2, 0.2)), 2.2574260516439182e-10, 3.611881682630269e-09)
    mom2_ffn_in = jnp.clip(jnp.exp(math.log(3.611881682630269e-09) - 2.7725887 * jax.random.uniform(splits[17], (D, FF), jnp.float32) ** shard_levels(splits[17], (D, FF), ((0, 16), (1, 2)), -0.2, 0.2)), 2.2574260516439182e-10, 3.611881682630269e-09)
    mom2_ffn_out = jnp.clip(jnp.exp(math.log(3.611881682630269e-09) - 2.7725887 * jax.random.uniform(splits[18], (D, FF), jnp.float32) ** shard_levels(splits[18], (D, FF), ((0, 16), (1, 2)), -0.2, 0.2)), 2.2574260516439182e-10, 3.611881682630269e-09)
    mom2_attn_b = jnp.clip(jnp.exp(math.log(3.611881682630269e-09) - 2.7725887 * jax.random.uniform(splits[19], (D, 3, D), jnp.float32) ** shard_levels(splits[19], (D, 3, D), ((0, 16), (2, 2)), -0.2, 0.2)), 2.2574260516439182e-10, 3.611881682630269e-09)
    mom2_vec_d = jnp.clip(jnp.exp(math.log(5.643564904289633e-08) - 2.748872 * jax.random.uniform(splits[20], (D, 8), jnp.float32) ** shard_levels(splits[20], (D, 8), ((0, 16),), -0.2, 0.2)), 3.611881682630269e-09, 5.643564904289633e-08)
    return {"states": states, "teacher_states": teacher_states, "lengths": lengths, "domain_ids": domain_ids, "domain_weight": domain_weight, "teacher_qkv": teacher_qkv, "attn_a": attn_a, "ffn_in": ffn_in, "ffn_out": ffn_out, "attn_b": attn_b, "vec_d": vec_d, "mom1_attn_a": mom1_attn_a, "mom1_ffn_in": mom1_ffn_in, "mom1_ffn_out": mom1_ffn_out, "mom1_attn_b": mom1_attn_b, "mom1_vec_d": mom1_vec_d, "mom2_attn_a": mom2_attn_a, "mom2_ffn_in": mom2_ffn_in, "mom2_ffn_out": mom2_ffn_out, "mom2_attn_b": mom2_attn_b, "mom2_vec_d": mom2_vec_d}


NORM_EPSILON = 1e-12
CLIP_NORM = 1.0
BETA_ONE = 0.9
BETA_TWO = 0.999
ADAM_EPSILON = 1e-08
RATE_MATRIX = 0.04
RATE_VECTOR = 0.2
DECAY_RATE = 0.01
MASK_VALUE = -1e+30

@jax.custom_vjp
def low(v):
    return lax.optimization_barrier(v.astype(jnp.bfloat16)).astype(jnp.float32)

@jax.custom_vjp
def low_back(v):
    return v

def low_keep(v):
    return (low(v), None)

def low_pass(kept, grad):
    return (grad,)

def back_keep(v):
    return (v, None)

def back_low(kept, grad):
    return (low(grad),)
low.defvjp(low_keep, low_pass)
low_back.defvjp(back_keep, back_low)

def round_both(value):
    return low(low_back(value))

def product(left, right):
    return jnp.dot(left, right, precision=lax.Precision.HIGHEST, preferred_element_type=jnp.float32)

def layer_norm(resid, gain, shift):
    centred = resid - lax.optimization_barrier(jnp.mean(resid, axis=-1, keepdims=True))
    inverse = lax.rsqrt(lax.optimization_barrier(jnp.mean(centred * centred, axis=-1, keepdims=True)) + NORM_EPSILON)
    return centred * inverse * gain + shift

def head_scores(left, right, head_size):
    return jnp.einsum('qhd,khd->hqk', left, right, precision=lax.Precision.HIGHEST) * head_size ** (-0.5)

def masked(scores, length):
    return jnp.where(jnp.arange(scores.shape[-1]) < length, scores, MASK_VALUE)

def divergence(student, teacher):
    target = jax.nn.softmax(teacher, axis=-1)
    return lax.optimization_barrier(jnp.sum(target * (jax.nn.log_softmax(teacher, axis=-1) - jax.nn.log_softmax(student, axis=-1)), axis=-1))

def sequence_loss(params, teacher_w, element):
    inputs, teacher_in, length, weight = element
    attn_a, ffn_in, ffn_out, attn_b, vec_d = [low(parameter) for parameter in params]
    query_bias, value_bias, output_bias, gain_one, shift_one, down_bias, gain_two, shift_two = [vec_d[:, column] for column in range(8)]
    query = round_both(product(inputs, attn_a[:, :D]) + query_bias).reshape(LEN, HEADS, HEAD)
    keys = round_both(product(inputs, attn_a[:, D:2 * D])).reshape(LEN, HEADS, HEAD)
    values = round_both(product(inputs, attn_a[:, 2 * D:3 * D]) + value_bias).reshape(LEN, HEADS, HEAD)
    probs = jax.nn.softmax(masked(low_back(head_scores(query, keys, HEAD)), length), axis=-1)
    mixed = round_both(jnp.einsum('hqk,khd->qhd', low(probs), values, precision=lax.Precision.HIGHEST).reshape(LEN, D))
    branch = low_back(product(mixed, attn_a[:, 3 * D:].T) + output_bias)
    hidden_one = layer_norm(inputs + branch, gain_one, shift_one)
    inner = low(jax.nn.gelu(low_back(product(low(hidden_one), ffn_in)), approximate=False))
    hidden_two = layer_norm(hidden_one + low_back(product(inner, ffn_out.T)) + down_bias, gain_two, shift_two)
    student = round_both(product(low(hidden_two), attn_b.reshape(D, 3 * D))).reshape(LEN, 3, HEADS, HEAD)
    teacher = low(product(teacher_in, teacher_w.reshape(TDIM, 3 * TDIM))).reshape(LEN, 3, HEADS, THEAD)
    row_weight = jnp.where(jnp.arange(LEN) < length, weight, 0.0)
    attention = divergence(masked(low_back(head_scores(student[:, 0], student[:, 1], HEAD)), length), masked(head_scores(teacher[:, 0], teacher[:, 1], THEAD), length))
    relation = divergence(masked(low_back(head_scores(student[:, 2], student[:, 2], HEAD)), length), masked(head_scores(teacher[:, 2], teacher[:, 2], THEAD), length))
    return jnp.sum((attention + relation) * row_weight[None, :])

def adam_update(weight, gradient, first, second, clipped, rate, decay):
    scaled = gradient * clipped
    first_new = BETA_ONE * first + (1.0 - BETA_ONE) * scaled
    second_new = BETA_TWO * second + (1.0 - BETA_TWO) * scaled * scaled
    ratio = first_new / (1.0 - BETA_ONE ** STEP) / (jnp.sqrt(second_new / (1.0 - BETA_TWO ** STEP)) + ADAM_EPSILON)
    return (weight - rate * (ratio + decay * weight), first_new, second_new)

def reference(states, teacher_states, lengths, domain_ids, domain_weight, teacher_qkv, attn_a, ffn_in, ffn_out, attn_b, vec_d, mom1_attn_a, mom1_ffn_in, mom1_ffn_out, mom1_attn_b, mom1_vec_d, mom2_attn_a, mom2_ffn_in, mom2_ffn_out, mom2_attn_b, mom2_vec_d):
    params = (attn_a, ffn_in, ffn_out, attn_b, vec_d)
    teacher_w = teacher_qkv.astype(jnp.float32)
    sequence_weight = domain_weight[domain_ids] / HEADS
    inputs = (states.astype(jnp.float32).reshape(SEQS, LEN, D), teacher_states.astype(jnp.float32).reshape(SEQS, LEN, TDIM), lengths, sequence_weight)
    checked = jax.checkpoint(sequence_loss)

    def total_loss(parameters):

        def scan_step(running, element):
            return (running + checked(parameters, teacher_w, element), None)
        loss_sum, unused = lax.scan(scan_step, jnp.zeros((), jnp.float32), inputs)
        return loss_sum
    loss_sum, pullback = jax.vjp(total_loss, params)
    gradients, = pullback(jnp.ones((), jnp.float32))
    squares = jnp.zeros((), jnp.float32)
    for gradient in gradients:
        squares = squares + jnp.sum(gradient * gradient)
    grad_norm = jnp.sqrt(squares)
    clipped = jnp.minimum(1.0, CLIP_NORM / grad_norm)
    firsts = (mom1_attn_a, mom1_ffn_in, mom1_ffn_out, mom1_attn_b, mom1_vec_d)
    seconds = (mom2_attn_a, mom2_ffn_in, mom2_ffn_out, mom2_attn_b, mom2_vec_d)
    rates = (RATE_MATRIX, RATE_MATRIX, RATE_MATRIX, RATE_MATRIX, RATE_VECTOR)
    decays = (DECAY_RATE, DECAY_RATE, DECAY_RATE, DECAY_RATE, 0.0)
    news = [adam_update(params[number], gradients[number], firsts[number], seconds[number], clipped, rates[number], decays[number]) for number in range(5)]
    return (grad_norm, news[0][0], news[1][0], news[2][0], news[3][0], news[4][0], news[0][1], news[1][1], news[2][1], news[3][1], news[4][1], news[0][2], news[1][2], news[2][2], news[3][2], news[4][2])
```

```python
import functools

import jax
import jax.numpy as jnp
from jax import lax
from jax.experimental import pallas as pl
from jax.experimental.pallas import tpu as pltpu
from jax.sharding import PartitionSpec as P

HEADS = 12
STEP = 10

NORM_EPSILON = 1e-12
CLIP_NORM = 1.0
BETA_ONE = 0.9
BETA_TWO = 0.999
ADAM_EPSILON = 1e-08
RATE_MATRIX = 0.04
RATE_VECTOR = 0.2
DECAY_RATE = 0.01
MASK_VALUE = -1e30
LOG2_E = 1.4426950408889634
BLOCK = 256
VMEM_BYTES = 56 * 2**20
F32 = jnp.float32
BF16 = jnp.bfloat16


def nn(left, right):
    return lax.dot_general(left, right, (((1,), (0,)), ((), ())), preferred_element_type=F32)


def nt(left, right):
    return lax.dot_general(left, right, (((1,), (1,)), ((), ())), preferred_element_type=F32)


def tn(left, right):
    return lax.dot_general(left, right, (((0,), (0,)), ((), ())), preferred_element_type=F32)


def lanes(block):
    return pl.ds(pl.multiple_of(block * BLOCK, BLOCK), BLOCK)


def live_blocks(len_ref):
    return (len_ref[0] + BLOCK - 1) // BLOCK


def for_size(blocks, most, body):
    for n in range(1, most + 1):
        pl.when(blocks == n)(functools.partial(body, n))


def norm_forward(resid):
    features = resid.shape[0]
    centred = resid - jnp.sum(resid, axis=0, keepdims=True) * (1.0 / features)
    variance = jnp.sum(centred * centred, axis=0, keepdims=True) * (1.0 / features)
    inverse = lax.rsqrt(variance + NORM_EPSILON)
    return centred * inverse, inverse


def norm_backward(scaled, normed, inverse):
    features = scaled.shape[0]
    mean = jnp.sum(scaled, axis=0, keepdims=True) * (1.0 / features)
    slope = jnp.sum(scaled * normed, axis=0, keepdims=True) * (1.0 / features)
    return inverse * (scaled - mean - normed * slope)


def mask_tail(scores, n, length):
    rows = (n - 1) * BLOCK + lax.broadcasted_iota(jnp.int32, (BLOCK, scores.shape[1]), 0)
    tail = jnp.where(rows < length, scores[(n - 1) * BLOCK :], MASK_VALUE)
    if n == 1:
        return tail
    return jnp.concatenate([scores[: (n - 1) * BLOCK], tail], axis=0)


def pad_rows(part, index, count):
    zeros = jnp.zeros_like(part)
    return jnp.concatenate([part if i == index else zeros for i in range(count)], axis=0)


def pad_lanes(pair, index, size):
    lane = lax.broadcasted_iota(jnp.int32, pair.shape, 1)
    return jnp.where((lane >= index * size) & (lane < (index + 1) * size), pair, jnp.zeros_like(pair))


def split_heads(flat, ref, columns, size):
    heads = flat.shape[0] // size
    for head in range(heads):
        ref[head, :, columns] = flat[head * size : (head + 1) * size]


def split_pairs(flat, ref, rows):
    pairs, width = ref.shape[0], ref.shape[2]
    for pair in range(pairs):
        ref[pair, rows, :] = flat[pair * width : (pair + 1) * width].T


def teacher_kernel(len_ref, rows_ref, weight_ref, qt_ref, k_ref, vt_ref, v_ref):
    flat = weight_ref.shape[0] // 3
    size = qt_ref.shape[1]

    def step(block, carry):
        where = lanes(block)
        rows = rows_ref[where, :]
        projected = nt(weight_ref[...], rows).astype(BF16)
        split_heads(projected[:flat], qt_ref, where, size)
        split_pairs(projected[flat : 2 * flat], k_ref, where)
        split_heads(projected[2 * flat :], vt_ref, where, size)
        split_pairs(projected[2 * flat :], v_ref, where)
        return carry

    lax.fori_loop(0, live_blocks(len_ref), step, 0)


def attend_kernel(
    len_ref, xt_ref, weight_ref, vec_ref, qt_ref, kt_ref, vt_ref, q_ref, k_ref, v_ref, ot_ref, lse_ref, at_ref,
    vone_ref,
):
    heads, size, rows = qt_ref.shape
    flat = heads * size
    scaling = LOG2_E * size ** (-0.5)
    blocks = live_blocks(len_ref)
    length = len_ref[0]
    vone_ref[...] = jnp.ones(vone_ref.shape, BF16)

    def project(block, carry):
        where = lanes(block)
        xt = xt_ref[:, where]
        projected = tn(weight_ref[:, : 3 * flat], xt)
        query = (projected[:flat] + vec_ref[:, 0:1]).astype(BF16)
        keys = projected[flat : 2 * flat].astype(BF16)
        values = (projected[2 * flat :] + vec_ref[:, 1:2]).astype(BF16)
        split_heads(query, qt_ref, where, size)
        split_heads(keys, kt_ref, where, size)
        split_heads(values, vt_ref, where, size)
        for head in range(heads):
            vone_ref[head, :size, where] = values[head * size : (head + 1) * size]
        split_pairs(query, q_ref, where)
        split_pairs(keys, k_ref, where)
        split_pairs(values, v_ref, where)
        return carry

    lax.fori_loop(0, blocks, project, 0)

    def attend(n):
        def step(index, carry):
            block, pair = index // (heads // 2), index % (heads // 2)
            where = lanes(block)
            keys = k_ref[pair, : n * BLOCK, :]
            for half in range(2):
                head = 2 * pair + half
                scores = nn(keys, pad_rows(qt_ref[head, :, where], half, 2))
                scores = mask_tail(scores, n, length)
                top = jnp.max(scores, axis=0, keepdims=True) * scaling
                grown = jnp.exp2(scores * scaling - top).astype(BF16)
                mixed = nn(vone_ref[head, :, : n * BLOCK], grown)
                total = mixed[size : size + 1]
                ot_ref[head, :, where] = mixed[:size] * (1.0 / total)
                lse_ref[head, :, where] = jnp.broadcast_to(top + jnp.log2(total), (8, BLOCK))
            return carry

        lax.fori_loop(0, n * (heads // 2), step, 0)

    for_size(blocks, rows // BLOCK, attend)

    def output(block, carry):
        where = lanes(block)
        mixed = ot_ref[:, :, where].reshape(flat, BLOCK).astype(BF16)
        at_ref[:, where] = nn(weight_ref[:, 3 * flat :], mixed).astype(BF16)
        return carry

    lax.fori_loop(0, blocks, output, 0)


def first_norm(xt, own, other, vec_ref):
    resid = xt.astype(F32) + (own.astype(F32) + other.astype(F32)) + vec_ref[:, 2:3]
    return norm_forward(resid)


def erf(value):
    return lax.erf(value)


def feed_kernel(len_ref, xt_ref, own_ref, other_ref, in_ref, out_ref, vec_ref, ht_ref, zt_ref, slope_ref, ft_ref):
    def step(block, carry):
        where = lanes(block)
        normed, _ = first_norm(xt_ref[:, where], own_ref[:, where], other_ref[:, where], vec_ref)
        hidden = normed * vec_ref[:, 3:4] + vec_ref[:, 4:5]
        ht_ref[:, where] = hidden
        pre = tn(in_ref[...], hidden.astype(BF16))
        cdf = 0.5 + 0.5 * erf(pre * (0.5**0.5))
        pdf = jnp.exp2(pre * pre * (-0.5 * LOG2_E)) * 0.3989422804014327
        active = (pre * cdf).astype(BF16)
        zt_ref[:, where] = active
        slope_ref[:, where] = (cdf + pre * pdf).astype(BF16)
        ft_ref[:, where] = nn(out_ref[...], active).astype(BF16)
        return carry

    lax.fori_loop(0, live_blocks(len_ref), step, 0)


def second_norm(ht, own, other, vec_ref):
    resid = ht + (own.astype(F32) + other.astype(F32)) + vec_ref[:, 5:6]
    return norm_forward(resid)


def relation_kernel(
    len_ref, weight_ref, ht_ref, own_ref, other_ref, rel_ref, vec_ref, tqt_ref, tk_ref, tvt_ref, tv_ref,
    grad_ref, dt_ref,
    h2_ref, qt_ref, kt_ref, vt_ref, q_ref, k_ref, v_ref, dqt_ref, dvt_ref, dk_ref, dv_ref,
):
    heads, size, rows = qt_ref.shape
    teacher_size = tqt_ref.shape[1]
    flat = heads * size
    plain = size ** (-0.5)
    scaling = LOG2_E * plain
    teacher_scaling = LOG2_E * teacher_size ** (-0.5)
    blocks = live_blocks(len_ref)
    length = len_ref[0]
    weight = weight_ref[0]

    def project(block, carry):
        where = lanes(block)
        normed, _ = second_norm(ht_ref[:, where], own_ref[:, where], other_ref[:, where], vec_ref)
        hidden = (normed * vec_ref[:, 6:7] + vec_ref[:, 7:8]).astype(BF16)
        h2_ref[:, where] = hidden
        projected = tn(rel_ref[...], hidden).astype(BF16)
        split_heads(projected[:flat], qt_ref, where, size)
        split_heads(projected[flat : 2 * flat], kt_ref, where, size)
        split_heads(projected[2 * flat :], vt_ref, where, size)
        split_pairs(projected[:flat], q_ref, where)
        split_pairs(projected[flat : 2 * flat], k_ref, where)
        split_pairs(projected[2 * flat :], v_ref, where)
        for pair in range(heads // 2):
            dk_ref[pair, where, :] = jnp.zeros((BLOCK, 2 * size), F32)
            dv_ref[pair, where, :] = jnp.zeros((BLOCK, 2 * size), F32)
        return carry

    lax.fori_loop(0, blocks, project, 0)

    def relate(n):
        def grown(left, right, scale):
            scores = mask_tail(nn(left, right), n, length)
            top = jnp.max(scores, axis=0, keepdims=True) * scale
            result = jnp.exp2(scores * scale - top)
            return result, jnp.sum(result, axis=0, keepdims=True)

        def step(index, carry):
            block, pair = index // (heads // 2), index % (heads // 2)
            where = lanes(block)
            column = block * BLOCK + lax.broadcasted_iota(jnp.int32, (1, BLOCK), 1)
            live = jnp.where(column < length, weight, 0.0)

            def relation(left, rightt, right, teacher_left, teacher_rightt, leftt, own_ref, running_ref):
                grads = []
                for half in range(2):
                    head = 2 * pair + half
                    student, student_sum = grown(
                        left[pair, : n * BLOCK, :], pad_rows(rightt[head, :, where], half, 2), scaling
                    )
                    teacher, teacher_sum = grown(
                        teacher_left[pair, : n * BLOCK, :],
                        pad_rows(teacher_rightt[head, :, where], half, 2),
                        teacher_scaling,
                    )
                    grad = (student * (live / student_sum) - teacher * (live / teacher_sum)).astype(BF16)
                    own_ref[head, :, where] = (nn(leftt[head, :, : n * BLOCK], grad) * plain).astype(own_ref.dtype)
                    grads.append(grad)
                queries = right[pair, where, :]
                stacked = jnp.concatenate([pad_lanes(queries, half, size) for half in range(2)], axis=0)
                running_ref[pair, : n * BLOCK, :] += nn(jnp.concatenate(grads, axis=1), stacked)

            relation(k_ref, qt_ref, q_ref, tk_ref, tqt_ref, kt_ref, dqt_ref, dk_ref)
            relation(v_ref, vt_ref, v_ref, tv_ref, tvt_ref, vt_ref, dvt_ref, dv_ref)
            return carry

        lax.fori_loop(0, n * (heads // 2), step, 0)

    for_size(blocks, rows // BLOCK, relate)
    grad_ref[...] = jnp.zeros(grad_ref.shape, F32)

    def finish(block, carry):
        where = lanes(block)
        queries = dqt_ref[:, :, where].reshape(flat, BLOCK)
        keys = jnp.concatenate([dk_ref[pair, where, :].T for pair in range(heads // 2)], axis=0) * plain
        values = jnp.concatenate([dv_ref[pair, where, :].T for pair in range(heads // 2)], axis=0) * plain
        values = values + dvt_ref[:, :, where].reshape(flat, BLOCK)
        grads = jnp.concatenate([queries, keys.astype(BF16), values.astype(BF16)], axis=0)
        grad_ref[...] += nt(h2_ref[:, where], grads)
        dt_ref[:, where] = nn(rel_ref[...], grads).astype(BF16)
        return carry

    lax.fori_loop(0, blocks, finish, 0)


def feed_back_kernel(
    len_ref, ht_ref, own_ref, other_ref, down_own_ref, down_other_ref, zt_ref, slope_ref, in_ref, out_ref, vec_ref,
    grad_in_ref, grad_out_ref, sums_ref, resid_ref, up_ref,
):
    grad_in_ref[...] = jnp.zeros(grad_in_ref.shape, F32)
    grad_out_ref[...] = jnp.zeros(grad_out_ref.shape, F32)
    sums_ref[...] = jnp.zeros(sums_ref.shape, F32)

    def step(block, carry):
        where = lanes(block)
        hidden = ht_ref[:, where]
        normed, inverse = second_norm(hidden, own_ref[:, where], other_ref[:, where], vec_ref)
        grad = down_own_ref[:, where].astype(F32) + down_other_ref[:, where].astype(F32)
        resid = norm_backward(grad * vec_ref[:, 6:7], normed, inverse)
        resid_ref[:, where] = resid
        sums_ref[:, 0:1] += jnp.sum(resid, axis=1, keepdims=True)
        sums_ref[:, 1:2] += jnp.sum(grad * normed, axis=1, keepdims=True)
        sums_ref[:, 2:3] += jnp.sum(grad, axis=1, keepdims=True)
        branch = resid.astype(BF16)
        grad_out_ref[...] += nt(branch, zt_ref[:, where])
        pre_grad = (tn(out_ref[...], branch) * slope_ref[:, where].astype(F32)).astype(BF16)
        grad_in_ref[...] += nt(hidden.astype(BF16), pre_grad)
        up_ref[:, where] = nn(in_ref[...], pre_grad).astype(BF16)
        return carry

    lax.fori_loop(0, live_blocks(len_ref), step, 0)


def attend_back_kernel(
    len_ref, xt_ref, own_ref, other_ref, resid_ref, up_own_ref, up_other_ref, weight_ref, vec_ref,
    qt_ref, kt_ref, q_ref, k_ref, v_ref, ot_ref, lse_ref,
    grad_ref, sums_ref, head_sums_ref,
    dot_ref, do_ref, inner_ref, dqt_ref, dk_ref, dv_ref,
):
    heads, size, rows = qt_ref.shape
    flat = heads * size
    plain = size ** (-0.5)
    scaling = LOG2_E * plain
    blocks = live_blocks(len_ref)
    length = len_ref[0]
    sums_ref[...] = jnp.zeros(sums_ref.shape, F32)
    head_sums_ref[...] = jnp.zeros(head_sums_ref.shape, F32)
    grad_ref[...] = jnp.zeros(grad_ref.shape, F32)

    def start(block, carry):
        where = lanes(block)
        normed, inverse = first_norm(xt_ref[:, where], own_ref[:, where], other_ref[:, where], vec_ref)
        grad = resid_ref[:, where] + (up_own_ref[:, where].astype(F32) + up_other_ref[:, where].astype(F32))
        branch = norm_backward(grad * vec_ref[:, 3:4], normed, inverse).astype(BF16)
        sums_ref[:, 0:1] += jnp.sum(branch.astype(F32), axis=1, keepdims=True)
        sums_ref[:, 1:2] += jnp.sum(grad * normed, axis=1, keepdims=True)
        sums_ref[:, 2:3] += jnp.sum(grad, axis=1, keepdims=True)
        mixed = ot_ref[:, :, where]
        grad_ref[:, 3 * flat :] += nt(branch, mixed.reshape(flat, BLOCK).astype(BF16))
        mixed_grad = tn(weight_ref[:, 3 * flat :], branch).astype(BF16)
        split_heads(mixed_grad, dot_ref, where, size)
        split_pairs(mixed_grad, do_ref, where)
        for head in range(heads):
            product = mixed_grad[head * size : (head + 1) * size].astype(F32) * mixed[head]
            inner_ref[head, :, where] = jnp.broadcast_to(jnp.sum(product, axis=0, keepdims=True), (8, BLOCK))
        for pair in range(heads // 2):
            dk_ref[pair, where, :] = jnp.zeros((BLOCK, 2 * size), F32)
            dv_ref[pair, where, :] = jnp.zeros((BLOCK, 2 * size), F32)
        return carry

    lax.fori_loop(0, blocks, start, 0)

    def attend(n):
        def step(index, carry):
            block, pair = index // (heads // 2), index % (heads // 2)
            where = lanes(block)
            probs, grads = [], []
            for half in range(2):
                head = 2 * pair + half
                scores = mask_tail(nn(k_ref[pair, : n * BLOCK, :], pad_rows(qt_ref[head, :, where], half, 2)), n, length)
                prob = jnp.exp2(scores * scaling - lse_ref[head, 0:1, where])
                prob_grad = nn(v_ref[pair, : n * BLOCK, :], pad_rows(dot_ref[head, :, where], half, 2))
                grad = (prob * (prob_grad - inner_ref[head, 0:1, where])).astype(BF16)
                dqt_ref[head, :, where] = (nn(kt_ref[head, :, : n * BLOCK], grad) * plain).astype(BF16)
                probs.append(prob.astype(BF16))
                grads.append(grad)
            for parts, right, running in ((grads, q_ref, dk_ref), (probs, do_ref, dv_ref)):
                queries = right[pair, where, :]
                stacked = jnp.concatenate([pad_lanes(queries, half, size) for half in range(2)], axis=0)
                running[pair, : n * BLOCK, :] += nn(jnp.concatenate(parts, axis=1), stacked)
            return carry

        lax.fori_loop(0, n * (heads // 2), step, 0)

    for_size(blocks, rows // BLOCK, attend)

    def finish(block, carry):
        where = lanes(block)
        queries = dqt_ref[:, :, where].reshape(flat, BLOCK)
        keys = jnp.concatenate([dk_ref[pair, where, :].T for pair in range(heads // 2)], axis=0) * plain
        values = jnp.concatenate([dv_ref[pair, where, :].T for pair in range(heads // 2)], axis=0).astype(BF16)
        head_sums_ref[:, 0:1] += jnp.sum(queries.astype(F32), axis=1, keepdims=True)
        head_sums_ref[:, 1:2] += jnp.sum(values.astype(F32), axis=1, keepdims=True)
        grads = jnp.concatenate([queries, keys.astype(BF16), values], axis=0)
        grad_ref[:, : 3 * flat] += nt(xt_ref[:, where], grads)
        return carry

    lax.fori_loop(0, blocks, finish, 0)


def call(kernel, name, scalars, arrays, outs, scratch=(), flops=0):
    vmem = pl.BlockSpec(memory_space=pltpu.VMEM)
    smem = pl.BlockSpec(memory_space=pltpu.SMEM)
    return pl.pallas_call(
        kernel,
        name=name,
        out_shape=tuple(jax.ShapeDtypeStruct(shape, dtype) for shape, dtype in outs),
        in_specs=[smem] * len(scalars) + [vmem] * len(arrays),
        out_specs=tuple(vmem for _ in outs),
        scratch_shapes=[pltpu.VMEM(shape, dtype) for shape, dtype in scratch],
        compiler_params=pltpu.CompilerParams(vmem_limit_bytes=VMEM_BYTES),
        cost_estimate=pl.CostEstimate(flops=flops, bytes_accessed=4 << 20, transcendentals=0),
    )(*scalars, *arrays)


def exchange(part):
    cores = lax.axis_size("ffn")
    return lax.ppermute(part, "ffn", [(core, core ^ 1) for core in range(cores)])


def adam_update(weight, gradient, first, second, clipped, rate, decay):
    scaled = gradient * clipped
    first_new = BETA_ONE * first + (1.0 - BETA_ONE) * scaled
    second_new = BETA_TWO * second + (1.0 - BETA_TWO) * scaled * scaled
    ratio = (
        first_new
        / (1.0 - BETA_ONE**STEP)
        / (jnp.sqrt(second_new / (1.0 - BETA_TWO**STEP)) + ADAM_EPSILON)
    )
    return (weight - rate * (ratio + decay * weight), first_new, second_new)


def per_device(
    states, teacher_states, lengths, domain_ids, domain_weight, teacher_qkv,
    attn_a, ffn_in, ffn_out, attn_b, vec_d,
    mom1_attn_a, mom1_ffn_in, mom1_ffn_out, mom1_attn_b, mom1_vec_d,
    mom2_attn_a, mom2_ffn_in, mom2_ffn_out, mom2_attn_b, mom2_vec_d,
):
    cores = lax.axis_size("ffn")
    core = lax.axis_index("ffn")
    replicas = lax.axis_size("dp")
    replica = lax.axis_index("dp")
    sequences = lengths.shape[0]
    rows = states.shape[0] // sequences
    features = states.shape[1]
    heads = HEADS // cores
    flat = features // cores
    size = flat // heads
    pairs = heads // 2
    hidden = ffn_in.shape[1]
    teacher_flat = teacher_qkv.shape[2]
    teacher_size = teacher_flat // heads
    shard = attn_a.shape[0]
    matched = domain_ids[:, None] == jnp.arange(domain_weight.shape[0])[None, :]
    sequence_weight = jnp.sum(jnp.where(matched, domain_weight[None, :], 0.0), axis=1) / HEADS

    attn_own = lax.dynamic_slice_in_dim(attn_a.reshape(shard, 4, features), core * flat, flat, 2).reshape(shard, 4 * flat)
    attn_full = lax.all_gather(attn_own.astype(BF16), "dp", axis=0, tiled=True)
    in_full = lax.all_gather(ffn_in.astype(BF16), "dp", axis=0, tiled=True)
    out_full = lax.all_gather(ffn_out.astype(BF16), "dp", axis=0, tiled=True)
    rel_full = lax.all_gather(attn_b.astype(BF16).reshape(shard, 3 * flat), "dp", axis=0, tiled=True)
    vec_full = lax.all_gather(vec_d.astype(BF16), "dp", axis=0, tiled=True).astype(F32)
    vec_own = lax.dynamic_slice_in_dim(vec_full, core * flat, flat, 0)
    teacher_w = teacher_qkv.reshape(teacher_qkv.shape[0], -1).T
    statest = states.T

    live = [lengths[i : i + 1] for i in range(sequences)]
    weights = [sequence_weight[i : i + 1] for i in range(sequences)]
    xt = [statest[:, i * rows : (i + 1) * rows] for i in range(sequences)]
    each = range(sequences)
    act = ((features, rows), BF16)
    wide = ((features, rows), F32)
    head_t = ((heads, size, rows), BF16)
    pair_rows = ((pairs, rows, 2 * size), BF16)

    teacher = [
        call(
            teacher_kernel, "teacher", (live[i],),
            (teacher_states[i * rows : (i + 1) * rows], teacher_w),
            (
                ((heads, teacher_size, rows), BF16),
                ((pairs, rows, 2 * teacher_size), BF16),
                ((heads, teacher_size, rows), BF16),
                ((pairs, rows, 2 * teacher_size), BF16),
            ),
            flops=2 * rows * 768 * 1152,
        )
        for i in each
    ]
    attended = [
        call(
            attend_kernel, "attend", (live[i],), (xt[i], attn_full, vec_own),
            (head_t, head_t, head_t, pair_rows, pair_rows, pair_rows, ((heads, size, rows), F32),
             ((heads, 8, rows), F32), act),
            scratch=(((heads, size + 16, rows), BF16),),
            flops=6 * 10**9,
        )
        for i in each
    ]
    mixed_other = [exchange(attended[i][8]) for i in each]
    fed = [
        call(
            feed_kernel, "feed", (live[i],),
            (xt[i], attended[i][8], mixed_other[i], in_full, out_full, vec_full),
            (wide, ((hidden, rows), BF16), ((hidden, rows), BF16), act),
            flops=3 * 10**9,
        )
        for i in each
    ]
    fed_other = [exchange(fed[i][3]) for i in each]
    related = [
        call(
            relation_kernel, "relation", (live[i], weights[i]),
            (fed[i][0], fed[i][3], fed_other[i], rel_full, vec_full, *teacher[i]),
            (((features, 3 * flat), F32), act),
            scratch=(
                act, head_t, head_t, head_t, pair_rows, pair_rows, pair_rows,
                head_t, ((heads, size, rows), F32),
                ((pairs, rows, 2 * size), F32), ((pairs, rows, 2 * size), F32),
            ),
            flops=30 * 10**9,
        )
        for i in each
    ]
    down_other = [exchange(related[i][1]) for i in each]
    fed_back = [
        call(
            feed_back_kernel, "feed_back", (live[i],),
            (fed[i][0], fed[i][3], fed_other[i], related[i][1], down_other[i], fed[i][1], fed[i][2],
             in_full, out_full, vec_full),
            (((features, hidden), F32), ((features, hidden), F32), ((features, 8), F32), wide, act),
            flops=4 * 10**9,
        )
        for i in each
    ]
    up_other = [exchange(fed_back[i][4]) for i in each]
    attended_back = [
        call(
            attend_back_kernel, "attend_back", (live[i],),
            (xt[i], attended[i][8], mixed_other[i], fed_back[i][3], fed_back[i][4], up_other[i], attn_full, vec_full,
             attended[i][0], attended[i][1], attended[i][3], attended[i][4], attended[i][5], attended[i][6],
             attended[i][7]),
            (((features, 4 * flat), F32), ((features, 8), F32), ((flat, 8), F32)),
            scratch=(
                head_t, pair_rows, ((heads, 8, rows), F32), head_t,
                ((pairs, rows, 2 * size), F32), ((pairs, rows, 2 * size), F32),
            ),
            flops=15 * 10**9,
        )
        for i in each
    ]

    def total(parts):
        result = parts[0]
        for part in parts[1:]:
            result = result + part
        return result

    def scatter(value):
        return lax.psum_scatter(value, "dp", scatter_dimension=0, tiled=True)

    shard_rel = scatter(total([related[i][0] for i in each]))
    shard_in = scatter(total([fed_back[i][0] for i in each]))
    shard_out = scatter(total([fed_back[i][1] for i in each]))
    shard_attn = scatter(total([attended_back[i][0] for i in each]))
    back_sums = total([fed_back[i][2] for i in each])
    first_sums = total([attended_back[i][1] for i in each])
    head_sums = total([attended_back[i][2] for i in each])
    placed = lax.dynamic_update_slice_in_dim(jnp.zeros((features, 2), F32), head_sums[:, :2] * cores, core * flat, 0)
    vec_local = jnp.concatenate(
        [placed, first_sums[:, :3], back_sums[:, :3]], axis=1
    )
    vec_total = lax.psum(vec_local, ("dp", "ffn")) / cores
    grad_vec = lax.dynamic_slice_in_dim(vec_total, replica * shard, shard, 0)
    halves = lax.all_gather(shard_attn.reshape(shard, 4, flat), "ffn", axis=2, tiled=True)
    grad_attn = halves.reshape(shard, 4 * features)
    grad_rel = shard_rel.reshape(attn_b.shape)
    gradients = (grad_attn, shard_in, shard_out, grad_rel, grad_vec)
    squares = (
        (jnp.sum(grad_attn * grad_attn) + jnp.sum(grad_vec * grad_vec)) / cores
        + jnp.sum(shard_in * shard_in)
        + jnp.sum(shard_out * shard_out)
        + jnp.sum(shard_rel * shard_rel)
    )
    grad_norm = jnp.sqrt(lax.psum(squares, ("dp", "ffn")))
    clipped = jnp.minimum(1.0, CLIP_NORM / grad_norm)
    masters = (attn_a, ffn_in, ffn_out, attn_b, vec_d)
    firsts = (mom1_attn_a, mom1_ffn_in, mom1_ffn_out, mom1_attn_b, mom1_vec_d)
    seconds = (mom2_attn_a, mom2_ffn_in, mom2_ffn_out, mom2_attn_b, mom2_vec_d)
    rates = (RATE_MATRIX, RATE_MATRIX, RATE_MATRIX, RATE_MATRIX, RATE_VECTOR)
    decays = (DECAY_RATE, DECAY_RATE, DECAY_RATE, DECAY_RATE, 0.0)
    news = [
        adam_update(masters[i], gradients[i], firsts[i], seconds[i], clipped, rates[i], decays[i])
        for i in range(5)
    ]
    return (grad_norm, *(new[0] for new in news), *(new[1] for new in news), *(new[2] for new in news))


def solution(mesh):
    matrix = P("dp", None)
    halved = P("dp", "ffn")
    cube = P("dp", None, "ffn")
    trained = (matrix, halved, halved, cube, matrix)
    in_specs = (matrix, matrix, P("dp"), P("dp"), P(), P(None, None, "ffn")) + trained * 3
    out_specs = (P(),) + trained * 3
    return jax.shard_map(per_device, mesh=mesh, in_specs=in_specs, out_specs=out_specs, check_vma=False)
```

```python
import functools

import jax
import jax.numpy as jnp
from jax import lax
from jax.experimental import pallas as pl
from jax.experimental.pallas import tpu as pltpu
from jax.sharding import PartitionSpec as P

HEADS = 12
STEP = 10

NORM_EPSILON = 1e-12
CLIP_NORM = 1.0
BETA_ONE = 0.9
BETA_TWO = 0.999
ADAM_EPSILON = 1e-08
RATE_MATRIX = 0.04
RATE_VECTOR = 0.2
DECAY_RATE = 0.01
MASK_VALUE = -1e30
LOG2_E = 1.4426950408889634
BLOCK = 256
SAFE_EXPONENT = 100.0
VMEM_BYTES = 56 * 2**20
F32 = jnp.float32
BF16 = jnp.bfloat16


def nn(left, right):
    return lax.dot_general(left, right, (((1,), (0,)), ((), ())), preferred_element_type=F32)


def nt(left, right):
    return lax.dot_general(left, right, (((1,), (1,)), ((), ())), preferred_element_type=F32)


def tn(left, right):
    return lax.dot_general(left, right, (((0,), (0,)), ((), ())), preferred_element_type=F32)


def lanes(block):
    return pl.ds(pl.multiple_of(block * BLOCK, BLOCK), BLOCK)


def live_blocks(len_ref):
    return (len_ref[0] + BLOCK - 1) // BLOCK


def for_size(blocks, most, safe, fast, slow):
    for n in range(1, most + 1):
        pl.when(jnp.logical_and(safe, blocks == n))(functools.partial(fast, n))
    pl.when(jnp.logical_not(safe))(slow)


def pipeline(count, first, second, third):
    firsts, seconds = {}, {}
    for t in range(count + 2):
        if t < count:
            firsts[t] = first(t)
        if 0 <= t - 1 < count:
            seconds[t - 1] = second(t - 1, firsts.pop(t - 1))
        if 0 <= t - 2 < count:
            third(t - 2, seconds.pop(t - 2))


def squared_lengths(flat, size):
    features = flat.shape[0]
    groups = -(-features // size // 8) * 8
    row = lax.broadcasted_iota(jnp.int32, (groups, features), 0)
    column = lax.broadcasted_iota(jnp.int32, (groups, features), 1)
    ones = jnp.where((column >= row * size) & (column < (row + 1) * size), 1.0, 0.0).astype(BF16)
    return nn(ones, flat * flat)


def clear_dead(blocks, rows, *refs):
    def step(block, carry):
        for ref in refs:
            ref[:, :, lanes(block)] = jnp.zeros(ref.shape[:2] + (BLOCK,), ref.dtype)
        return carry

    lax.fori_loop(blocks, rows // BLOCK, step, 0)


def norm_forward(resid):
    features = resid.shape[0]
    centred = resid - jnp.sum(resid, axis=0, keepdims=True) * (1.0 / features)
    variance = jnp.sum(centred * centred, axis=0, keepdims=True) * (1.0 / features)
    inverse = lax.rsqrt(variance + NORM_EPSILON)
    return centred * inverse, inverse


def norm_backward(scaled, normed, inverse):
    features = scaled.shape[0]
    mean = jnp.sum(scaled, axis=0, keepdims=True) * (1.0 / features)
    slope = jnp.sum(scaled * normed, axis=0, keepdims=True) * (1.0 / features)
    return inverse * (scaled - mean - normed * slope)


def mask_tail(scores, n, length, start=None):
    start = (n - 1) * BLOCK if start is None else start
    rows = start + lax.broadcasted_iota(jnp.int32, (n * BLOCK - start, scores.shape[1]), 0)
    tail = jnp.where(rows < length, scores[start:], MASK_VALUE)
    if start == 0:
        return tail
    return jnp.concatenate([scores[:start], tail], axis=0)


def pad_rows(part, index, count):
    zeros = jnp.zeros_like(part)
    return jnp.concatenate([part if i == index else zeros for i in range(count)], axis=0)


def pad_lanes(pair, index, size):
    lane = lax.broadcasted_iota(jnp.int32, pair.shape, 1)
    return jnp.where((lane >= index * size) & (lane < (index + 1) * size), pair, jnp.zeros_like(pair))


def split_heads(flat, ref, columns, size):
    heads = flat.shape[0] // size
    for head in range(heads):
        ref[head, :, columns] = flat[head * size : (head + 1) * size]


def split_pairs(flat, ref, rows):
    pairs, width = ref.shape[0], ref.shape[2]
    for pair in range(pairs):
        ref[pair, rows, :] = flat[pair * width : (pair + 1) * width].T


def teacher_kernel(traffic, len_ref, rows_ref, weight_ref, qt_ref, k_ref, vt_ref, v_ref, bound_ref):
    flat = weight_ref.shape[0] // 3
    size = qt_ref.shape[1]
    bound_ref[...] = jnp.zeros(bound_ref.shape, F32)

    def step(block, carry):
        where = lanes(block)
        traffic.take(block)
        rows = rows_ref[where, :]
        projected = nt(weight_ref[...], rows).astype(BF16)
        bound_ref[...] = jnp.maximum(bound_ref[...], squared_lengths(projected, size))
        split_heads(projected[:flat], qt_ref, where, size)
        split_pairs(projected[flat : 2 * flat], k_ref, where)
        split_heads(projected[2 * flat :], vt_ref, where, size)
        split_pairs(projected[2 * flat :], v_ref, where)
        traffic.give(block, 0, 1, 2, 3)
        return carry

    lax.fori_loop(0, live_blocks(len_ref), step, 0)


def attend_kernel(
    traffic, len_ref, xt_ref, weight_ref, vec_ref, qt_ref, kt_ref, q_ref, k_ref, v_ref, ot_ref, lse_ref, at_ref,
    vone_ref, bound_ref,
):
    heads, size, rows = qt_ref.shape
    flat = heads * size
    scaling = LOG2_E * size ** (-0.5)
    blocks = live_blocks(len_ref)
    length = len_ref[0]
    bound_ref[...] = jnp.zeros(bound_ref.shape, F32)

    def project(block, carry):
        where = lanes(block)
        traffic.take(block)
        xt = xt_ref[:, where]
        projected = tn(weight_ref[:, : 3 * flat], xt)
        query = (projected[:flat] + vec_ref[:, 0:1]).astype(BF16)
        keys = projected[flat : 2 * flat].astype(BF16)
        values = (projected[2 * flat :] + vec_ref[:, 1:2]).astype(BF16)
        split_heads(query, qt_ref, where, size)
        split_heads(keys, kt_ref, where, size)
        bound_ref[...] = jnp.maximum(
            bound_ref[...], squared_lengths(jnp.concatenate([query, keys], axis=0), size)
        )
        column = block * BLOCK + lax.broadcasted_iota(jnp.int32, (1, BLOCK), 1)
        live = jnp.where(column < length, 1.0, 0.0)
        live_values = (values.astype(F32) * live).astype(BF16)
        for head in range(heads):
            vone_ref[head, :size, where] = live_values[head * size : (head + 1) * size]
            vone_ref[head, size:, where] = jnp.broadcast_to(live, (16, BLOCK)).astype(BF16)
        split_pairs(query, q_ref, where)
        split_pairs(keys, k_ref, where)
        split_pairs(values, v_ref, where)
        traffic.give(block, 0, 1, 2, 3, 4)
        return carry

    lax.fori_loop(0, blocks, project, 0)

    longest = jnp.max(bound_ref[...], axis=1, keepdims=True)
    safe = jnp.max(longest[:heads] * longest[heads : 2 * heads]) * scaling**2 <= SAFE_EXPONENT**2

    def scores(head, where, n):
        return nn(k_ref[head // 2, : n * BLOCK, :], pad_rows(qt_ref[head, :, where], head % 2, 2))

    def mix(head, where, n, grown, top):
        mixed = nn(vone_ref[head, :, : n * BLOCK], grown)
        total = mixed[size : size + 1]
        ot_ref[head, :, where] = mixed[:size] * (1.0 / total)
        lse_ref[head, :, where] = jnp.broadcast_to(top + jnp.log2(total), (8, BLOCK))

    def fast(n):
        def step(block, carry):
            where = lanes(block)
            pipeline(
                heads,
                lambda head: scores(head, where, n),
                lambda head, score: jnp.exp2(score * scaling).astype(BF16),
                lambda head, grown: mix(head, where, n, grown, 0.0),
            )
            traffic.give(block, 5, 6)
            return carry

        lax.fori_loop(0, n, step, 0)

    def slow():
        most = rows // BLOCK
        clear_dead(blocks, rows, vone_ref)

        def step(block, carry):
            where = lanes(block)
            for head in range(heads):
                score = mask_tail(scores(head, where, most), most, length, 0)
                top = jnp.max(score, axis=0, keepdims=True) * scaling
                mix(head, where, most, jnp.exp2(score * scaling - top).astype(BF16), top)
            traffic.give(block, 5, 6)
            return carry

        lax.fori_loop(0, blocks, step, 0)

    for_size(blocks, rows // BLOCK, safe, fast, slow)

    def output(block, carry):
        where = lanes(block)
        mixed = ot_ref[:, :, where].reshape(flat, BLOCK).astype(BF16)
        at_ref[:, where] = nn(weight_ref[:, 3 * flat :], mixed).astype(BF16)
        traffic.give(block, 7)
        return carry

    lax.fori_loop(0, blocks, output, 0)


def first_norm(xt, own, other, vec_ref):
    resid = xt.astype(F32) + (own.astype(F32) + other.astype(F32)) + vec_ref[:, 2:3]
    return norm_forward(resid)


def erf(value):
    return lax.erf(value)


def feed_kernel(traffic, len_ref, xt_ref, own_ref, other_ref, in_ref, out_ref, vec_ref, ht_ref, zt_ref, slope_ref, ft_ref):
    def step(block, carry):
        where = lanes(block)
        traffic.take(block)
        normed, _ = first_norm(xt_ref[:, where], own_ref[:, where], other_ref[:, where], vec_ref)
        hidden = normed * vec_ref[:, 3:4] + vec_ref[:, 4:5]
        ht_ref[:, where] = hidden
        pre = tn(in_ref[...], hidden.astype(BF16))
        cdf = 0.5 + 0.5 * erf(pre * (0.5**0.5))
        pdf = jnp.exp2(pre * pre * (-0.5 * LOG2_E)) * 0.3989422804014327
        active = (pre * cdf).astype(BF16)
        zt_ref[:, where] = active
        slope_ref[:, where] = (cdf + pre * pdf).astype(BF16)
        ft_ref[:, where] = nn(out_ref[...], active).astype(BF16)
        traffic.give(block, 0, 1, 2, 3)
        return carry

    lax.fori_loop(0, live_blocks(len_ref), step, 0)


def second_norm(ht, own, other, vec_ref):
    resid = ht + (own.astype(F32) + other.astype(F32)) + vec_ref[:, 5:6]
    return norm_forward(resid)


def relation_kernel(
    traffic, len_ref, weight_ref, ht_ref, own_ref, other_ref, rel_ref, vec_ref, tqt_ref, tk_ref, tvt_ref, tv_ref,
    tbound_ref, grad_ref, dt_ref,
    h2_ref, qt_ref, kt_ref, vt_ref, q_ref, k_ref, v_ref, dqt_ref, dvt_ref, dk_ref, dv_ref, bound_ref,
):
    heads, size, rows = qt_ref.shape
    teacher_size = tqt_ref.shape[1]
    flat = heads * size
    plain = size ** (-0.5)
    scaling = LOG2_E * plain
    teacher_scaling = LOG2_E * teacher_size ** (-0.5)
    blocks = live_blocks(len_ref)
    length = len_ref[0]
    weight = weight_ref[0]
    bound_ref[...] = jnp.zeros(bound_ref.shape, F32)

    def project(block, carry):
        where = lanes(block)
        traffic.take(block)
        normed, _ = second_norm(ht_ref[:, where], own_ref[:, where], other_ref[:, where], vec_ref)
        hidden = (normed * vec_ref[:, 6:7] + vec_ref[:, 7:8]).astype(BF16)
        h2_ref[:, where] = hidden
        projected = tn(rel_ref[...], hidden).astype(BF16)
        bound_ref[...] = jnp.maximum(bound_ref[...], squared_lengths(projected, size))
        split_heads(projected[:flat], qt_ref, where, size)
        split_heads(projected[flat : 2 * flat], kt_ref, where, size)
        split_heads(projected[2 * flat :], vt_ref, where, size)
        split_pairs(projected[:flat], q_ref, where)
        split_pairs(projected[flat : 2 * flat], k_ref, where)
        split_pairs(projected[2 * flat :], v_ref, where)
        for pair in range(heads // 2):
            dk_ref[pair, where, :] = jnp.zeros((BLOCK, 2 * size), F32)
            dv_ref[pair, where, :] = jnp.zeros((BLOCK, 2 * size), F32)
        return carry

    lax.fori_loop(0, blocks, project, 0)

    traffic.take_rest()

    def exponents(ref, scale):
        longest = jnp.max(ref[...], axis=1, keepdims=True)
        attention = jnp.max(longest[:heads] * longest[heads : 2 * heads]) * scale**2
        relation = jnp.max(longest[2 * heads : 3 * heads]) * scale
        return jnp.logical_and(attention <= SAFE_EXPONENT**2, relation <= SAFE_EXPONENT)

    safe = jnp.logical_and(exponents(bound_ref, scaling), exponents(tbound_ref, teacher_scaling))
    attention = (k_ref, qt_ref, q_ref, tk_ref, tqt_ref, kt_ref, dqt_ref, dk_ref)
    relation = (v_ref, vt_ref, v_ref, tv_ref, tvt_ref, vt_ref, dvt_ref, dv_ref)
    tasks = [(2 * pair + half, refs) for pair in range(heads // 2) for refs in (attention, relation) for half in range(2)]

    def steps(n, where, mask, grow):
        column = where.start + lax.broadcasted_iota(jnp.int32, (1, BLOCK), 1)
        live = jnp.where(column < length, weight, 0.0)
        kept = {}

        def first(t):
            head, (left, rightt, _, teacher_left, teacher_rightt, _, _, _) = tasks[t]
            student = nn(left[head // 2, : n * BLOCK, :], pad_rows(rightt[head, :, where], head % 2, 2))
            teacher = nn(teacher_left[head // 2, : n * BLOCK, :], pad_rows(teacher_rightt[head, :, where], head % 2, 2))
            return student, teacher

        def second(t, scores):
            student, teacher = grow(mask(scores[0]), scaling), grow(mask(scores[1]), teacher_scaling)
            student_part = live / jnp.sum(student, axis=0, keepdims=True)
            teacher_part = live / jnp.sum(teacher, axis=0, keepdims=True)
            return (student * student_part - teacher * teacher_part).astype(BF16)

        def third(t, grad):
            head, (_, _, right, _, _, leftt, own_ref, running_ref) = tasks[t]
            own_ref[head, :, where] = (nn(leftt[head, :, : n * BLOCK], grad) * plain).astype(own_ref.dtype)
            kept[head % 2] = grad
            if head % 2 == 1:
                queries = right[head // 2, where, :]
                stacked = jnp.concatenate([pad_lanes(queries, half, size) for half in range(2)], axis=0)
                running_ref[head // 2, : n * BLOCK, :] += nn(jnp.concatenate([kept[0], kept[1]], axis=1), stacked)

        return first, second, third

    def fast(n):
        def step(block, carry):
            stages = steps(
                n, lanes(block), lambda score: mask_tail(score, n, length), lambda score, scale: jnp.exp2(score * scale)
            )
            pipeline(len(tasks), *stages)
            return carry

        lax.fori_loop(0, n, step, 0)

    def slow():
        most = rows // BLOCK
        clear_dead(blocks, rows, kt_ref, vt_ref)

        def grow(score, scale):
            return jnp.exp2(score * scale - jnp.max(score, axis=0, keepdims=True) * scale)

        def step(block, carry):
            first, second, third = steps(
                most, lanes(block), lambda score: mask_tail(score, most, length, 0), grow
            )
            for t in range(len(tasks)):
                third(t, second(t, first(t)))
            return carry

        lax.fori_loop(0, blocks, step, 0)

    for_size(blocks, rows // BLOCK, safe, fast, slow)
    grad_ref[...] = jnp.zeros(grad_ref.shape, F32)

    def finish(block, carry):
        where = lanes(block)
        queries = dqt_ref[:, :, where].reshape(flat, BLOCK)
        keys = jnp.concatenate([dk_ref[pair, where, :].T for pair in range(heads // 2)], axis=0) * plain
        values = jnp.concatenate([dv_ref[pair, where, :].T for pair in range(heads // 2)], axis=0) * plain
        values = values + dvt_ref[:, :, where].reshape(flat, BLOCK)
        grads = jnp.concatenate([queries, keys.astype(BF16), values.astype(BF16)], axis=0)
        grad_ref[...] += nt(h2_ref[:, where], grads)
        dt_ref[:, where] = nn(rel_ref[...], grads).astype(BF16)
        traffic.give(block, 1)
        return carry

    lax.fori_loop(0, blocks, finish, 0)


def feed_back_kernel(
    traffic, len_ref, ht_ref, own_ref, other_ref, down_own_ref, down_other_ref, zt_ref, slope_ref, in_ref, out_ref, vec_ref,
    grad_in_ref, grad_out_ref, sums_ref, resid_ref, up_ref,
):
    grad_in_ref[...] = jnp.zeros(grad_in_ref.shape, F32)
    grad_out_ref[...] = jnp.zeros(grad_out_ref.shape, F32)
    sums_ref[...] = jnp.zeros(sums_ref.shape, F32)

    def step(block, carry):
        where = lanes(block)
        traffic.take(block)
        hidden = ht_ref[:, where]
        normed, inverse = second_norm(hidden, own_ref[:, where], other_ref[:, where], vec_ref)
        grad = down_own_ref[:, where].astype(F32) + down_other_ref[:, where].astype(F32)
        resid = norm_backward(grad * vec_ref[:, 6:7], normed, inverse)
        resid_ref[:, where] = resid
        sums_ref[:, 0:1] += jnp.sum(resid, axis=1, keepdims=True)
        sums_ref[:, 1:2] += jnp.sum(grad * normed, axis=1, keepdims=True)
        sums_ref[:, 2:3] += jnp.sum(grad, axis=1, keepdims=True)
        branch = resid.astype(BF16)
        grad_out_ref[...] += nt(branch, zt_ref[:, where])
        pre_grad = (tn(out_ref[...], branch) * slope_ref[:, where].astype(F32)).astype(BF16)
        grad_in_ref[...] += nt(hidden.astype(BF16), pre_grad)
        up_ref[:, where] = nn(in_ref[...], pre_grad).astype(BF16)
        traffic.give(block, 3, 4)
        return carry

    lax.fori_loop(0, live_blocks(len_ref), step, 0)


def attend_back_kernel(
    traffic, len_ref, xt_ref, own_ref, other_ref, resid_ref, up_own_ref, up_other_ref, weight_ref, vec_ref,
    qt_ref, kt_ref, q_ref, k_ref, v_ref, ot_ref, lse_ref,
    grad_ref, sums_ref, head_sums_ref,
    dot_ref, do_ref, inner_ref, dqt_ref, dk_ref, dv_ref,
):
    heads, size, rows = qt_ref.shape
    flat = heads * size
    plain = size ** (-0.5)
    scaling = LOG2_E * plain
    blocks = live_blocks(len_ref)
    length = len_ref[0]
    sums_ref[...] = jnp.zeros(sums_ref.shape, F32)
    head_sums_ref[...] = jnp.zeros(head_sums_ref.shape, F32)
    grad_ref[...] = jnp.zeros(grad_ref.shape, F32)

    def start(block, carry):
        where = lanes(block)
        traffic.take(block)
        normed, inverse = first_norm(xt_ref[:, where], own_ref[:, where], other_ref[:, where], vec_ref)
        grad = resid_ref[:, where] + (up_own_ref[:, where].astype(F32) + up_other_ref[:, where].astype(F32))
        branch = norm_backward(grad * vec_ref[:, 3:4], normed, inverse).astype(BF16)
        sums_ref[:, 0:1] += jnp.sum(branch.astype(F32), axis=1, keepdims=True)
        sums_ref[:, 1:2] += jnp.sum(grad * normed, axis=1, keepdims=True)
        sums_ref[:, 2:3] += jnp.sum(grad, axis=1, keepdims=True)
        mixed = ot_ref[:, :, where]
        grad_ref[:, 3 * flat :] += nt(branch, mixed.reshape(flat, BLOCK).astype(BF16))
        mixed_grad = tn(weight_ref[:, 3 * flat :], branch).astype(BF16)
        split_heads(mixed_grad, dot_ref, where, size)
        split_pairs(mixed_grad, do_ref, where)
        for head in range(heads):
            product = mixed_grad[head * size : (head + 1) * size].astype(F32) * mixed[head]
            inner_ref[head, :, where] = jnp.broadcast_to(jnp.sum(product, axis=0, keepdims=True), (8, BLOCK))
        for pair in range(heads // 2):
            dk_ref[pair, where, :] = jnp.zeros((BLOCK, 2 * size), F32)
            dv_ref[pair, where, :] = jnp.zeros((BLOCK, 2 * size), F32)
        return carry

    lax.fori_loop(0, blocks, start, 0)
    traffic.take_rest()

    def attend(n):
        def step(block, carry):
            where = lanes(block)
            kept = {}

            def first(head):
                pair, half = head // 2, head % 2
                scores = nn(k_ref[pair, : n * BLOCK, :], pad_rows(qt_ref[head, :, where], half, 2))
                prob_grad = nn(v_ref[pair, : n * BLOCK, :], pad_rows(dot_ref[head, :, where], half, 2))
                return scores, prob_grad

            def second(head, parts):
                scores, prob_grad = parts
                prob = jnp.exp2(mask_tail(scores, n, length) * scaling - lse_ref[head, 0:1, where])
                grad = (prob * (prob_grad - inner_ref[head, 0:1, where])).astype(BF16)
                return prob.astype(BF16), grad

            def third(head, parts):
                pair = head // 2
                dqt_ref[head, :, where] = (nn(kt_ref[head, :, : n * BLOCK], parts[1]) * plain).astype(BF16)
                kept[head % 2] = parts
                if head % 2 == 1:
                    for index, right, running in ((1, q_ref, dk_ref), (0, do_ref, dv_ref)):
                        queries = right[pair, where, :]
                        stacked = jnp.concatenate([pad_lanes(queries, half, size) for half in range(2)], axis=0)
                        running[pair, : n * BLOCK, :] += nn(
                            jnp.concatenate([kept[0][index], kept[1][index]], axis=1), stacked
                        )

            pipeline(heads, first, second, third)
            return carry

        lax.fori_loop(0, n, step, 0)

    for n in range(1, rows // BLOCK + 1):
        pl.when(blocks == n)(functools.partial(attend, n))

    def finish(block, carry):
        where = lanes(block)
        queries = dqt_ref[:, :, where].reshape(flat, BLOCK)
        keys = jnp.concatenate([dk_ref[pair, where, :].T for pair in range(heads // 2)], axis=0) * plain
        values = jnp.concatenate([dv_ref[pair, where, :].T for pair in range(heads // 2)], axis=0).astype(BF16)
        head_sums_ref[:, 0:1] += jnp.sum(queries.astype(F32), axis=1, keepdims=True)
        head_sums_ref[:, 1:2] += jnp.sum(values.astype(F32), axis=1, keepdims=True)
        grads = jnp.concatenate([queries, keys.astype(BF16), values], axis=0)
        grad_ref[:, : 3 * flat] += nt(xt_ref[:, where], grads)
        return carry

    lax.fori_loop(0, blocks, finish, 0)


class Traffic:
    def __init__(self, blocks, ins, outs, in_sems, out_sems):
        self.blocks, self.ins, self.outs, self.in_sems, self.out_sems = blocks, ins, outs, in_sems, out_sems

    def copy(self, source, target, axis, block, sem):
        if axis is not None:
            where = (slice(None),) * axis + (lanes(block),)
            source, target = source.at[where], target.at[where]
        return pltpu.make_async_copy(source, target, sem)

    def inward(self, index, block):
        source, target, axis, _ = self.ins[index]
        return self.copy(source, target, axis, block, self.in_sems.at[index, block])

    def outward(self, index, block):
        target, source, axis = self.outs[index]
        return self.copy(source, target, axis, block, self.out_sems.at[index, block])

    def chosen(self, group):
        return [i for i, entry in enumerate(self.ins) if entry[2] is not None and entry[3] == group]

    def start(self):
        for index, entry in enumerate(self.ins):
            if entry[2] is None:
                self.inward(index, 0).start()
        for group in (0, 1):
            indices = self.chosen(group)

            def step(block, carry):
                for index in indices:
                    self.inward(index, block).start()
                return carry

            if indices:
                lax.fori_loop(0, self.blocks, step, 0)
        for index, entry in enumerate(self.ins):
            if entry[2] is None:
                self.inward(index, 0).wait()

    def take(self, block):
        for index in self.chosen(0):
            self.inward(index, block).wait()

    def take_rest(self):
        def step(block, carry):
            for index in self.chosen(1):
                self.inward(index, block).wait()
            return carry

        lax.fori_loop(0, self.blocks, step, 0)

    def give(self, block, *indices):
        for index in indices:
            self.outward(index, block).start()

    def finish(self):
        whole = [i for i, entry in enumerate(self.outs) if entry[2] is None]
        parts = [i for i, entry in enumerate(self.outs) if entry[2] is not None]
        for index in whole:
            self.outward(index, 0).start()

        def step(block, carry):
            for index in parts:
                self.outward(index, block).wait()
            return carry

        if parts:
            lax.fori_loop(0, self.blocks, step, 0)
        for index in whole:
            self.outward(index, 0).wait()


def call(kernel, name, scalars, arrays, outs, scratch=(), flops=0):
    smem = pl.BlockSpec(memory_space=pltpu.SMEM)
    hbm = pl.BlockSpec(memory_space=pl.ANY)
    most = max(array.shape[axis] // BLOCK for array, axis, _ in arrays if axis is not None)
    count, ins, results = len(scalars), len(arrays), len(outs)

    def body(*refs):
        scalar_refs, refs = refs[:count], refs[count:]
        in_refs, refs = refs[:ins], refs[ins:]
        out_refs, refs = refs[:results], refs[results:]
        in_copies, refs = refs[:ins], refs[ins:]
        out_copies, refs = refs[:results], refs[results:]
        in_sems, out_sems, refs = refs[0], refs[1], refs[2:]
        traffic = Traffic(
            live_blocks(scalar_refs[0]),
            [(ref, copy, axis, group) for ref, copy, (_, axis, group) in zip(in_refs, in_copies, arrays)],
            [(ref, copy, axis) for ref, copy, (_, _, axis) in zip(out_refs, out_copies, outs)],
            in_sems,
            out_sems,
        )
        traffic.start()
        kernel(traffic, *scalar_refs, *in_copies, *out_copies, *refs)
        traffic.finish()

    return pl.pallas_call(
        body,
        name=name,
        out_shape=tuple(jax.ShapeDtypeStruct(shape, dtype) for shape, dtype, _ in outs),
        in_specs=[smem] * count + [hbm] * ins,
        out_specs=tuple(hbm for _ in outs),
        scratch_shapes=[pltpu.VMEM(array.shape, array.dtype) for array, _, _ in arrays]
        + [pltpu.VMEM(shape, dtype) for shape, dtype, _ in outs]
        + [pltpu.SemaphoreType.DMA((ins, most)), pltpu.SemaphoreType.DMA((results, most))]
        + [pltpu.VMEM(shape, dtype) for shape, dtype in scratch],
        compiler_params=pltpu.CompilerParams(vmem_limit_bytes=VMEM_BYTES),
        cost_estimate=pl.CostEstimate(flops=flops, bytes_accessed=4 << 20, transcendentals=0),
    )(*scalars, *(array for array, _, _ in arrays))


def exchange(part):
    return swap(part, "ffn", 0)


def total(parts):
    result = parts[0]
    for part in parts[1:]:
        result = result + part
    return result


def swap(value, axis, bit):
    count = lax.axis_size(axis)
    return lax.ppermute(value, axis, [(i, i ^ (1 << bit)) for i in range(count)])


def bit_of(axis, bit):
    return (lax.axis_index(axis) >> bit) & 1


def dp_bits():
    return lax.axis_size("dp").bit_length() - 1


def after(value, *others):
    return lax.optimization_barrier((value, *others))[0]


def gather_step(whole, other, bit):
    dim = dp_bits() - 1 - bit
    upper = bit_of("dp", bit) == 1
    return jnp.where(upper, jnp.concatenate([other, whole], axis=dim), jnp.concatenate([whole, other], axis=dim))


def split_rows(value):
    bits = dp_bits()
    return value.reshape((2,) * bits + (value.shape[0] >> bits,) + value.shape[1:])


def reduce_step(part, bits, tokens=()):
    count = dp_bits()
    dims = [count - 1 - bit for bit in bits]
    mine = [bit_of("dp", bit) for bit in bits]

    def piece(flips):
        result = part
        for dim, bit, flip in zip(dims, mine, flips):
            result = lax.dynamic_slice_in_dim(result, 1 - bit if flip else bit, 1, dim)
        return result

    size = lax.axis_size("dp")
    arrived = []
    for code in range(1, 1 << len(bits)):
        flips = [(code >> i) & 1 for i in range(len(bits))]
        mask = sum(flip << bit for flip, bit in zip(flips, bits))
        arrived.append(lax.ppermute(piece(flips).astype(BF16), "dp", [(i, i ^ mask) for i in range(size)]))
    kept = piece([0] * len(bits))

    def finish(*tokens):
        result = kept
        for other in arrived:
            result = result + (after(other, *tokens) if tokens else other).astype(F32)
        return result

    return finish


def reduce_owner(value):
    count = lax.axis_size("dp")
    rows = value.shape[0] // count
    spread = lax.all_to_all(value.astype(BF16).reshape((count, rows) + value.shape[1:]), "dp", 0, 0, tiled=True)
    return jnp.sum(spread.astype(F32), axis=0)


def all_sum(value):
    count = lax.axis_size("dp") * lax.axis_size("ffn")
    spread = jnp.broadcast_to(value.reshape(1, 1), (count, 128))
    return jnp.sum(lax.all_to_all(spread, ("dp", "ffn"), 0, 0, tiled=True)[:, 0])


def adam_update(weight, gradient, first, second, clipped, rate, decay):
    scaled = gradient * clipped
    first_new = BETA_ONE * first + (1.0 - BETA_ONE) * scaled
    second_new = BETA_TWO * second + (1.0 - BETA_TWO) * scaled * scaled
    ratio = (
        first_new
        / (1.0 - BETA_ONE**STEP)
        / (jnp.sqrt(second_new / (1.0 - BETA_TWO**STEP)) + ADAM_EPSILON)
    )
    return (weight - rate * (ratio + decay * weight), first_new, second_new)


def per_device(
    states, teacher_states, lengths, domain_ids, domain_weight, teacher_qkv,
    attn_a, ffn_in, ffn_out, attn_b, vec_d,
    mom1_attn_a, mom1_ffn_in, mom1_ffn_out, mom1_attn_b, mom1_vec_d,
    mom2_attn_a, mom2_ffn_in, mom2_ffn_out, mom2_attn_b, mom2_vec_d,
):
    cores = lax.axis_size("ffn")
    core = lax.axis_index("ffn")
    replicas = lax.axis_size("dp")
    replica = lax.axis_index("dp")
    sequences = lengths.shape[0]
    rows = states.shape[0] // sequences
    features = states.shape[1]
    heads = HEADS // cores
    flat = features // cores
    size = flat // heads
    pairs = heads // 2
    hidden = ffn_in.shape[1]
    teacher_flat = teacher_qkv.shape[2]
    teacher_size = teacher_flat // heads
    shard = attn_a.shape[0]
    matched = domain_ids[:, None] == jnp.arange(domain_weight.shape[0])[None, :]
    sequence_weight = jnp.sum(jnp.where(matched, domain_weight[None, :], 0.0), axis=1) / HEADS

    teacher_w = teacher_qkv.reshape(teacher_qkv.shape[0], -1).T
    statest = states.T
    live = [lengths[i : i + 1] for i in range(sequences)]
    weights = [sequence_weight[i : i + 1] for i in range(sequences)]
    xt = [statest[:, i * rows : (i + 1) * rows] for i in range(sequences)]
    each = range(sequences)
    act = ((features, rows), BF16)
    wide = ((features, rows), F32)
    head_t = ((heads, size, rows), BF16)
    pair_rows = ((pairs, rows, 2 * size), BF16)

    bound_rows = -(-3 * heads // 8) * 8

    def project_teacher(i, token):
        return call(
            teacher_kernel, "teacher", (live[i],),
            ((after(teacher_states[i * rows : (i + 1) * rows], token), 0, 0), (teacher_w, None, 0)),
            (
                ((heads, teacher_size, rows), BF16, 2),
                ((pairs, rows, 2 * teacher_size), BF16, 1),
                ((heads, teacher_size, rows), BF16, 2),
                ((pairs, rows, 2 * teacher_size), BF16, 1),
                ((bound_rows, BLOCK), F32, None),
            ),
            flops=2 * rows * 768 * 1152,
        )

    attn_own = lax.dynamic_slice_in_dim(attn_a.reshape(shard, 4, features), core * flat, flat, 2).reshape(shard, 4 * flat)
    bits = dp_bits()
    unit = (1,) * bits
    early = jnp.concatenate([attn_own, vec_d], axis=1).astype(BF16).reshape(unit + (shard, -1))
    late = jnp.concatenate([ffn_in, ffn_out, attn_b.reshape(shard, 3 * flat)], axis=1).astype(BF16)
    late = late.reshape(unit + (shard, -1))
    teacher = []
    for step, bit in enumerate(range(bits)[::-1]):
        early_other = swap(early, "dp", bit)
        late_other = swap(late, "dp", bit + 1) if step else None
        if step == 0:
            tokens = (teacher_w, statest)
        elif step <= sequences:
            teacher.append(project_teacher(step - 1, early))
            tokens = teacher[-1]
        else:
            tokens = ()
        early = gather_step(early, after(early_other, *tokens), bit)
        if step:
            late = gather_step(late, after(late_other, *tokens), bit + 1)
    early = early.reshape(features, -1)
    attn_full, vec_full = early[:, : 4 * flat], early[:, 4 * flat :].astype(F32)
    vec_own = lax.dynamic_slice_in_dim(vec_full, core * flat, flat, 0)
    late_other = swap(late, "dp", 0)

    attended = [
        call(
            attend_kernel, "attend", (live[i],),
            ((after(xt[i], late), 1, 0), (attn_full, None, 0), (vec_own, None, 0)),
            ((*head_t, 2), (*head_t, 2), (*pair_rows, 1), (*pair_rows, 1), (*pair_rows, 1),
             ((heads, size, rows), F32, 2), ((heads, 8, rows), F32, 2), (*act, 1)),
            scratch=(((heads, size + 16, rows), BF16), ((-(-2 * heads // 8) * 8, BLOCK), F32)),
            flops=6 * 10**9,
        )
        for i in each
    ]
    late = gather_step(late, after(late_other, *attended), 0).reshape(features, -1)
    in_full, out_full, rel_full = late[:, :hidden], late[:, hidden : 2 * hidden], late[:, 2 * hidden :]
    mixed_other = [exchange(attended[i][7]) for i in each]
    fed = [
        call(
            feed_kernel, "feed", (live[i],),
            ((xt[i], 1, 0), (attended[i][7], 1, 0), (mixed_other[i], 1, 0), (in_full, None, 0), (out_full, None, 0),
             (vec_full, None, 0)),
            ((*wide, 1), ((hidden, rows), BF16, 1), ((hidden, rows), BF16, 1), (*act, 1)),
            flops=3 * 10**9,
        )
        for i in each
    ]
    fed_other = [exchange(fed[i][3]) for i in each]
    related = [
        call(
            relation_kernel, "relation", (live[i], weights[i]),
            ((fed[i][0], 1, 0), (fed[i][3], 1, 0), (fed_other[i], 1, 0), (rel_full, None, 0), (vec_full, None, 0),
             (teacher[i][0], 2, 1), (teacher[i][1], 1, 1), (teacher[i][2], 2, 1), (teacher[i][3], 1, 1),
             (teacher[i][4], None, 0)),
            (((features, 3 * flat), F32, None), (*act, 1)),
            scratch=(
                act, head_t, head_t, head_t, pair_rows, pair_rows, pair_rows,
                head_t, ((heads, size, rows), F32),
                ((pairs, rows, 2 * size), F32), ((pairs, rows, 2 * size), F32), ((bound_rows, BLOCK), F32),
            ),
            flops=30 * 10**9,
        )
        for i in each
    ]
    down_other = [exchange(related[i][1]) for i in each]
    rel_part = split_rows(total([related[i][0] for i in each]))
    fed_back, up_other = [], []
    for i in each:
        finish = reduce_step(rel_part, (i,))
        fed_back.append(
            call(
                feed_back_kernel, "feed_back", (live[i],),
                ((fed[i][0], 1, 0), (fed[i][3], 1, 0), (fed_other[i], 1, 0), (related[i][1], 1, 0), (down_other[i], 1, 0),
                 (fed[i][1], 1, 0), (fed[i][2], 1, 0), (in_full, None, 0), (out_full, None, 0), (vec_full, None, 0)),
                (((features, hidden), F32, None), ((features, hidden), F32, None), ((features, 8), F32, None),
                 (*wide, 1), (*act, 1)),
                flops=4 * 10**9,
            )
        )
        rel_part = finish(*fed_back[i])
        up_other.append(exchange(fed_back[i][4]))
    feed_part = split_rows(
        total([jnp.concatenate([fed_back[i][0], fed_back[i][1]], axis=1) for i in each])
    )
    attended_back = []
    groups = ((0, 1), tuple(range(2, bits)))
    for i in each:
        finish_feed = reduce_step(feed_part, groups[i])
        finish_rel = reduce_step(rel_part, (2 + i,)) if i + 1 < sequences else reduce_step(rel_part, tuple(range(2 + i, bits)))
        attended_back.append(
            call(
                attend_back_kernel, "attend_back", (live[i],),
                ((xt[i], 1, 0), (attended[i][7], 1, 0), (mixed_other[i], 1, 0), (fed_back[i][3], 1, 0),
                 (fed_back[i][4], 1, 0), (up_other[i], 1, 0), (attn_full, None, 0), (vec_full, None, 0),
                 (attended[i][0], 2, 1), (attended[i][1], 2, 1), (attended[i][2], 1, 1), (attended[i][3], 1, 1),
                 (attended[i][4], 1, 1), (attended[i][5], 2, 0), (attended[i][6], 2, 1)),
                (((features, 4 * flat), F32, None), ((features, 8), F32, None), ((flat, 8), F32, None)),
                scratch=(
                    head_t, pair_rows, ((heads, 8, rows), F32), head_t,
                    ((pairs, rows, 2 * size), F32), ((pairs, rows, 2 * size), F32),
                ),
                flops=15 * 10**9,
            )
        )
        feed_part = finish_feed(*attended_back[i])
        rel_part = finish_rel(*attended_back[i])

    shard_rel = rel_part.reshape(shard, -1)
    shard_feed = feed_part.reshape(shard, -1)
    shard_in, shard_out = shard_feed[:, :hidden], shard_feed[:, hidden:]
    back_sums = total([fed_back[i][2] for i in each])
    first_sums = total([attended_back[i][1] for i in each])
    head_sums = total([attended_back[i][2] for i in each])
    placed = lax.dynamic_update_slice_in_dim(jnp.zeros((features, 2), F32), head_sums[:, :2], core * flat, 0)
    attn_local = total([attended_back[i][0] for i in each])
    own = jnp.concatenate([attn_local, placed, first_sums[:, :3], back_sums[:, :3]], axis=1)
    own = reduce_owner(after(own, shard_rel, shard_feed))
    other = swap(own, "ffn", 0)
    grad_rel = shard_rel.reshape(attn_b.shape)
    upper = core == 1
    low, high = jnp.where(upper, other, own), jnp.where(upper, own, other)
    columns = [
        half[:, start : start + flat] for start in range(0, 4 * flat, flat) for half in (low, high)
    ]
    grad_attn = jnp.concatenate(columns, axis=1)
    grad_vec = jnp.concatenate([(low + high)[:, 4 * flat : 4 * flat + 2], own[:, 4 * flat + 2 :]], axis=1)
    gradients = (grad_attn, shard_in, shard_out, grad_rel, grad_vec)
    shared = own[:, 4 * flat + 2 :]
    squares = (
        jnp.sum(own[:, : 4 * flat + 2] * own[:, : 4 * flat + 2])
        + jnp.sum(shared * shared) / cores
        + jnp.sum(shard_feed * shard_feed)
        + jnp.sum(shard_rel * shard_rel)
    )
    grad_norm = jnp.sqrt(all_sum(squares))
    clipped = jnp.minimum(1.0, CLIP_NORM / grad_norm)
    masters = (attn_a, ffn_in, ffn_out, attn_b, vec_d)
    firsts = (mom1_attn_a, mom1_ffn_in, mom1_ffn_out, mom1_attn_b, mom1_vec_d)
    seconds = (mom2_attn_a, mom2_ffn_in, mom2_ffn_out, mom2_attn_b, mom2_vec_d)
    rates = (RATE_MATRIX, RATE_MATRIX, RATE_MATRIX, RATE_MATRIX, RATE_VECTOR)
    decays = (DECAY_RATE, DECAY_RATE, DECAY_RATE, DECAY_RATE, 0.0)
    news = [
        adam_update(masters[i], gradients[i], firsts[i], seconds[i], clipped, rates[i], decays[i])
        for i in range(5)
    ]
    return (grad_norm, *(new[0] for new in news), *(new[1] for new in news), *(new[2] for new in news))


def solution(mesh):
    matrix = P("dp", None)
    halved = P("dp", "ffn")
    cube = P("dp", None, "ffn")
    trained = (matrix, halved, halved, cube, matrix)
    in_specs = (matrix, matrix, P("dp"), P("dp"), P(), P(None, None, "ffn")) + trained * 3
    out_specs = (P(),) + trained * 3
    return jax.shard_map(per_device, mesh=mesh, in_specs=in_specs, out_specs=out_specs, check_vma=False)
```

```python
import functools

import jax
import jax.numpy as jnp
from jax import lax
from jax.experimental import pallas as pl
from jax.experimental.pallas import tpu as pltpu
from jax.sharding import PartitionSpec as P

HEADS = 12
STEP = 10

NORM_EPSILON = 1e-12
CLIP_NORM = 1.0
BETA_ONE = 0.9
BETA_TWO = 0.999
ADAM_EPSILON = 1e-08
RATE_MATRIX = 0.04
RATE_VECTOR = 0.2
DECAY_RATE = 0.01
MASK_VALUE = -1e30
LOG2_E = 1.4426950408889634
BLOCK = 256
SAFE_EXPONENT = 100.0
VMEM_BYTES = 64 * 2**20 - 2**17
F32 = jnp.float32
BF16 = jnp.bfloat16


def nn(left, right):
    return lax.dot_general(left, right, (((1,), (0,)), ((), ())), preferred_element_type=F32)


def nt(left, right):
    return lax.dot_general(left, right, (((1,), (1,)), ((), ())), preferred_element_type=F32)


def tn(left, right):
    return lax.dot_general(left, right, (((0,), (0,)), ((), ())), preferred_element_type=F32)


def lanes(block):
    return pl.ds(pl.multiple_of(block * BLOCK, BLOCK), BLOCK)


def live_blocks(len_ref):
    return (len_ref[0] + BLOCK - 1) // BLOCK


def for_size(blocks, most, safe, fast, slow):
    for n in range(1, most + 1):
        pl.when(jnp.logical_and(safe, blocks == n))(functools.partial(fast, n))
    pl.when(jnp.logical_not(safe))(slow)


def pipeline(count, first, second, third):
    firsts, seconds = {}, {}
    for t in range(count + 2):
        if t < count:
            firsts[t] = first(t)
        if 0 <= t - 1 < count:
            seconds[t - 1] = second(t - 1, firsts.pop(t - 1))
        if 0 <= t - 2 < count:
            third(t - 2, seconds.pop(t - 2))


def squared_lengths(flat, size):
    features = flat.shape[0]
    groups = -(-features // size // 8) * 8
    row = lax.broadcasted_iota(jnp.int32, (groups, features), 0)
    column = lax.broadcasted_iota(jnp.int32, (groups, features), 1)
    ones = jnp.where((column >= row * size) & (column < (row + 1) * size), 1.0, 0.0).astype(BF16)
    return nn(ones, flat * flat)


def clear_dead(blocks, rows, *refs):
    def step(block, carry):
        for ref in refs:
            ref[:, :, lanes(block)] = jnp.zeros(ref.shape[:2] + (BLOCK,), ref.dtype)
        return carry

    lax.fori_loop(blocks, rows // BLOCK, step, 0)


def norm_forward(resid):
    features = resid.shape[0]
    centred = resid - jnp.sum(resid, axis=0, keepdims=True) * (1.0 / features)
    variance = jnp.sum(centred * centred, axis=0, keepdims=True) * (1.0 / features)
    inverse = lax.rsqrt(variance + NORM_EPSILON)
    return centred * inverse, inverse


def norm_backward(scaled, normed, inverse):
    features = scaled.shape[0]
    mean = jnp.sum(scaled, axis=0, keepdims=True) * (1.0 / features)
    slope = jnp.sum(scaled * normed, axis=0, keepdims=True) * (1.0 / features)
    return inverse * (scaled - mean - normed * slope)


def mask_tail(scores, n, length, start=None):
    start = (n - 1) * BLOCK if start is None else start
    rows = start + lax.broadcasted_iota(jnp.int32, (n * BLOCK - start, scores.shape[1]), 0)
    tail = jnp.where(rows < length, scores[start:], MASK_VALUE)
    if start == 0:
        return tail
    return jnp.concatenate([scores[:start], tail], axis=0)


def pad_rows(part, index, count):
    zeros = jnp.zeros_like(part)
    return jnp.concatenate([part if i == index else zeros for i in range(count)], axis=0)


def pad_lanes(pair, index, size):
    lane = lax.broadcasted_iota(jnp.int32, pair.shape, 1)
    return jnp.where((lane >= index * size) & (lane < (index + 1) * size), pair, jnp.zeros_like(pair))


def split_heads(flat, ref, columns, size):
    heads = flat.shape[0] // size
    for head in range(heads):
        ref[head, :, columns] = flat[head * size : (head + 1) * size]


def split_pairs(flat, ref, rows):
    pairs, width = ref.shape[0], ref.shape[2]
    for pair in range(pairs):
        ref[pair, rows, :] = flat[pair * width : (pair + 1) * width].T


def teacher_kernel(traffic, len_ref, rows_ref, weight_ref, qt_ref, k_ref, vt_ref, v_ref, bound_ref):
    size = qt_ref.shape[1]
    bound_ref[...] = jnp.zeros(bound_ref.shape, F32)

    def step(block, carry):
        where = lanes(block)
        traffic.take(block)
        rows = rows_ref[where, :]
        queries, keys, values = [nn(rows, weight_ref[index]).astype(BF16) for index in range(3)]
        columns = [part.T for part in (queries, keys, values)]
        bound_ref[...] = jnp.maximum(bound_ref[...], squared_lengths(jnp.concatenate(columns, axis=0), size))
        split_heads(columns[0], qt_ref, where, size)
        split_heads(columns[2], vt_ref, where, size)
        for pair in range(k_ref.shape[0]):
            k_ref[pair, where, :] = keys[:, 2 * size * pair : 2 * size * (pair + 1)]
            v_ref[pair, where, :] = values[:, 2 * size * pair : 2 * size * (pair + 1)]
        traffic.give(block, 0, 1, 2, 3)
        return carry

    lax.fori_loop(0, live_blocks(len_ref), step, 0)


def attend_kernel(
    traffic, len_ref, xt_ref, weight_ref, vec_ref, qt_ref, kt_ref, q_ref, k_ref, v_ref, ot_ref, lse_ref, at_ref,
    vone_ref, bound_ref,
):
    heads, size, rows = qt_ref.shape
    flat = heads * size
    scaling = LOG2_E * size ** (-0.5)
    blocks = live_blocks(len_ref)
    length = len_ref[0]
    bound_ref[...] = jnp.zeros(bound_ref.shape, F32)

    def project(block, carry):
        where = lanes(block)
        traffic.take(block)
        xt = xt_ref[:, where]
        projected = tn(weight_ref[:, : 3 * flat], xt)
        query = (projected[:flat] + vec_ref[:, 0:1]).astype(BF16)
        keys = projected[flat : 2 * flat].astype(BF16)
        values = (projected[2 * flat :] + vec_ref[:, 1:2]).astype(BF16)
        split_heads(query, qt_ref, where, size)
        split_heads(keys, kt_ref, where, size)
        bound_ref[...] = jnp.maximum(
            bound_ref[...], squared_lengths(jnp.concatenate([query, keys], axis=0), size)
        )
        column = block * BLOCK + lax.broadcasted_iota(jnp.int32, (1, BLOCK), 1)
        live = jnp.where(column < length, 1.0, 0.0)
        live_values = (values.astype(F32) * live).astype(BF16)
        for head in range(heads):
            vone_ref[head, :size, where] = live_values[head * size : (head + 1) * size]
            vone_ref[head, size:, where] = jnp.broadcast_to(live, (16, BLOCK)).astype(BF16)
        split_pairs(query, q_ref, where)
        split_pairs(keys, k_ref, where)
        split_pairs(values, v_ref, where)
        traffic.give(block, 0, 1, 2, 3, 4)
        return carry

    lax.fori_loop(0, blocks, project, 0)

    longest = jnp.max(bound_ref[...], axis=1, keepdims=True)
    safe = jnp.max(longest[:heads] * longest[heads : 2 * heads]) * scaling**2 <= SAFE_EXPONENT**2

    def scores(head, where, n):
        return nn(k_ref[head // 2, : n * BLOCK, :], pad_rows(qt_ref[head, :, where], head % 2, 2))

    def mix(head, where, n, grown, top):
        mixed = nn(vone_ref[head, :, : n * BLOCK], grown)
        total = mixed[size : size + 1]
        ot_ref[head, :, where] = mixed[:size] * (1.0 / total)
        lse_ref[head, :, where] = jnp.broadcast_to(top + jnp.log2(total), (8, BLOCK))

    def fast(n):
        def step(block, carry):
            where = lanes(block)
            pipeline(
                heads,
                lambda head: scores(head, where, n),
                lambda head, score: jnp.exp2(score * scaling).astype(BF16),
                lambda head, grown: mix(head, where, n, grown, 0.0),
            )
            traffic.give(block, 5, 6)
            return carry

        lax.fori_loop(0, n, step, 0)

    def slow():
        most = rows // BLOCK
        clear_dead(blocks, rows, vone_ref)

        def step(block, carry):
            where = lanes(block)
            for head in range(heads):
                score = mask_tail(scores(head, where, most), most, length, 0)
                top = jnp.max(score, axis=0, keepdims=True) * scaling
                mix(head, where, most, jnp.exp2(score * scaling - top).astype(BF16), top)
            traffic.give(block, 5, 6)
            return carry

        lax.fori_loop(0, blocks, step, 0)

    for_size(blocks, rows // BLOCK, safe, fast, slow)

    def output(block, carry):
        where = lanes(block)
        mixed = ot_ref[:, :, where].reshape(flat, BLOCK).astype(BF16)
        at_ref[:, where] = nn(weight_ref[:, 3 * flat :], mixed).astype(BF16)
        traffic.give(block, 7)
        return carry

    lax.fori_loop(0, blocks, output, 0)


def first_norm(xt, own, other, vec_ref):
    resid = xt.astype(F32) + (own.astype(F32) + other.astype(F32)) + vec_ref[:, 2:3]
    return norm_forward(resid)


def erf(value):
    return lax.erf(value)


def feed_kernel(traffic, len_ref, xt_ref, own_ref, other_ref, in_ref, out_ref, vec_ref, ht_ref, zt_ref, slope_ref, ft_ref):
    def step(block, carry):
        where = lanes(block)
        traffic.take(block)
        normed, _ = first_norm(xt_ref[:, where], own_ref[:, where], other_ref[:, where], vec_ref)
        hidden = normed * vec_ref[:, 3:4] + vec_ref[:, 4:5]
        ht_ref[:, where] = hidden
        pre = tn(in_ref[...], hidden.astype(BF16))
        cdf = 0.5 + 0.5 * erf(pre * (0.5**0.5))
        pdf = jnp.exp2(pre * pre * (-0.5 * LOG2_E)) * 0.3989422804014327
        active = (pre * cdf).astype(BF16)
        zt_ref[:, where] = active
        slope_ref[:, where] = (cdf + pre * pdf).astype(BF16)
        ft_ref[:, where] = nn(out_ref[...], active).astype(BF16)
        traffic.give(block, 0, 1, 2, 3)
        return carry

    lax.fori_loop(0, live_blocks(len_ref), step, 0)


def second_norm(ht, own, other, vec_ref):
    resid = ht + (own.astype(F32) + other.astype(F32)) + vec_ref[:, 5:6]
    return norm_forward(resid)


def relation_kernel(
    chained, traffic, len_ref, weight_ref, ht_ref, own_ref, other_ref, rel_ref, vec_ref, tqt_ref, tk_ref, tvt_ref, tv_ref,
    tbound_ref, *refs,
):
    earlier_ref, refs = (refs[0], refs[1:]) if chained else (None, refs)
    grad_out_ref, dt_ref, refs = refs[0], refs[1], refs[2:]
    grad_ref, refs = refs[0], refs[1:]
    relation_body(
        traffic, len_ref, weight_ref, ht_ref, own_ref, other_ref, rel_ref, vec_ref, tqt_ref, tk_ref, tvt_ref, tv_ref,
        tbound_ref, grad_ref, dt_ref, *refs,
    )
    traffic.take_last()
    grad = grad_ref[...] + earlier_ref[...] if chained else grad_ref[...]
    grad_out_ref[...] = grad.astype(grad_out_ref.dtype)


def relation_body(
    traffic, len_ref, weight_ref, ht_ref, own_ref, other_ref, rel_ref, vec_ref, tqt_ref, tk_ref, tvt_ref, tv_ref,
    tbound_ref, grad_ref, dt_ref,
    h2_ref, qt_ref, kt_ref, vt_ref, q_ref, k_ref, v_ref, dqt_ref, dvt_ref, dk_ref, dv_ref, bound_ref,
):
    heads, size, rows = qt_ref.shape
    teacher_size = tqt_ref.shape[1]
    flat = heads * size
    plain = size ** (-0.5)
    scaling = LOG2_E * plain
    teacher_scaling = LOG2_E * teacher_size ** (-0.5)
    blocks = live_blocks(len_ref)
    length = len_ref[0]
    weight = weight_ref[0]
    bound_ref[...] = jnp.zeros(bound_ref.shape, F32)

    def project(block, carry):
        where = lanes(block)
        traffic.take(block)
        normed, _ = second_norm(ht_ref[:, where], own_ref[:, where], other_ref[:, where], vec_ref)
        hidden = (normed * vec_ref[:, 6:7] + vec_ref[:, 7:8]).astype(BF16)
        h2_ref[:, where] = hidden
        projected = tn(rel_ref[...], hidden).astype(BF16)
        bound_ref[...] = jnp.maximum(bound_ref[...], squared_lengths(projected, size))
        split_heads(projected[:flat], qt_ref, where, size)
        split_heads(projected[flat : 2 * flat], kt_ref, where, size)
        split_heads(projected[2 * flat :], vt_ref, where, size)
        split_pairs(projected[:flat], q_ref, where)
        split_pairs(projected[flat : 2 * flat], k_ref, where)
        split_pairs(projected[2 * flat :], v_ref, where)
        for pair in range(heads // 2):
            dk_ref[pair, where, :] = jnp.zeros((BLOCK, 2 * size), F32)
            dv_ref[pair, where, :] = jnp.zeros((BLOCK, 2 * size), F32)
        return carry

    lax.fori_loop(0, blocks, project, 0)

    traffic.take_rest()

    def exponents(ref, scale):
        longest = jnp.max(ref[...], axis=1, keepdims=True)
        attention = jnp.max(longest[:heads] * longest[heads : 2 * heads]) * scale**2
        relation = jnp.max(longest[2 * heads : 3 * heads]) * scale
        return jnp.logical_and(attention <= SAFE_EXPONENT**2, relation <= SAFE_EXPONENT)

    safe = jnp.logical_and(exponents(bound_ref, scaling), exponents(tbound_ref, teacher_scaling))
    pairs = heads // 2
    attention = (k_ref, qt_ref, q_ref, tk_ref, tqt_ref, kt_ref, dqt_ref, dk_ref)
    relation = (v_ref, vt_ref, v_ref, tv_ref, tvt_ref, vt_ref, dvt_ref, dv_ref)
    tasks = [(half, refs) for refs in (attention, relation) for half in range(2)]

    def steps(n, pair, where, mask, grow):
        column = where.start + lax.broadcasted_iota(jnp.int32, (1, BLOCK), 1)
        live = jnp.where(column < length, weight, 0.0)
        kept = {}

        def first(t):
            half, (left, rightt, _, teacher_left, teacher_rightt, _, _, _) = tasks[t]
            head = 2 * pair + half
            student = nn(left[pair, : n * BLOCK, :], pad_rows(rightt[head, :, where], half, 2))
            teacher = nn(teacher_left[pair, : n * BLOCK, :], pad_rows(teacher_rightt[head, :, where], half, 2))
            return student, teacher

        def second(t, scores):
            student, teacher = grow(mask(scores[0]), scaling), grow(mask(scores[1]), teacher_scaling)
            student_part = live / jnp.sum(student, axis=0, keepdims=True)
            teacher_part = live / jnp.sum(teacher, axis=0, keepdims=True)
            return (student * student_part - teacher * teacher_part).astype(BF16)

        def third(t, grad):
            half, (_, _, right, _, _, leftt, own_ref, running_ref) = tasks[t]
            head = 2 * pair + half
            own_ref[head, :, where] = (nn(leftt[head, :, : n * BLOCK], grad) * plain).astype(own_ref.dtype)
            kept[half] = grad
            if half == 1:
                queries = right[pair, where, :]
                stacked = jnp.concatenate([pad_lanes(queries, i, size) for i in range(2)], axis=0)
                running_ref[pair, : n * BLOCK, :] += nn(jnp.concatenate([kept[0], kept[1]], axis=1), stacked)

        return first, second, third

    def fast(n):
        def step(index, carry):
            stages = steps(
                n, index % pairs, lanes(index // pairs), lambda score: mask_tail(score, n, length),
                lambda score, scale: jnp.exp2(score * scale),
            )
            pipeline(len(tasks), *stages)
            return carry

        lax.fori_loop(0, n * pairs, step, 0)

    def slow():
        most = rows // BLOCK
        clear_dead(blocks, rows, kt_ref, vt_ref)

        def grow(score, scale):
            return jnp.exp2(score * scale - jnp.max(score, axis=0, keepdims=True) * scale)

        def step(index, carry):
            first, second, third = steps(
                most, index % pairs, lanes(index // pairs), lambda score: mask_tail(score, most, length, 0), grow
            )
            for t in range(len(tasks)):
                third(t, second(t, first(t)))
            return carry

        lax.fori_loop(0, blocks * pairs, step, 0)

    for_size(blocks, rows // BLOCK, safe, fast, slow)
    grad_ref[...] = jnp.zeros(grad_ref.shape, F32)

    def finish(block, carry):
        where = lanes(block)
        queries = dqt_ref[:, :, where].reshape(flat, BLOCK)
        keys = jnp.concatenate([dk_ref[pair, where, :].T for pair in range(heads // 2)], axis=0) * plain
        values = jnp.concatenate([dv_ref[pair, where, :].T for pair in range(heads // 2)], axis=0) * plain
        values = values + dvt_ref[:, :, where].reshape(flat, BLOCK)
        grads = jnp.concatenate([queries, keys.astype(BF16), values.astype(BF16)], axis=0)
        grad_ref[...] += nt(h2_ref[:, where], grads)
        dt_ref[:, where] = nn(rel_ref[...], grads).astype(BF16)
        traffic.give(block, 1)
        return carry

    lax.fori_loop(0, blocks, finish, 0)


def feed_back_kernel(
    chained, traffic, len_ref, ht_ref, own_ref, other_ref, down_own_ref, down_other_ref, zt_ref, slope_ref, in_ref, out_ref, vec_ref, *refs,
):
    earlier, refs = (refs[:2], refs[2:]) if chained else (None, refs)
    total_ref, sums_out_ref, resid_ref, up_ref, refs = *refs[:4], refs[4:]
    grad_ref, sums_ref = refs
    hidden_units = in_ref.shape[1]
    grad_ref[...] = jnp.zeros(grad_ref.shape, F32)
    sums_ref[...] = jnp.zeros(sums_ref.shape, F32)

    def step(block, carry):
        where = lanes(block)
        traffic.take(block)
        hidden = ht_ref[:, where]
        normed, inverse = second_norm(hidden, own_ref[:, where], other_ref[:, where], vec_ref)
        grad = down_own_ref[:, where].astype(F32) + down_other_ref[:, where].astype(F32)
        resid = norm_backward(grad * vec_ref[:, 6:7], normed, inverse)
        resid_ref[:, where] = resid
        sums_ref[:, 0:1] += jnp.sum(resid, axis=1, keepdims=True)
        sums_ref[:, 1:2] += jnp.sum(grad * normed, axis=1, keepdims=True)
        sums_ref[:, 2:3] += jnp.sum(grad, axis=1, keepdims=True)
        branch = resid.astype(BF16)
        grad_ref[:, hidden_units:] += nt(branch, zt_ref[:, where])
        pre_grad = (tn(out_ref[...], branch) * slope_ref[:, where].astype(F32)).astype(BF16)
        grad_ref[:, :hidden_units] += nt(hidden.astype(BF16), pre_grad)
        up_ref[:, where] = nn(in_ref[...], pre_grad).astype(BF16)
        traffic.give(block, 2, 3)
        return carry

    lax.fori_loop(0, live_blocks(len_ref), step, 0)
    traffic.take_last()
    grad, sums = grad_ref[...], sums_ref[...]
    if chained:
        grad, sums = grad + earlier[0][...], sums + earlier[1][...]
    total_ref[...] = grad.astype(total_ref.dtype)
    sums_out_ref[...] = sums


def attend_back_kernel(
    chained, last, traffic, len_ref, core_ref, xt_ref, own_ref, other_ref, resid_ref, up_own_ref, up_other_ref, weight_ref, vec_ref,
    qt_ref, kt_ref, q_ref, k_ref, v_ref, ot_ref, lse_ref, *refs,
):
    back_sums_ref, refs = (refs[0], refs[1:]) if last else (None, refs)
    earlier, refs = (refs[:3], refs[3:]) if chained else (None, refs)
    outs, refs = (refs[:1], refs[1:]) if last else (refs[:3], refs[3:])
    running, refs = refs[:3], refs[3:]
    grad_ref, sums_ref, head_sums_ref = running
    for ref in running:
        ref[...] = jnp.zeros(ref.shape, F32)
    attend_back_body(
        traffic, len_ref, xt_ref, own_ref, other_ref, resid_ref, up_own_ref, up_other_ref, weight_ref, vec_ref,
        qt_ref, kt_ref, q_ref, k_ref, v_ref, ot_ref, lse_ref, grad_ref, sums_ref, head_sums_ref, *refs,
    )
    traffic.take_last()
    if chained:
        for ref, value in zip(running, earlier):
            ref[...] += value[...]
    if not last:
        for ref, value in zip(outs, running):
            ref[...] = value[...]
        return
    total_ref = outs[0]
    columns, flat = grad_ref.shape[1], head_sums_ref.shape[0]
    total_ref[:, :columns] = grad_ref[...].astype(BF16)
    biases = head_sums_ref[:, 0:2].astype(BF16)
    total_ref[:, columns : columns + 2] = jnp.zeros((total_ref.shape[0], 2), BF16)
    for core in range(total_ref.shape[0] // flat):

        @pl.when(core_ref[0] == core)
        def _(core=core):
            total_ref[core * flat : (core + 1) * flat, columns : columns + 2] = biases

    total_ref[:, columns + 2 : columns + 5] = sums_ref[:, 0:3].astype(BF16)
    total_ref[:, columns + 5 : columns + 8] = back_sums_ref[:, 0:3].astype(BF16)


def attend_back_body(
    traffic, len_ref, xt_ref, own_ref, other_ref, resid_ref, up_own_ref, up_other_ref, weight_ref, vec_ref,
    qt_ref, kt_ref, q_ref, k_ref, v_ref, ot_ref, lse_ref, grad_ref, sums_ref, head_sums_ref,
    dot_ref, do_ref, inner_ref, dqt_ref, dk_ref, dv_ref,
):
    heads, size, rows = qt_ref.shape
    flat = heads * size
    plain = size ** (-0.5)
    scaling = LOG2_E * plain
    blocks = live_blocks(len_ref)
    length = len_ref[0]

    def start(block, carry):
        where = lanes(block)
        traffic.take(block)
        normed, inverse = first_norm(xt_ref[:, where], own_ref[:, where], other_ref[:, where], vec_ref)
        grad = resid_ref[:, where] + (up_own_ref[:, where].astype(F32) + up_other_ref[:, where].astype(F32))
        branch = norm_backward(grad * vec_ref[:, 3:4], normed, inverse).astype(BF16)
        sums_ref[:, 0:1] += jnp.sum(branch.astype(F32), axis=1, keepdims=True)
        sums_ref[:, 1:2] += jnp.sum(grad * normed, axis=1, keepdims=True)
        sums_ref[:, 2:3] += jnp.sum(grad, axis=1, keepdims=True)
        mixed = ot_ref[:, :, where]
        grad_ref[:, 3 * flat :] += nt(branch, mixed.reshape(flat, BLOCK).astype(BF16))
        mixed_grad = tn(weight_ref[:, 3 * flat :], branch).astype(BF16)
        split_heads(mixed_grad, dot_ref, where, size)
        split_pairs(mixed_grad, do_ref, where)
        for head in range(heads):
            product = mixed_grad[head * size : (head + 1) * size].astype(F32) * mixed[head]
            inner_ref[head, :, where] = jnp.broadcast_to(jnp.sum(product, axis=0, keepdims=True), (8, BLOCK))
        for pair in range(heads // 2):
            dk_ref[pair, where, :] = jnp.zeros((BLOCK, 2 * size), F32)
            dv_ref[pair, where, :] = jnp.zeros((BLOCK, 2 * size), F32)
        return carry

    lax.fori_loop(0, blocks, start, 0)
    traffic.take_rest()

    def attend(n):
        def step(block, carry):
            where = lanes(block)
            kept = {}

            def first(head):
                pair, half = head // 2, head % 2
                scores = nn(k_ref[pair, : n * BLOCK, :], pad_rows(qt_ref[head, :, where], half, 2))
                prob_grad = nn(v_ref[pair, : n * BLOCK, :], pad_rows(dot_ref[head, :, where], half, 2))
                return scores, prob_grad

            def second(head, parts):
                scores, prob_grad = parts
                prob = jnp.exp2(mask_tail(scores, n, length) * scaling - lse_ref[head, 0:1, where])
                grad = (prob * (prob_grad - inner_ref[head, 0:1, where])).astype(BF16)
                return prob.astype(BF16), grad

            def third(head, parts):
                pair = head // 2
                dqt_ref[head, :, where] = (nn(kt_ref[head, :, : n * BLOCK], parts[1]) * plain).astype(BF16)
                kept[head % 2] = parts
                if head % 2 == 1:
                    for index, right, running in ((1, q_ref, dk_ref), (0, do_ref, dv_ref)):
                        queries = right[pair, where, :]
                        stacked = jnp.concatenate([pad_lanes(queries, half, size) for half in range(2)], axis=0)
                        running[pair, : n * BLOCK, :] += nn(
                            jnp.concatenate([kept[0][index], kept[1][index]], axis=1), stacked
                        )

            pipeline(heads, first, second, third)
            return carry

        lax.fori_loop(0, n, step, 0)

    for n in range(1, rows // BLOCK + 1):
        pl.when(blocks == n)(functools.partial(attend, n))

    def finish(block, carry):
        where = lanes(block)
        queries = dqt_ref[:, :, where].reshape(flat, BLOCK)
        keys = jnp.concatenate([dk_ref[pair, where, :].T for pair in range(heads // 2)], axis=0) * plain
        values = jnp.concatenate([dv_ref[pair, where, :].T for pair in range(heads // 2)], axis=0).astype(BF16)
        head_sums_ref[:, 0:1] += jnp.sum(queries.astype(F32), axis=1, keepdims=True)
        head_sums_ref[:, 1:2] += jnp.sum(values.astype(F32), axis=1, keepdims=True)
        grads = jnp.concatenate([queries, keys.astype(BF16), values], axis=0)
        grad_ref[:, : 3 * flat] += nt(xt_ref[:, where], grads)
        return carry

    lax.fori_loop(0, blocks, finish, 0)


class Traffic:
    def __init__(self, blocks, ins, outs, in_sems, out_sems):
        self.blocks, self.ins, self.outs, self.in_sems, self.out_sems = blocks, ins, outs, in_sems, out_sems

    def part(self, ref, axis, block):
        return ref if axis is None else ref.at[(slice(None),) * axis + (lanes(block),)]

    def inward(self, index, block):
        source, target, axis, _, first = self.ins[index]
        if axis is None:
            if first:
                source = source.at[:, first[0] : first[0] + first[1]]
            return pltpu.make_async_copy(source, target, self.in_sems.at[index, 0])
        return pltpu.make_async_copy(
            self.part(source, axis, first + block), self.part(target, axis, block), self.in_sems.at[index, block]
        )

    def outward(self, index, block):
        target, source, axis = self.outs[index]
        return pltpu.make_async_copy(
            self.part(source, axis, block), self.part(target, axis, block), self.out_sems.at[index, block]
        )

    def chosen(self, group, whole=False):
        return [i for i, entry in enumerate(self.ins) if (entry[2] is None) == whole and entry[3] == group]

    def start(self):
        for index in self.chosen(0, whole=True):
            self.inward(index, 0).start()
        for group in (0, 1):
            indices = self.chosen(group)

            def step(block, carry):
                for index in indices:
                    self.inward(index, block).start()
                return carry

            if indices:
                lax.fori_loop(0, self.blocks, step, 0)
        for index in self.chosen(1, whole=True):
            self.inward(index, 0).start()
        for index in self.chosen(0, whole=True):
            self.inward(index, 0).wait()

    def take(self, block):
        for index in self.chosen(0):
            self.inward(index, block).wait()

    def take_rest(self):
        def step(block, carry):
            for index in self.chosen(1):
                self.inward(index, block).wait()
            return carry

        lax.fori_loop(0, self.blocks, step, 0)

    def take_last(self):
        for index in self.chosen(1, whole=True):
            self.inward(index, 0).wait()

    def give(self, block, *indices):
        for index in indices:
            self.outward(index, block).start()

    def finish(self):
        whole = [i for i, entry in enumerate(self.outs) if entry[2] is None]
        parts = [i for i, entry in enumerate(self.outs) if entry[2] is not None]
        for index in whole:
            self.outward(index, 0).start()

        def step(block, carry):
            for index in parts:
                self.outward(index, block).wait()
            return carry

        if parts:
            lax.fori_loop(0, self.blocks, step, 0)
        for index in whole:
            self.outward(index, 0).wait()


def call(blocks, kernel, name, scalars, arrays, outs, scratch=(), flops=0):
    smem = pl.BlockSpec(memory_space=pltpu.SMEM)
    hbm = pl.BlockSpec(memory_space=pl.ANY)
    arrays = [entry if len(entry) == 4 else (*entry, 0) for entry in arrays]

    def held(array, axis, group, first):
        shape = list(array.shape)
        if axis is not None:
            shape[axis] = blocks * BLOCK
        elif first:
            shape[1] = first[1]
        return pltpu.VMEM(tuple(shape), array.dtype)

    count, ins, results = len(scalars), len(arrays), len(outs)
    copied = [i for i in range(ins) if arrays[i][2] is not None]

    def body(*refs):
        scalar_refs, refs = refs[:count], refs[count:]
        in_refs, refs = refs[:ins], refs[ins:]
        out_refs, refs = refs[:results], refs[results:]
        in_copies = list(in_refs)
        for index, ref in zip(copied, refs):
            in_copies[index] = ref
        refs = refs[len(copied) :]
        out_copies, refs = refs[:results], refs[results:]
        in_sems, out_sems, refs = refs[0], refs[1], refs[2:]
        traffic = Traffic(
            live_blocks(scalar_refs[0]),
            [(in_refs[i], in_copies[i], *arrays[i][1:]) for i in copied],
            [(ref, copy, axis) for ref, copy, (_, _, axis) in zip(out_refs, out_copies, outs)],
            in_sems,
            out_sems,
        )
        traffic.start()
        kernel(traffic, *scalar_refs, *in_copies, *out_copies, *refs)
        traffic.finish()

    return pl.pallas_call(
        body,
        name=name,
        out_shape=tuple(jax.ShapeDtypeStruct(shape, dtype) for shape, dtype, _ in outs),
        in_specs=[smem] * count
        + [hbm if group is not None else pl.BlockSpec(memory_space=pltpu.VMEM) for _, _, group, _ in arrays],
        out_specs=tuple(hbm for _ in outs),
        scratch_shapes=[held(*arrays[i]) for i in copied]
        + [pltpu.VMEM(shape, dtype) for shape, dtype, _ in outs]
        + [pltpu.SemaphoreType.DMA((ins, blocks)), pltpu.SemaphoreType.DMA((results, blocks))]
        + [pltpu.VMEM(shape, dtype) for shape, dtype in scratch],
        compiler_params=pltpu.CompilerParams(vmem_limit_bytes=VMEM_BYTES),
        cost_estimate=pl.CostEstimate(flops=flops, bytes_accessed=4 << 20, transcendentals=0),
    )(*scalars, *(entry[0] for entry in arrays))


def exchange(part):
    return swap(part, "ffn", 0)


def swap(value, axis, bit):
    count = lax.axis_size(axis)
    return lax.ppermute(value, axis, [(i, i ^ (1 << bit)) for i in range(count)])


def bit_of(axis, bit):
    return (lax.axis_index(axis) >> bit) & 1


def dp_bits():
    return lax.axis_size("dp").bit_length() - 1


def after(value, *others):
    return lax.optimization_barrier((value, *others))[0]


def gather_step(whole, other, bit):
    dim = dp_bits() - 1 - bit
    upper = bit_of("dp", bit) == 1
    return jnp.where(upper, jnp.concatenate([other, whole], axis=dim), jnp.concatenate([whole, other], axis=dim))


def gather_direct(shard, *tokens):
    count = lax.axis_size("dp")
    spread = after(jnp.broadcast_to(shard[None], (count,) + shard.shape), *tokens)
    return lax.all_to_all(spread, "dp", 0, 0, tiled=True).reshape((-1,) + shard.shape[1:])


def reduce_owner(value):
    count = lax.axis_size("dp")
    rows = value.shape[0] // count
    spread = lax.all_to_all(value.astype(BF16).reshape((count, rows) + value.shape[1:]), "dp", 0, 0, tiled=True)
    return jnp.sum(spread.astype(F32), axis=0)


def all_sum(value):
    count = lax.axis_size("dp") * lax.axis_size("ffn")
    spread = jnp.broadcast_to(value.reshape(1, 1), (count, 128))
    return jnp.sum(lax.all_to_all(spread, ("dp", "ffn"), 0, 0, tiled=True)[:, 0])


def adam_update(weight, gradient, first, second, clipped, rate, decay):
    scaled = gradient * clipped
    first_new = BETA_ONE * first + (1.0 - BETA_ONE) * scaled
    second_new = BETA_TWO * second + (1.0 - BETA_TWO) * scaled * scaled
    ratio = (
        first_new
        / (1.0 - BETA_ONE**STEP)
        / (jnp.sqrt(second_new / (1.0 - BETA_TWO**STEP)) + ADAM_EPSILON)
    )
    return (weight - rate * (ratio + decay * weight), first_new, second_new)


def per_device(
    states, teacher_states, lengths, domain_ids, domain_weight, teacher_qkv,
    attn_a, ffn_in, ffn_out, attn_b, vec_d,
    mom1_attn_a, mom1_ffn_in, mom1_ffn_out, mom1_attn_b, mom1_vec_d,
    mom2_attn_a, mom2_ffn_in, mom2_ffn_out, mom2_attn_b, mom2_vec_d,
):
    cores = lax.axis_size("ffn")
    core = lax.axis_index("ffn")
    replicas = lax.axis_size("dp")
    replica = lax.axis_index("dp")
    sequences = lengths.shape[0]
    rows = states.shape[0] // sequences
    features = states.shape[1]
    heads = HEADS // cores
    flat = features // cores
    size = flat // heads
    pairs = heads // 2
    hidden = ffn_in.shape[1]
    teacher_flat = teacher_qkv.shape[2]
    teacher_size = teacher_flat // heads
    shard = attn_a.shape[0]
    matched = domain_ids[:, None] == jnp.arange(domain_weight.shape[0])[None, :]
    sequence_weight = jnp.sum(jnp.where(matched, domain_weight[None, :], 0.0), axis=1) / HEADS

    teacher_w = teacher_qkv.transpose(1, 0, 2)
    statest = states.T
    live = [lengths[i : i + 1] for i in range(sequences)]
    weights = [sequence_weight[i : i + 1] for i in range(sequences)]
    each = range(sequences)
    launch = functools.partial(call, rows // BLOCK)
    act = ((features, rows), BF16)
    wide = ((features, rows), F32)
    head_t = ((heads, size, rows), BF16)
    pair_rows = ((pairs, rows, 2 * size), BF16)

    bound_rows = -(-3 * heads // 8) * 8

    def project_teacher(i, token):
        return launch(
            teacher_kernel, "teacher", (live[i],),
            ((after(teacher_states, *token), 0, 0, i * rows // BLOCK), (teacher_w, None, 0)),
            (
                ((heads, teacher_size, rows), BF16, 2),
                ((pairs, rows, 2 * teacher_size), BF16, 1),
                ((heads, teacher_size, rows), BF16, 2),
                ((pairs, rows, 2 * teacher_size), BF16, 1),
                ((bound_rows, BLOCK), F32, None),
            ),
            flops=2 * rows * 768 * 1152,
        )

    attn_own = lax.dynamic_slice_in_dim(attn_a.reshape(shard, 4, features), core * flat, flat, 2).reshape(shard, 4 * flat)
    early = gather_direct(jnp.concatenate([attn_own, vec_d], axis=1).astype(BF16))
    teacher = [project_teacher(0, (statest,))]
    late_feed = gather_direct(jnp.concatenate([ffn_in, ffn_out], axis=1).astype(BF16), *teacher[0])
    teacher += [project_teacher(i, teacher[0]) for i in each[1:]]
    early = after(early, *teacher[1])
    vec_full = early[:, 4 * flat :].astype(F32)
    vec_own = lax.dynamic_slice_in_dim(vec_full, core * flat, flat, 0)
    attn_full = (early, None, 0, (0, 4 * flat))

    attended = [
        launch(
            attend_kernel, "attend", (live[i],),
            ((statest, 1, 0, i * rows // BLOCK), attn_full, (vec_own, None, 0)),
            ((*head_t, 2), (*head_t, 2), (*pair_rows, 1), (*pair_rows, 1), (*pair_rows, 1),
             ((heads, size, rows), F32, 2), ((heads, 8, rows), F32, 2), (*act, 1)),
            scratch=(((heads, size + 16, rows), BF16), ((-(-2 * heads // 8) * 8, BLOCK), F32)),
            flops=6 * 10**9,
        )
        for i in each
    ]
    in_full, out_full = (late_feed, None, 0, (0, hidden)), (late_feed, None, 0, (hidden, hidden))
    late_rel = gather_direct(after(attn_b.reshape(shard, 3 * flat).astype(BF16), *attended[0]))
    rel_full = (late_rel, None, 0)
    mixed_other = [exchange(attended[i][7]) for i in each]
    fed = [
        launch(
            feed_kernel, "feed", (live[i],),
            ((statest, 1, 0, i * rows // BLOCK), (attended[i][7], 1, 0), (mixed_other[i], None, None), in_full,
             out_full, (vec_full, None, 0)),
            ((*wide, 1), ((hidden, rows), BF16, 1), ((hidden, rows), BF16, 1), (*act, 1)),
            flops=3 * 10**9,
        )
        for i in each
    ]
    fed_other = [exchange(fed[i][3]) for i in each]

    def relate(i, earlier):
        last = i + 1 == sequences
        return launch(
            functools.partial(relation_kernel, bool(earlier)), "relation", (live[i], weights[i]),
            ((fed[i][0], 1, 0), (fed[i][3], 1, 0), (fed_other[i], None, None), rel_full,
             (vec_full, None, 0), (teacher[i][0], 2, 1), (teacher[i][1], 1, 1), (teacher[i][2], 2, 1),
             (teacher[i][3], 1, 1), (teacher[i][4], None, 0), *((value, None, 1) for value in earlier)),
            (((features, 3 * flat), BF16 if last else F32, None), (*act, 1)),
            scratch=(
                ((features, 3 * flat), F32), act, head_t, head_t, head_t, pair_rows, pair_rows, pair_rows,
                head_t, ((heads, size, rows), F32),
                ((pairs, rows, 2 * size), F32), ((pairs, rows, 2 * size), F32), ((bound_rows, BLOCK), F32),
            ),
            flops=30 * 10**9,
        )

    def feed_back(i, earlier):
        last = i + 1 == sequences
        sums = ((features, 8), F32)
        return launch(
            functools.partial(feed_back_kernel, bool(earlier)), "feed_back", (live[i],),
            ((fed[i][0], 1, 0), (fed[i][3], 1, 0), (fed_other[i], None, None), (related[i][1], 1, 0),
             (down_other[i], None, None), (fed[i][1], 1, 0), (fed[i][2], 1, 0), in_full,
             out_full, (vec_full, None, 0), *((value, None, 1) for value in earlier)),
            (((features, 2 * hidden), BF16 if last else F32, None), (*sums, None), (*wide, 1), (*act, 1)),
            scratch=(((features, 2 * hidden), F32), sums),
            flops=4 * 10**9,
        )

    def attend_back(i, earlier):
        last = i + 1 == sequences
        running = (((features, 4 * flat), F32), ((features, 8), F32), ((flat, 8), F32))
        return launch(
            functools.partial(attend_back_kernel, bool(earlier), last), "attend_back",
            (live[i], core.reshape(1).astype(jnp.int32)),
            ((statest, 1, 0, i * rows // BLOCK), (attended[i][7], 1, 0), (mixed_other[i], None, None), (fed_back[i][2], 1, 0),
             (fed_back[i][3], 1, 0), (up_other[i], None, None), attn_full, (vec_full, None, 0),
             (attended[i][0], 2, 1), (attended[i][1], 2, 1), (attended[i][2], 1, 1), (attended[i][3], 1, 1),
             (attended[i][4], 1, 1), (attended[i][5], 2, 0), (attended[i][6], 2, 1),
             *([(fed_back[i][1], None, 0)] if last else []), *((value, None, 1) for value in earlier)),
            (((features, 4 * flat + 8), BF16, None),) if last else tuple((*spec, None) for spec in running),
            scratch=running + (
                head_t, pair_rows, ((heads, 8, rows), F32), head_t,
                ((pairs, rows, 2 * size), F32), ((pairs, rows, 2 * size), F32),
            ),
            flops=15 * 10**9,
        )

    related, down_other = [], []
    for i in each:
        related.append(relate(i, related[-1][:1] if related else ()))
        down_other.append(exchange(related[i][1]))
    shard_rel = reduce_owner(related[-1][0])
    fed_back, up_other = [], []
    for i in each:
        fed_back.append(feed_back(i, fed_back[-1][:2] if fed_back else ()))
        up_other.append(exchange(fed_back[i][3]))
    shard_feed = reduce_owner(fed_back[-1][0])
    attended_back = []
    for i in each:
        attended_back.append(attend_back(i, attended_back[-1] if attended_back else ()))
    shard_in, shard_out = shard_feed[:, :hidden], shard_feed[:, hidden:]
    own = reduce_owner(after(attended_back[-1][0], shard_rel, shard_feed))
    other = swap(own, "ffn", 0)
    grad_rel = shard_rel.reshape(attn_b.shape)
    upper = core == 1
    low, high = jnp.where(upper, other, own), jnp.where(upper, own, other)
    columns = [
        half[:, start : start + flat] for start in range(0, 4 * flat, flat) for half in (low, high)
    ]
    grad_attn = jnp.concatenate(columns, axis=1)
    grad_vec = jnp.concatenate([(low + high)[:, 4 * flat : 4 * flat + 2], own[:, 4 * flat + 2 :]], axis=1)
    gradients = (grad_attn, shard_in, shard_out, grad_rel, grad_vec)
    shared = own[:, 4 * flat + 2 :]
    squares = (
        jnp.sum(own[:, : 4 * flat + 2] * own[:, : 4 * flat + 2])
        + jnp.sum(shared * shared) / cores
        + jnp.sum(shard_feed * shard_feed)
        + jnp.sum(shard_rel * shard_rel)
    )
    grad_norm = jnp.sqrt(all_sum(squares))
    clipped = jnp.minimum(1.0, CLIP_NORM / grad_norm)
    masters = (attn_a, ffn_in, ffn_out, attn_b, vec_d)
    firsts = (mom1_attn_a, mom1_ffn_in, mom1_ffn_out, mom1_attn_b, mom1_vec_d)
    seconds = (mom2_attn_a, mom2_ffn_in, mom2_ffn_out, mom2_attn_b, mom2_vec_d)
    rates = (RATE_MATRIX, RATE_MATRIX, RATE_MATRIX, RATE_MATRIX, RATE_VECTOR)
    decays = (DECAY_RATE, DECAY_RATE, DECAY_RATE, DECAY_RATE, 0.0)
    news = [
        adam_update(masters[i], gradients[i], firsts[i], seconds[i], clipped, rates[i], decays[i])
        for i in range(5)
    ]
    return (grad_norm, *(new[0] for new in news), *(new[1] for new in news), *(new[2] for new in news))


def solution(mesh):
    matrix = P("dp", None)
    halved = P("dp", "ffn")
    cube = P("dp", None, "ffn")
    trained = (matrix, halved, halved, cube, matrix)
    in_specs = (matrix, matrix, P("dp"), P("dp"), P(), P(None, None, "ffn")) + trained * 3
    out_specs = (P(),) + trained * 3
    return jax.shard_map(per_device, mesh=mesh, in_specs=in_specs, out_specs=out_specs, check_vma=False)
```

```python
import functools

import jax
import jax.numpy as jnp
from jax import lax
from jax.experimental import pallas as pl
from jax.experimental.pallas import tpu as pltpu
from jax.sharding import PartitionSpec as P

HEADS = 12
STEP = 10

NORM_EPSILON = 1e-12
CLIP_NORM = 1.0
BETA_ONE = 0.9
BETA_TWO = 0.999
ADAM_EPSILON = 1e-08
RATE_MATRIX = 0.04
RATE_VECTOR = 0.2
DECAY_RATE = 0.01
MASK_VALUE = -1e30
LOG2_E = 1.4426950408889634
BLOCK = 256
SAFE_EXPONENT = 100.0
HELD = -1
VMEM_BYTES = 24 * 2**20
F32 = jnp.float32
BF16 = jnp.bfloat16


def nn(left, right):
    return lax.dot_general(left, right, (((1,), (0,)), ((), ())), preferred_element_type=F32)


def nt(left, right):
    return lax.dot_general(left, right, (((1,), (1,)), ((), ())), preferred_element_type=F32)


def tn(left, right):
    return lax.dot_general(left, right, (((0,), (0,)), ((), ())), preferred_element_type=F32)


def lanes(block):
    return pl.ds(pl.multiple_of(block * BLOCK, BLOCK), BLOCK)


def live_blocks(len_ref):
    return (len_ref[0] + BLOCK - 1) // BLOCK


def for_size(blocks, most, safe, fast, slow):
    for n in range(1, most + 1):
        pl.when(jnp.logical_and(safe, blocks == n))(functools.partial(fast, n))
    pl.when(jnp.logical_not(safe))(slow)


def pipeline(count, first, second, third):
    firsts, seconds = {}, {}
    for t in range(count + 2):
        if t < count:
            firsts[t] = first(t)
        if 0 <= t - 1 < count:
            seconds[t - 1] = second(t - 1, firsts.pop(t - 1))
        if 0 <= t - 2 < count:
            third(t - 2, seconds.pop(t - 2))


def squared_lengths(flat, size):
    features = flat.shape[0]
    groups = -(-features // size // 8) * 8
    row = lax.broadcasted_iota(jnp.int32, (groups, features), 0)
    column = lax.broadcasted_iota(jnp.int32, (groups, features), 1)
    ones = jnp.where((column >= row * size) & (column < (row + 1) * size), 1.0, 0.0).astype(BF16)
    return nn(ones, flat * flat)


def clear_dead(blocks, rows, *refs):
    def step(block, carry):
        for ref in refs:
            ref[:, :, lanes(block)] = jnp.zeros(ref.shape[:2] + (BLOCK,), ref.dtype)
        return carry

    lax.fori_loop(blocks, rows // BLOCK, step, 0)


def norm_forward(resid):
    features = resid.shape[0]
    centred = resid - jnp.sum(resid, axis=0, keepdims=True) * (1.0 / features)
    variance = jnp.sum(centred * centred, axis=0, keepdims=True) * (1.0 / features)
    inverse = lax.rsqrt(variance + NORM_EPSILON)
    return centred * inverse, inverse


def norm_backward(scaled, normed, inverse):
    features = scaled.shape[0]
    mean = jnp.sum(scaled, axis=0, keepdims=True) * (1.0 / features)
    slope = jnp.sum(scaled * normed, axis=0, keepdims=True) * (1.0 / features)
    return inverse * (scaled - mean - normed * slope)


def mask_tail(scores, n, length, start=None):
    start = (n - 1) * BLOCK if start is None else start
    rows = start + lax.broadcasted_iota(jnp.int32, (n * BLOCK - start, scores.shape[1]), 0)
    tail = jnp.where(rows < length, scores[start:], MASK_VALUE)
    if start == 0:
        return tail
    return jnp.concatenate([scores[:start], tail], axis=0)


def pad_rows(part, index, count):
    zeros = jnp.zeros_like(part)
    return jnp.concatenate([part if i == index else zeros for i in range(count)], axis=0)


def pad_lanes(pair, index, size):
    lane = lax.broadcasted_iota(jnp.int32, pair.shape, 1)
    return jnp.where((lane >= index * size) & (lane < (index + 1) * size), pair, jnp.zeros_like(pair))


def split_heads(flat, ref, columns, size):
    heads = flat.shape[0] // size
    for head in range(heads):
        ref[head, :, columns] = flat[head * size : (head + 1) * size]


def split_pairs(flat, ref, rows):
    pairs, width = ref.shape[0], ref.shape[2]
    for pair in range(pairs):
        ref[pair, rows, :] = flat[pair * width : (pair + 1) * width].T


def teacher_kernel(traffic, len_ref, rows_ref, weight_ref, qt_ref, k_ref, vt_ref, v_ref, bound_ref):
    size = qt_ref.shape[1]
    bound_ref[...] = jnp.zeros(bound_ref.shape, F32)

    def step(block, carry):
        where = lanes(block)
        traffic.take(block)
        rows = rows_ref[where, :]
        queries, keys, values = [nn(rows, weight_ref[index]).astype(BF16) for index in range(3)]
        columns = [part.T for part in (queries, keys, values)]
        bound_ref[...] = jnp.maximum(bound_ref[...], squared_lengths(jnp.concatenate(columns, axis=0), size))
        split_heads(columns[0], qt_ref, where, size)
        split_heads(columns[2], vt_ref, where, size)
        for pair in range(k_ref.shape[0]):
            k_ref[pair, where, :] = keys[:, 2 * size * pair : 2 * size * (pair + 1)]
            v_ref[pair, where, :] = values[:, 2 * size * pair : 2 * size * (pair + 1)]
        traffic.give(block, 0, 1, 2, 3)
        return carry

    lax.fori_loop(0, live_blocks(len_ref), step, 0)


def attend_kernel(
    traffic, len_ref, xt_ref, weight_ref, vec_ref, qt_ref, kt_ref, q_ref, k_ref, v_ref, ot_ref, lse_ref, at_ref,
    vone_ref, bound_ref,
):
    heads, size, rows = qt_ref.shape
    flat = heads * size
    scaling = LOG2_E * size ** (-0.5)
    blocks = live_blocks(len_ref)
    length = len_ref[0]
    bound_ref[...] = jnp.zeros(bound_ref.shape, F32)

    def project(block, carry):
        where = lanes(block)
        traffic.take(block)
        xt = xt_ref[:, where]
        projected = tn(weight_ref[:, : 3 * flat], xt)
        query = (projected[:flat] + vec_ref[:, 0:1]).astype(BF16)
        keys = projected[flat : 2 * flat].astype(BF16)
        values = (projected[2 * flat :] + vec_ref[:, 1:2]).astype(BF16)
        split_heads(query, qt_ref, where, size)
        split_heads(keys, kt_ref, where, size)
        bound_ref[...] = jnp.maximum(
            bound_ref[...], squared_lengths(jnp.concatenate([query, keys], axis=0), size)
        )
        column = block * BLOCK + lax.broadcasted_iota(jnp.int32, (1, BLOCK), 1)
        live = jnp.where(column < length, 1.0, 0.0)
        live_values = (values.astype(F32) * live).astype(BF16)
        for head in range(heads):
            vone_ref[head, :size, where] = live_values[head * size : (head + 1) * size]
            vone_ref[head, size:, where] = jnp.broadcast_to(live, (16, BLOCK)).astype(BF16)
        split_pairs(query, q_ref, where)
        split_pairs(keys, k_ref, where)
        split_pairs(values, v_ref, where)
        traffic.give(block, 0, 1, 2, 3, 4)
        return carry

    lax.fori_loop(0, blocks, project, 0)

    longest = jnp.max(bound_ref[...], axis=1, keepdims=True)
    safe = jnp.max(longest[:heads] * longest[heads : 2 * heads]) * scaling**2 <= SAFE_EXPONENT**2

    def scores(head, where, n):
        return nn(k_ref[head // 2, : n * BLOCK, :], pad_rows(qt_ref[head, :, where], head % 2, 2))

    def mix(head, where, n, grown, top):
        mixed = nn(vone_ref[head, :, : n * BLOCK], grown)
        total = mixed[size : size + 1]
        ot_ref[head, :, where] = mixed[:size] * (1.0 / total)
        lse_ref[head, :, where] = jnp.broadcast_to(top + jnp.log2(total), (8, BLOCK))

    def fast(n):
        def step(block, carry):
            where = lanes(block)
            pipeline(
                heads,
                lambda head: scores(head, where, n),
                lambda head, score: jnp.exp2(score * scaling).astype(BF16),
                lambda head, grown: mix(head, where, n, grown, 0.0),
            )
            traffic.give(block, 5, 6)
            return carry

        lax.fori_loop(0, n, step, 0)

    def slow():
        most = rows // BLOCK
        clear_dead(blocks, rows, vone_ref)

        def step(block, carry):
            where = lanes(block)
            for head in range(heads):
                score = mask_tail(scores(head, where, most), most, length, 0)
                top = jnp.max(score, axis=0, keepdims=True) * scaling
                mix(head, where, most, jnp.exp2(score * scaling - top).astype(BF16), top)
            traffic.give(block, 5, 6)
            return carry

        lax.fori_loop(0, blocks, step, 0)

    for_size(blocks, rows // BLOCK, safe, fast, slow)

    def output(block, carry):
        where = lanes(block)
        mixed = ot_ref[:, :, where].reshape(flat, BLOCK).astype(BF16)
        at_ref[:, where] = nn(weight_ref[:, 3 * flat :], mixed).astype(BF16)
        traffic.give(block, 7)
        return carry

    lax.fori_loop(0, blocks, output, 0)


def first_norm(xt, own, other, vec_ref):
    resid = xt.astype(F32) + (own.astype(F32) + other.astype(F32)) + vec_ref[:, 2:3]
    return norm_forward(resid)


def erf(value):
    return lax.erf(value)


def feed_kernel(traffic, len_ref, xt_ref, own_ref, other_ref, in_ref, out_ref, vec_ref, ht_ref, zt_ref, slope_ref, ft_ref):
    def step(block, carry):
        where = lanes(block)
        traffic.take(block)
        normed, _ = first_norm(xt_ref[:, where], own_ref[:, where], other_ref[:, where], vec_ref)
        hidden = normed * vec_ref[:, 3:4] + vec_ref[:, 4:5]
        ht_ref[:, where] = hidden
        pre = tn(in_ref[...], hidden.astype(BF16))
        cdf = 0.5 + 0.5 * erf(pre * (0.5**0.5))
        pdf = jnp.exp2(pre * pre * (-0.5 * LOG2_E)) * 0.3989422804014327
        active = (pre * cdf).astype(BF16)
        zt_ref[:, where] = active
        slope_ref[:, where] = (cdf + pre * pdf).astype(BF16)
        ft_ref[:, where] = nn(out_ref[...], active).astype(BF16)
        traffic.give(block, 0, 1, 2, 3)
        return carry

    lax.fori_loop(0, live_blocks(len_ref), step, 0)


def second_norm(ht, own, other, vec_ref):
    resid = ht + (own.astype(F32) + other.astype(F32)) + vec_ref[:, 5:6]
    return norm_forward(resid)


def relation_kernel(
    chained, traffic, len_ref, weight_ref, ht_ref, own_ref, other_ref, rel_ref, vec_ref, tqt_ref, tk_ref, tvt_ref, tv_ref,
    tbound_ref, *refs,
):
    earlier_ref, refs = (refs[0], refs[1:]) if chained else (None, refs)
    grad_out_ref, dt_ref, refs = refs[0], refs[1], refs[2:]
    grad_ref, refs = refs[0], refs[1:]
    relation_body(
        traffic, len_ref, weight_ref, ht_ref, own_ref, other_ref, rel_ref, vec_ref, tqt_ref, tk_ref, tvt_ref, tv_ref,
        tbound_ref, grad_ref, dt_ref, *refs,
    )
    traffic.take_last()
    grad = grad_ref[...] + earlier_ref[...] if chained else grad_ref[...]
    grad_out_ref[...] = grad.astype(grad_out_ref.dtype)


def relation_body(
    traffic, len_ref, weight_ref, ht_ref, own_ref, other_ref, rel_ref, vec_ref, tqt_ref, tk_ref, tvt_ref, tv_ref,
    tbound_ref, grad_ref, dt_ref,
    h2_ref, qt_ref, kt_ref, vt_ref, q_ref, k_ref, v_ref, dqt_ref, dvt_ref, dk_ref, dv_ref, bound_ref,
):
    heads, size, rows = qt_ref.shape
    teacher_size = tqt_ref.shape[1]
    flat = heads * size
    plain = size ** (-0.5)
    scaling = LOG2_E * plain
    teacher_scaling = LOG2_E * teacher_size ** (-0.5)
    blocks = live_blocks(len_ref)
    length = len_ref[0]
    weight = weight_ref[0]
    bound_ref[...] = jnp.zeros(bound_ref.shape, F32)

    def project(block, carry):
        where = lanes(block)
        traffic.take(block)
        normed, _ = second_norm(ht_ref[:, where], own_ref[:, where], other_ref[:, where], vec_ref)
        hidden = (normed * vec_ref[:, 6:7] + vec_ref[:, 7:8]).astype(BF16)
        h2_ref[:, where] = hidden
        projected = tn(rel_ref[...], hidden).astype(BF16)
        bound_ref[...] = jnp.maximum(bound_ref[...], squared_lengths(projected, size))
        split_heads(projected[:flat], qt_ref, where, size)
        split_heads(projected[flat : 2 * flat], kt_ref, where, size)
        split_heads(projected[2 * flat :], vt_ref, where, size)
        split_pairs(projected[:flat], q_ref, where)
        split_pairs(projected[flat : 2 * flat], k_ref, where)
        split_pairs(projected[2 * flat :], v_ref, where)
        for pair in range(heads // 2):
            dk_ref[pair, where, :] = jnp.zeros((BLOCK, 2 * size), F32)
            dv_ref[pair, where, :] = jnp.zeros((BLOCK, 2 * size), F32)
        return carry

    lax.fori_loop(0, blocks, project, 0)

    traffic.take_rest()

    def exponents(ref, scale):
        longest = jnp.max(ref[...], axis=1, keepdims=True)
        attention = jnp.max(longest[:heads] * longest[heads : 2 * heads]) * scale**2
        relation = jnp.max(longest[2 * heads : 3 * heads]) * scale
        return jnp.logical_and(attention <= SAFE_EXPONENT**2, relation <= SAFE_EXPONENT)

    safe = jnp.logical_and(exponents(bound_ref, scaling), exponents(tbound_ref, teacher_scaling))
    pairs = heads // 2
    attention = (k_ref, qt_ref, q_ref, tk_ref, tqt_ref, kt_ref, dqt_ref, dk_ref)
    relation = (v_ref, vt_ref, v_ref, tv_ref, tvt_ref, vt_ref, dvt_ref, dv_ref)
    tasks = [(half, refs) for refs in (attention, relation) for half in range(2)]

    def steps(n, pair, where, mask, grow):
        column = where.start + lax.broadcasted_iota(jnp.int32, (1, BLOCK), 1)
        live = jnp.where(column < length, weight, 0.0)
        kept = {}

        def first(t):
            half, (left, rightt, _, teacher_left, teacher_rightt, _, _, _) = tasks[t]
            head = 2 * pair + half
            student = nn(left[pair, : n * BLOCK, :], pad_rows(rightt[head, :, where], half, 2))
            teacher = nn(teacher_left[pair, : n * BLOCK, :], pad_rows(teacher_rightt[head, :, where], half, 2))
            return student, teacher

        def second(t, scores):
            student, teacher = grow(mask(scores[0]), scaling), grow(mask(scores[1]), teacher_scaling)
            student_part = live / jnp.sum(student, axis=0, keepdims=True)
            teacher_part = live / jnp.sum(teacher, axis=0, keepdims=True)
            return (student * student_part - teacher * teacher_part).astype(BF16)

        def third(t, grad):
            half, (_, _, right, _, _, leftt, own_ref, running_ref) = tasks[t]
            head = 2 * pair + half
            own_ref[head, :, where] = (nn(leftt[head, :, : n * BLOCK], grad) * plain).astype(own_ref.dtype)
            kept[half] = grad
            if half == 1:
                queries = right[pair, where, :]
                stacked = jnp.concatenate([pad_lanes(queries, i, size) for i in range(2)], axis=0)
                running_ref[pair, : n * BLOCK, :] += nn(jnp.concatenate([kept[0], kept[1]], axis=1), stacked)

        return first, second, third

    def fast(n):
        def step(index, carry):
            stages = steps(
                n, index % pairs, lanes(index // pairs), lambda score: mask_tail(score, n, length),
                lambda score, scale: jnp.exp2(score * scale),
            )
            pipeline(len(tasks), *stages)
            return carry

        lax.fori_loop(0, n * pairs, step, 0)

    def slow():
        most = rows // BLOCK
        clear_dead(blocks, rows, kt_ref, vt_ref)

        def grow(score, scale):
            return jnp.exp2(score * scale - jnp.max(score, axis=0, keepdims=True) * scale)

        def step(index, carry):
            first, second, third = steps(
                most, index % pairs, lanes(index // pairs), lambda score: mask_tail(score, most, length, 0), grow
            )
            for t in range(len(tasks)):
                third(t, second(t, first(t)))
            return carry

        lax.fori_loop(0, blocks * pairs, step, 0)

    for_size(blocks, rows // BLOCK, safe, fast, slow)
    grad_ref[...] = jnp.zeros(grad_ref.shape, F32)

    def finish(block, carry):
        where = lanes(block)
        queries = dqt_ref[:, :, where].reshape(flat, BLOCK)
        keys = jnp.concatenate([dk_ref[pair, where, :].T for pair in range(heads // 2)], axis=0) * plain
        values = jnp.concatenate([dv_ref[pair, where, :].T for pair in range(heads // 2)], axis=0) * plain
        values = values + dvt_ref[:, :, where].reshape(flat, BLOCK)
        grads = jnp.concatenate([queries, keys.astype(BF16), values.astype(BF16)], axis=0)
        grad_ref[...] += nt(h2_ref[:, where], grads)
        dt_ref[:, where] = nn(rel_ref[...], grads).astype(BF16)
        traffic.give(block, 1)
        return carry

    lax.fori_loop(0, blocks, finish, 0)


def feed_back_kernel(
    chained, traffic, len_ref, ht_ref, own_ref, other_ref, down_own_ref, down_other_ref, zt_ref, slope_ref, in_ref, out_ref, vec_ref, *refs,
):
    earlier, refs = (refs[:2], refs[2:]) if chained else (None, refs)
    total_ref, sums_out_ref, resid_ref, up_ref, refs = *refs[:4], refs[4:]
    grad_ref, sums_ref = refs
    hidden_units = in_ref.shape[1]
    grad_ref[...] = jnp.zeros(grad_ref.shape, F32)
    sums_ref[...] = jnp.zeros(sums_ref.shape, F32)

    def step(block, carry):
        where = lanes(block)
        traffic.take(block)
        hidden = ht_ref[:, where]
        normed, inverse = second_norm(hidden, own_ref[:, where], other_ref[:, where], vec_ref)
        grad = down_own_ref[:, where].astype(F32) + down_other_ref[:, where].astype(F32)
        resid = norm_backward(grad * vec_ref[:, 6:7], normed, inverse)
        resid_ref[:, where] = resid
        sums_ref[:, 0:1] += jnp.sum(resid, axis=1, keepdims=True)
        sums_ref[:, 1:2] += jnp.sum(grad * normed, axis=1, keepdims=True)
        sums_ref[:, 2:3] += jnp.sum(grad, axis=1, keepdims=True)
        branch = resid.astype(BF16)
        grad_ref[:, hidden_units:] += nt(branch, zt_ref[:, where])
        pre_grad = (tn(out_ref[...], branch) * slope_ref[:, where].astype(F32)).astype(BF16)
        grad_ref[:, :hidden_units] += nt(hidden.astype(BF16), pre_grad)
        up_ref[:, where] = nn(in_ref[...], pre_grad).astype(BF16)
        traffic.give(block, 2, 3)
        return carry

    lax.fori_loop(0, live_blocks(len_ref), step, 0)
    traffic.take_last()
    grad, sums = grad_ref[...], sums_ref[...]
    if chained:
        grad, sums = grad + earlier[0][...], sums + earlier[1][...]
    total_ref[...] = grad.astype(total_ref.dtype)
    sums_out_ref[...] = sums


def attend_back_kernel(
    chained, last, traffic, len_ref, core_ref, xt_ref, own_ref, other_ref, resid_ref, up_own_ref, up_other_ref, weight_ref, vec_ref,
    qt_ref, kt_ref, q_ref, k_ref, v_ref, ot_ref, lse_ref, *refs,
):
    back_sums_ref, refs = (refs[0], refs[1:]) if last else (None, refs)
    earlier, refs = (refs[:3], refs[3:]) if chained else (None, refs)
    outs, refs = (refs[:1], refs[1:]) if last else (refs[:3], refs[3:])
    running, refs = refs[:3], refs[3:]
    grad_ref, sums_ref, head_sums_ref = running
    for ref in running:
        ref[...] = jnp.zeros(ref.shape, F32)
    attend_back_body(
        traffic, len_ref, xt_ref, own_ref, other_ref, resid_ref, up_own_ref, up_other_ref, weight_ref, vec_ref,
        qt_ref, kt_ref, q_ref, k_ref, v_ref, ot_ref, lse_ref, grad_ref, sums_ref, head_sums_ref, *refs,
    )
    traffic.take_last()
    if chained:
        for ref, value in zip(running, earlier):
            ref[...] += value[...]
    if not last:
        for ref, value in zip(outs, running):
            ref[...] = value[...]
        return
    total_ref = outs[0]
    columns, flat = grad_ref.shape[1], head_sums_ref.shape[0]
    total_ref[:, :columns] = grad_ref[...].astype(BF16)
    biases = head_sums_ref[:, 0:2].astype(BF16)
    total_ref[:, columns : columns + 2] = jnp.zeros((total_ref.shape[0], 2), BF16)
    for core in range(total_ref.shape[0] // flat):

        @pl.when(core_ref[0] == core)
        def _(core=core):
            total_ref[core * flat : (core + 1) * flat, columns : columns + 2] = biases

    total_ref[:, columns + 2 : columns + 5] = sums_ref[:, 0:3].astype(BF16)
    total_ref[:, columns + 5 : columns + 8] = back_sums_ref[:, 0:3].astype(BF16)


def attend_back_body(
    traffic, len_ref, xt_ref, own_ref, other_ref, resid_ref, up_own_ref, up_other_ref, weight_ref, vec_ref,
    qt_ref, kt_ref, q_ref, k_ref, v_ref, ot_ref, lse_ref, grad_ref, sums_ref, head_sums_ref,
    dot_ref, do_ref, inner_ref, dqt_ref, dk_ref, dv_ref,
):
    heads, size, rows = qt_ref.shape
    flat = heads * size
    plain = size ** (-0.5)
    scaling = LOG2_E * plain
    blocks = live_blocks(len_ref)
    length = len_ref[0]

    def start(block, carry):
        where = lanes(block)
        traffic.take(block)
        normed, inverse = first_norm(xt_ref[:, where], own_ref[:, where], other_ref[:, where], vec_ref)
        grad = resid_ref[:, where] + (up_own_ref[:, where].astype(F32) + up_other_ref[:, where].astype(F32))
        branch = norm_backward(grad * vec_ref[:, 3:4], normed, inverse).astype(BF16)
        sums_ref[:, 0:1] += jnp.sum(branch.astype(F32), axis=1, keepdims=True)
        sums_ref[:, 1:2] += jnp.sum(grad * normed, axis=1, keepdims=True)
        sums_ref[:, 2:3] += jnp.sum(grad, axis=1, keepdims=True)
        mixed = ot_ref[:, :, where]
        grad_ref[:, 3 * flat :] += nt(branch, mixed.reshape(flat, BLOCK).astype(BF16))
        mixed_grad = tn(weight_ref[:, 3 * flat :], branch).astype(BF16)
        split_heads(mixed_grad, dot_ref, where, size)
        split_pairs(mixed_grad, do_ref, where)
        for head in range(heads):
            product = mixed_grad[head * size : (head + 1) * size].astype(F32) * mixed[head]
            inner_ref[head, :, where] = jnp.broadcast_to(jnp.sum(product, axis=0, keepdims=True), (8, BLOCK))
        for pair in range(heads // 2):
            dk_ref[pair, where, :] = jnp.zeros((BLOCK, 2 * size), F32)
            dv_ref[pair, where, :] = jnp.zeros((BLOCK, 2 * size), F32)
        return carry

    lax.fori_loop(0, blocks, start, 0)
    traffic.take_rest()

    def attend(n):
        def step(block, carry):
            where = lanes(block)
            kept = {}

            def first(head):
                pair, half = head // 2, head % 2
                scores = nn(k_ref[pair, : n * BLOCK, :], pad_rows(qt_ref[head, :, where], half, 2))
                prob_grad = nn(v_ref[pair, : n * BLOCK, :], pad_rows(dot_ref[head, :, where], half, 2))
                return scores, prob_grad

            def second(head, parts):
                scores, prob_grad = parts
                prob = jnp.exp2(mask_tail(scores, n, length) * scaling - lse_ref[head, 0:1, where])
                grad = (prob * (prob_grad - inner_ref[head, 0:1, where])).astype(BF16)
                return prob.astype(BF16), grad

            def third(head, parts):
                pair = head // 2
                dqt_ref[head, :, where] = (nn(kt_ref[head, :, : n * BLOCK], parts[1]) * plain).astype(BF16)
                kept[head % 2] = parts
                if head % 2 == 1:
                    for index, right, running in ((1, q_ref, dk_ref), (0, do_ref, dv_ref)):
                        queries = right[pair, where, :]
                        stacked = jnp.concatenate([pad_lanes(queries, half, size) for half in range(2)], axis=0)
                        running[pair, : n * BLOCK, :] += nn(
                            jnp.concatenate([kept[0][index], kept[1][index]], axis=1), stacked
                        )

            pipeline(heads, first, second, third)
            return carry

        lax.fori_loop(0, n, step, 0)

    for n in range(1, rows // BLOCK + 1):
        pl.when(blocks == n)(functools.partial(attend, n))

    def finish(block, carry):
        where = lanes(block)
        queries = dqt_ref[:, :, where].reshape(flat, BLOCK)
        keys = jnp.concatenate([dk_ref[pair, where, :].T for pair in range(heads // 2)], axis=0) * plain
        values = jnp.concatenate([dv_ref[pair, where, :].T for pair in range(heads // 2)], axis=0).astype(BF16)
        head_sums_ref[:, 0:1] += jnp.sum(queries.astype(F32), axis=1, keepdims=True)
        head_sums_ref[:, 1:2] += jnp.sum(values.astype(F32), axis=1, keepdims=True)
        grads = jnp.concatenate([queries, keys.astype(BF16), values], axis=0)
        grad_ref[:, : 3 * flat] += nt(xt_ref[:, where], grads)
        return carry

    lax.fori_loop(0, blocks, finish, 0)


class Traffic:
    def __init__(self, blocks, ins, outs, in_sems, out_sems):
        self.blocks, self.ins, self.outs, self.in_sems, self.out_sems = blocks, ins, outs, in_sems, out_sems

    def part(self, ref, axis, block):
        return ref if axis is None else ref.at[(slice(None),) * axis + (lanes(block),)]

    def inward(self, index, block):
        source, target, axis, _, first = self.ins[index]
        if axis is None:
            if first:
                source = source.at[:, first[0] : first[0] + first[1]]
            return pltpu.make_async_copy(source, target, self.in_sems.at[index, 0])
        return pltpu.make_async_copy(
            self.part(source, axis, first + block), self.part(target, axis, block), self.in_sems.at[index, block]
        )

    def outward(self, index, block):
        target, source, axis = self.outs[index]
        return pltpu.make_async_copy(
            self.part(source, axis, block), self.part(target, axis, block), self.out_sems.at[index, block]
        )

    def chosen(self, group, whole=False):
        return [i for i, entry in enumerate(self.ins) if (entry[2] is None) == whole and entry[3] == group]

    def start(self):
        for index in self.chosen(0, whole=True):
            self.inward(index, 0).start()
        for group in (0, 1):
            indices = self.chosen(group)

            def step(block, carry):
                for index in indices:
                    self.inward(index, block).start()
                return carry

            if indices:
                lax.fori_loop(0, self.blocks, step, 0)
        for index in self.chosen(1, whole=True):
            self.inward(index, 0).start()
        for index in self.chosen(0, whole=True):
            self.inward(index, 0).wait()

    def take(self, block):
        for index in self.chosen(0):
            self.inward(index, block).wait()

    def take_rest(self):
        def step(block, carry):
            for index in self.chosen(1):
                self.inward(index, block).wait()
            return carry

        lax.fori_loop(0, self.blocks, step, 0)

    def take_last(self):
        for index in self.chosen(1, whole=True):
            self.inward(index, 0).wait()

    def give(self, block, *indices):
        for index in indices:
            if self.outs[index][2] != HELD:
                self.outward(index, block).start()

    def finish(self):
        whole = [i for i, entry in enumerate(self.outs) if entry[2] is None]
        parts = [i for i, entry in enumerate(self.outs) if entry[2] not in (None, HELD)]
        for index in whole:
            self.outward(index, 0).start()

        def step(block, carry):
            for index in parts:
                self.outward(index, block).wait()
            return carry

        if parts:
            lax.fori_loop(0, self.blocks, step, 0)
        for index in whole:
            self.outward(index, 0).wait()


def call(blocks, kernel, name, scalars, arrays, outs, scratch=(), flops=0):
    smem = pl.BlockSpec(memory_space=pltpu.SMEM)
    hbm = pl.BlockSpec(memory_space=pltpu.HBM)
    vmem = pl.BlockSpec(memory_space=pltpu.VMEM)
    arrays = [entry if len(entry) == 4 else (*entry, 0) for entry in arrays]

    def held(array, axis, group, first):
        shape = list(array.shape)
        if axis is not None:
            shape[axis] = blocks * BLOCK
        elif first:
            shape[1] = first[1]
        return pltpu.VMEM(tuple(shape), array.dtype)

    count, ins, results = len(scalars), len(arrays), len(outs)
    copied = [i for i in range(ins) if arrays[i][2] != HELD]
    filled = [i for i in range(results) if outs[i][2] != HELD]

    def view(ref, axis, group, first):
        if group != HELD or not first:
            return ref
        if axis is None:
            return ref.at[:, first[0] : first[0] + first[1]]
        return ref.at[(slice(None),) * axis + (slice(first * BLOCK, (first + blocks) * BLOCK),)]

    def body(*refs):
        scalar_refs, refs = refs[:count], refs[count:]
        in_refs, refs = refs[:ins], refs[ins:]
        out_refs, refs = refs[:results], refs[results:]
        in_copies = [view(ref, *entry[1:]) for ref, entry in zip(in_refs, arrays)]
        for index, ref in zip(copied, refs):
            in_copies[index] = ref
        refs = refs[len(copied) :]
        out_copies = list(out_refs)
        for index, ref in zip(filled, refs):
            out_copies[index] = ref
        refs = refs[len(filled) :]
        in_sems, out_sems, refs = refs[0], refs[1], refs[2:]
        traffic = Traffic(
            live_blocks(scalar_refs[0]),
            [(in_refs[i], in_copies[i], *arrays[i][1:]) for i in copied],
            [(ref, copy, axis) for ref, copy, (_, _, axis) in zip(out_refs, out_copies, outs)],
            in_sems,
            out_sems,
        )
        traffic.start()
        kernel(traffic, *scalar_refs, *in_copies, *out_copies, *refs)
        traffic.finish()

    return pl.pallas_call(
        body,
        name=name,
        out_shape=tuple(
            (pltpu.VMEM if axis == HELD else pltpu.HBM)(shape, dtype) for shape, dtype, axis in outs
        ),
        in_specs=[smem] * count
        + [vmem if group == HELD else hbm for _, _, group, _ in arrays],
        out_specs=tuple(vmem if axis == HELD else hbm for _, _, axis in outs),
        scratch_shapes=[held(*arrays[i]) for i in copied]
        + [pltpu.VMEM(*outs[i][:2]) for i in filled]
        + [pltpu.SemaphoreType.DMA((ins, blocks)), pltpu.SemaphoreType.DMA((results, blocks))]
        + [pltpu.VMEM(shape, dtype) for shape, dtype in scratch],
        compiler_params=pltpu.CompilerParams(vmem_limit_bytes=VMEM_BYTES),
        cost_estimate=pl.CostEstimate(flops=flops, bytes_accessed=4 << 20, transcendentals=0),
    )(
        *scalars,
        *(
            pltpu.with_memory_space_constraint(array, pltpu.VMEM if group == HELD else pltpu.HBM)
            for array, _, group, _ in arrays
        ),
    )


def exchange(part):
    return swap(part, "ffn", 0)


def swap(value, axis, bit):
    count = lax.axis_size(axis)
    return lax.ppermute(value, axis, [(i, i ^ (1 << bit)) for i in range(count)])


def bit_of(axis, bit):
    return (lax.axis_index(axis) >> bit) & 1


def dp_bits():
    return lax.axis_size("dp").bit_length() - 1


def after(value, *others):
    return lax.optimization_barrier((value, *others))[0]


def gather_step(whole, other, bit):
    dim = dp_bits() - 1 - bit
    upper = bit_of("dp", bit) == 1
    return jnp.where(upper, jnp.concatenate([other, whole], axis=dim), jnp.concatenate([whole, other], axis=dim))


def gather_direct(shard, *tokens):
    count = lax.axis_size("dp")
    spread = after(jnp.broadcast_to(shard[None], (count,) + shard.shape), *tokens)
    return lax.all_to_all(spread, "dp", 0, 0, tiled=True).reshape((-1,) + shard.shape[1:])


def collect_kernel(shared_columns, shared_weight, squares_ref, spread_ref, own_ref, message_ref):
    own = spread_ref[0].astype(F32)
    for source in range(1, spread_ref.shape[0]):
        own = own + spread_ref[source].astype(F32)
    own_ref[...] = own
    column = lax.broadcasted_iota(jnp.int32, own.shape, 1)
    weights = jnp.where(column < own.shape[1] - shared_columns, 1.0, shared_weight)
    squares = jnp.sum(jnp.sum(own * own * weights, axis=0, keepdims=True), axis=1, keepdims=True)
    message_ref[...] = jnp.broadcast_to(squares + squares_ref[0], message_ref.shape)


def collect(spread, squares, shared_columns, shared_weight):
    vmem = pl.BlockSpec(memory_space=pltpu.VMEM)
    count = lax.axis_size("dp") * lax.axis_size("ffn")
    return pl.pallas_call(
        functools.partial(collect_kernel, shared_columns, shared_weight),
        name="collect",
        out_shape=(pltpu.VMEM(spread.shape[1:], F32), pltpu.VMEM((count, 128), F32)),
        in_specs=[pl.BlockSpec(memory_space=pltpu.SMEM), vmem],
        out_specs=(vmem, vmem),
    )(squares.reshape(1), pltpu.with_memory_space_constraint(spread, pltpu.VMEM))


def send_owner(value):
    count = lax.axis_size("dp")
    rows = value.shape[0] // count
    return lax.all_to_all(value.astype(BF16).reshape((count, rows) + value.shape[1:]), "dp", 0, 0, tiled=True)


def add_parts(spread):
    return jnp.sum(spread.astype(F32), axis=0)


def adam_update(weight, gradient, first, second, clipped, rate, decay):
    scaled = gradient * clipped
    first_new = BETA_ONE * first + (1.0 - BETA_ONE) * scaled
    second_new = BETA_TWO * second + (1.0 - BETA_TWO) * scaled * scaled
    ratio = (
        first_new
        / (1.0 - BETA_ONE**STEP)
        / (jnp.sqrt(second_new / (1.0 - BETA_TWO**STEP)) + ADAM_EPSILON)
    )
    return (weight - rate * (ratio + decay * weight), first_new, second_new)


def per_device(
    states, teacher_states, lengths, domain_ids, domain_weight, teacher_qkv,
    attn_a, ffn_in, ffn_out, attn_b, vec_d,
    mom1_attn_a, mom1_ffn_in, mom1_ffn_out, mom1_attn_b, mom1_vec_d,
    mom2_attn_a, mom2_ffn_in, mom2_ffn_out, mom2_attn_b, mom2_vec_d,
):
    cores = lax.axis_size("ffn")
    core = lax.axis_index("ffn")
    replicas = lax.axis_size("dp")
    replica = lax.axis_index("dp")
    sequences = lengths.shape[0]
    rows = states.shape[0] // sequences
    features = states.shape[1]
    heads = HEADS // cores
    flat = features // cores
    size = flat // heads
    pairs = heads // 2
    hidden = ffn_in.shape[1]
    teacher_flat = teacher_qkv.shape[2]
    teacher_size = teacher_flat // heads
    shard = attn_a.shape[0]
    matched = domain_ids[:, None] == jnp.arange(domain_weight.shape[0])[None, :]
    sequence_weight = jnp.sum(jnp.where(matched, domain_weight[None, :], 0.0), axis=1) / HEADS

    teacher_w = teacher_qkv.transpose(1, 0, 2)
    statest = states.T
    live = [lengths[i : i + 1] for i in range(sequences)]
    weights = [sequence_weight[i : i + 1] for i in range(sequences)]
    each = range(sequences)
    launch = functools.partial(call, rows // BLOCK)
    act = ((features, rows), BF16)
    wide = ((features, rows), F32)
    head_t = ((heads, size, rows), BF16)
    pair_rows = ((pairs, rows, 2 * size), BF16)

    bound_rows = -(-3 * heads // 8) * 8

    def project_teacher(i, token):
        return launch(
            teacher_kernel, "teacher", (live[i],),
            ((after(teacher_states, *token), 0, 0, i * rows // BLOCK), (teacher_w, None, 0)),
            (
                ((heads, teacher_size, rows), BF16, 2),
                ((pairs, rows, 2 * teacher_size), BF16, 1),
                ((heads, teacher_size, rows), BF16, 2),
                ((pairs, rows, 2 * teacher_size), BF16, 1),
                ((bound_rows, BLOCK), F32, None),
            ),
            flops=2 * rows * 768 * 1152,
        )

    attn_own = lax.dynamic_slice_in_dim(attn_a.reshape(shard, 4, features), core * flat, flat, 2).reshape(shard, 4 * flat)
    early = gather_direct(jnp.concatenate([attn_own, vec_d], axis=1).astype(BF16))
    teacher = [project_teacher(i, (statest,)) for i in each]
    late_feed = gather_direct(jnp.concatenate([ffn_in, ffn_out], axis=1).astype(BF16), *teacher[0], *teacher[1])
    early = after(early, *teacher[0], *teacher[1])
    vec_full = early[:, 4 * flat :].astype(F32)
    vec_own = lax.dynamic_slice_in_dim(vec_full, core * flat, flat, 0)
    attn_full = (early, None, 0, (0, 4 * flat))

    attended = [
        launch(
            attend_kernel, "attend", (live[i],),
            ((statest, 1, 0, i * rows // BLOCK), attn_full, (vec_own, None, 0)),
            ((*head_t, 2), (*head_t, 2), (*pair_rows, 1), (*pair_rows, 1), (*pair_rows, 1),
             ((heads, size, rows), F32, 2), ((heads, 8, rows), F32, 2), (*act, 1)),
            scratch=(((heads, size + 16, rows), BF16), ((-(-2 * heads // 8) * 8, BLOCK), F32)),
            flops=6 * 10**9,
        )
        for i in each
    ]
    in_full, out_full = (late_feed, None, 0, (0, hidden)), (late_feed, None, 0, (hidden, hidden))
    late_rel = gather_direct(after(attn_b.reshape(shard, 3 * flat).astype(BF16), *attended[0]))
    rel_full = (late_rel, None, 0)
    mixed_other = [exchange(attended[i][7]) for i in each]
    fed = [
        launch(
            feed_kernel, "feed", (live[i],),
            ((statest, 1, 0, i * rows // BLOCK), (attended[i][7], 1, 0), (mixed_other[i], 1, HELD), in_full,
             out_full, (vec_full, None, 0)),
            ((*wide, 1), ((hidden, rows), BF16, 1), ((hidden, rows), BF16, 1), (*act, 1)),
            flops=3 * 10**9,
        )
        for i in each
    ]
    fed_other = [exchange(fed[i][3]) for i in each]

    def relate(i, earlier):
        last = i + 1 == sequences
        return launch(
            functools.partial(relation_kernel, bool(earlier)), "relation", (live[i], weights[i]),
            ((fed[i][0], 1, 0), (fed[i][3], 1, 0), (fed_other[i], 1, HELD), rel_full,
             (vec_full, None, 0), (teacher[i][0], 2, 1), (teacher[i][1], 1, 1), (teacher[i][2], 2, 1),
             (teacher[i][3], 1, 1), (teacher[i][4], None, 0), *((value, None, HELD) for value in earlier)),
            (((features, 3 * flat), BF16 if last else F32, HELD), (*act, 1)),
            scratch=(
                ((features, 3 * flat), F32), act, head_t, head_t, head_t, pair_rows, pair_rows, pair_rows,
                head_t, ((heads, size, rows), F32),
                ((pairs, rows, 2 * size), F32), ((pairs, rows, 2 * size), F32), ((bound_rows, BLOCK), F32),
            ),
            flops=30 * 10**9,
        )

    def feed_back(i, earlier):
        last = i + 1 == sequences
        sums = ((features, 8), F32)
        return launch(
            functools.partial(feed_back_kernel, bool(earlier)), "feed_back", (live[i],),
            ((fed[i][0], 1, 0), (fed[i][3], 1, 0), (fed_other[i], 1, 0), (related[i][1], 1, 0),
             (down_other[i], None, HELD), (fed[i][1], 1, 0), (fed[i][2], 1, 0), in_full,
             out_full, (vec_full, None, 0), *((value, None, HELD) for value in earlier)),
            (((features, 2 * hidden), BF16 if last else F32, HELD), (*sums, HELD), (*wide, 1), (*act, HELD)),
            scratch=(((features, 2 * hidden), F32), sums),
            flops=4 * 10**9,
        )

    def attend_back(i, earlier):
        last = i + 1 == sequences
        running = (((features, 4 * flat), F32), ((features, 8), F32), ((flat, 8), F32))
        return launch(
            functools.partial(attend_back_kernel, bool(earlier), last), "attend_back",
            (live[i], core.reshape(1).astype(jnp.int32)),
            ((statest, 1, 0, i * rows // BLOCK), (attended[i][7], 1, 0), (mixed_other[i], 1, 0), (fed_back[i][2], 1, 0),
             (fed_back[i][3], 1, HELD), (up_other[i], None, HELD), attn_full, (vec_full, None, 0),
             (attended[i][0], 2, 1), (attended[i][1], 2, 1), (attended[i][2], 1, 1), (attended[i][3], 1, 1),
             (attended[i][4], 1, 1), (attended[i][5], 2, 0), (attended[i][6], 2, 1),
             *([(fed_back[i][1], None, HELD)] if last else []), *((value, None, HELD) for value in earlier)),
            (((features, 4 * flat + 8), BF16, HELD),) if last else tuple((*spec, HELD) for spec in running),
            scratch=running + (
                head_t, pair_rows, ((heads, 8, rows), F32), head_t,
                ((pairs, rows, 2 * size), F32), ((pairs, rows, 2 * size), F32),
            ),
            flops=15 * 10**9,
        )

    related, down_other = [], []
    for i in each:
        related.append(relate(i, related[-1][:1] if related else ()))
        down_other.append(exchange(related[i][1]))
    sent_rel = send_owner(related[-1][0])
    fed_back, up_other = [], []
    for i in each:
        fed_back.append(feed_back(i, fed_back[-1][:2] if fed_back else ()))
        up_other.append(exchange(fed_back[i][3]))
    sent_feed = send_owner(fed_back[-1][0])
    attended_back = []
    for i in each:
        attended_back.append(attend_back(i, attended_back[-1] if attended_back else ()))
    sent_attn = send_owner(after(attended_back[-1][0], sent_rel, sent_feed))
    shard_rel, shard_feed = add_parts(sent_rel), add_parts(sent_feed)
    shard_in, shard_out = shard_feed[:, :hidden], shard_feed[:, hidden:]
    own, message = collect(sent_attn, jnp.sum(shard_feed * shard_feed) + jnp.sum(shard_rel * shard_rel), 6, 1.0 / cores)
    grad_norm = jnp.sqrt(jnp.sum(lax.all_to_all(message, ("dp", "ffn"), 0, 0, tiled=True)[:, 0]))
    other = swap(own, "ffn", 0)
    grad_rel = shard_rel.reshape(attn_b.shape)
    upper = core == 1
    low, high = jnp.where(upper, other, own), jnp.where(upper, own, other)
    columns = [
        half[:, start : start + flat] for start in range(0, 4 * flat, flat) for half in (low, high)
    ]
    grad_attn = jnp.concatenate(columns, axis=1)
    grad_vec = jnp.concatenate([(low + high)[:, 4 * flat : 4 * flat + 2], own[:, 4 * flat + 2 :]], axis=1)
    gradients = (grad_attn, shard_in, shard_out, grad_rel, grad_vec)
    clipped = jnp.minimum(1.0, CLIP_NORM / grad_norm)
    masters = (attn_a, ffn_in, ffn_out, attn_b, vec_d)
    firsts = (mom1_attn_a, mom1_ffn_in, mom1_ffn_out, mom1_attn_b, mom1_vec_d)
    seconds = (mom2_attn_a, mom2_ffn_in, mom2_ffn_out, mom2_attn_b, mom2_vec_d)
    rates = (RATE_MATRIX, RATE_MATRIX, RATE_MATRIX, RATE_MATRIX, RATE_VECTOR)
    decays = (DECAY_RATE, DECAY_RATE, DECAY_RATE, DECAY_RATE, 0.0)
    news = [
        adam_update(masters[i], gradients[i], firsts[i], seconds[i], clipped, rates[i], decays[i])
        for i in range(5)
    ]
    return (grad_norm, *(new[0] for new in news), *(new[1] for new in news), *(new[2] for new in news))


def solution(mesh):
    matrix = P("dp", None)
    halved = P("dp", "ffn")
    cube = P("dp", None, "ffn")
    trained = (matrix, halved, halved, cube, matrix)
    in_specs = (matrix, matrix, P("dp"), P("dp"), P(), P(None, None, "ffn")) + trained * 3
    out_specs = (P(),) + trained * 3
    return jax.shard_map(per_device, mesh=mesh, in_specs=in_specs, out_specs=out_specs, check_vma=False)
```

```python
import functools

import jax
import jax.numpy as jnp
from jax import lax
from jax.experimental import pallas as pl
from jax.experimental.pallas import tpu as pltpu
from jax.sharding import PartitionSpec as P

HEADS = 12
STEP = 10

NORM_EPSILON = 1e-12
CLIP_NORM = 1.0
BETA_ONE = 0.9
BETA_TWO = 0.999
ADAM_EPSILON = 1e-08
RATE_MATRIX = 0.04
RATE_VECTOR = 0.2
DECAY_RATE = 0.01
MASK_VALUE = -1e30
LOG2_E = 1.4426950408889634
BLOCK = 256
SAFE_EXPONENT = 100.0
HELD = -1
VMEM_BYTES = 24 * 2**20
F32 = jnp.float32
BF16 = jnp.bfloat16


def nn(left, right):
    return lax.dot_general(left, right, (((1,), (0,)), ((), ())), preferred_element_type=F32)


def nt(left, right):
    return lax.dot_general(left, right, (((1,), (1,)), ((), ())), preferred_element_type=F32)


def tn(left, right):
    return lax.dot_general(left, right, (((0,), (0,)), ((), ())), preferred_element_type=F32)


def lanes(block):
    return pl.ds(pl.multiple_of(block * BLOCK, BLOCK), BLOCK)


def live_blocks(len_ref):
    return (len_ref[0] + BLOCK - 1) // BLOCK


def for_size(blocks, most, safe, fast, slow):
    for n in range(1, most + 1):
        pl.when(jnp.logical_and(safe, blocks == n))(functools.partial(fast, n))
    pl.when(jnp.logical_not(safe))(slow)


def pipeline(count, first, second, third):
    firsts, seconds = {}, {}
    for t in range(count + 2):
        if t < count:
            firsts[t] = first(t)
        if 0 <= t - 1 < count:
            seconds[t - 1] = second(t - 1, firsts.pop(t - 1))
        if 0 <= t - 2 < count:
            third(t - 2, seconds.pop(t - 2))


def staged(blocks, first, second):
    def step(block, held):
        ahead = first(block)
        second(block - 1, held)
        return ahead

    second(blocks - 1, lax.fori_loop(1, blocks, step, first(jnp.int32(0))))


def squared_lengths(flat, size):
    features = flat.shape[0]
    groups = -(-features // size // 8) * 8
    row = lax.broadcasted_iota(jnp.int32, (groups, features), 0)
    column = lax.broadcasted_iota(jnp.int32, (groups, features), 1)
    ones = jnp.where((column >= row * size) & (column < (row + 1) * size), 1.0, 0.0).astype(BF16)
    return nn(ones, flat * flat)


def clear_dead(blocks, rows, *refs):
    def step(block, carry):
        for ref in refs:
            ref[:, :, lanes(block)] = jnp.zeros(ref.shape[:2] + (BLOCK,), ref.dtype)
        return carry

    lax.fori_loop(blocks, rows // BLOCK, step, 0)


def norm_forward(resid):
    features = resid.shape[0]
    centred = resid - jnp.sum(resid, axis=0, keepdims=True) * (1.0 / features)
    variance = jnp.sum(centred * centred, axis=0, keepdims=True) * (1.0 / features)
    inverse = lax.rsqrt(variance + NORM_EPSILON)
    return centred * inverse, inverse


def norm_backward(scaled, normed, inverse):
    features = scaled.shape[0]
    mean = jnp.sum(scaled, axis=0, keepdims=True) * (1.0 / features)
    slope = jnp.sum(scaled * normed, axis=0, keepdims=True) * (1.0 / features)
    return inverse * (scaled - mean - normed * slope)


def mask_tail(scores, n, length, start=None):
    start = (n - 1) * BLOCK if start is None else start
    rows = start + lax.broadcasted_iota(jnp.int32, (n * BLOCK - start, scores.shape[1]), 0)
    tail = jnp.where(rows < length, scores[start:], MASK_VALUE)
    if start == 0:
        return tail
    return jnp.concatenate([scores[:start], tail], axis=0)


def pad_rows(part, index, count):
    zeros = jnp.zeros_like(part)
    return jnp.concatenate([part if i == index else zeros for i in range(count)], axis=0)


def pad_lanes(pair, index, size):
    lane = lax.broadcasted_iota(jnp.int32, pair.shape, 1)
    return jnp.where((lane >= index * size) & (lane < (index + 1) * size), pair, jnp.zeros_like(pair))


def split_heads(flat, ref, columns, size):
    heads = flat.shape[0] // size
    for head in range(heads):
        ref[head, :, columns] = flat[head * size : (head + 1) * size]


def split_pairs(flat, ref, rows):
    pairs, width = ref.shape[0], ref.shape[2]
    for pair in range(pairs):
        ref[pair, rows, :] = flat[pair * width : (pair + 1) * width].T


def teacher_kernel(traffic, len_ref, rows_ref, weight_ref, qt_ref, k_ref, vt_ref, v_ref, bound_ref):
    size = qt_ref.shape[1]
    scaling = LOG2_E * size ** (-0.5)
    bound_ref[...] = jnp.zeros(bound_ref.shape, F32)

    def step(block, carry):
        where = lanes(block)
        traffic.take(block)
        rows = rows_ref[where, :]
        queries, keys, values = [nn(rows, weight_ref[index]) for index in range(3)]
        scaled = [(part * scaling).astype(BF16).T for part in (queries, values)]
        queries, keys, values = queries.astype(BF16), keys.astype(BF16), values.astype(BF16)
        columns = [scaled[0], keys.T, scaled[1]]
        bound_ref[...] = jnp.maximum(bound_ref[...], squared_lengths(jnp.concatenate(columns, axis=0), size))
        split_heads(columns[0], qt_ref, where, size)
        split_heads(columns[2], vt_ref, where, size)
        for pair in range(k_ref.shape[0]):
            k_ref[pair, where, :] = keys[:, 2 * size * pair : 2 * size * (pair + 1)]
            v_ref[pair, where, :] = values[:, 2 * size * pair : 2 * size * (pair + 1)]
        traffic.give(block, 0, 1, 2, 3)
        return carry

    lax.fori_loop(0, live_blocks(len_ref), step, 0)


def attend_kernel(
    traffic, len_ref, xt_ref, weight_ref, vec_ref, qt_ref, kt_ref, q_ref, k_ref, v_ref, ot_ref, lse_ref, at_ref,
    vone_ref, bound_ref,
):
    heads, size, rows = qt_ref.shape
    flat = heads * size
    scaling = LOG2_E * size ** (-0.5)
    blocks = live_blocks(len_ref)
    length = len_ref[0]
    bound_ref[...] = jnp.zeros(bound_ref.shape, F32)

    def project(block, carry):
        where = lanes(block)
        traffic.take(block)
        xt = xt_ref[:, where]
        projected = tn(weight_ref[:, : 3 * flat], xt)
        query = projected[:flat] + vec_ref[:, 0:1]
        scaled = (query * scaling).astype(BF16)
        query = query.astype(BF16)
        keys = projected[flat : 2 * flat].astype(BF16)
        values = (projected[2 * flat :] + vec_ref[:, 1:2]).astype(BF16)
        split_heads(scaled, qt_ref, where, size)
        split_heads(keys, kt_ref, where, size)
        bound_ref[...] = jnp.maximum(
            bound_ref[...], squared_lengths(jnp.concatenate([query, keys], axis=0), size)
        )
        column = block * BLOCK + lax.broadcasted_iota(jnp.int32, (1, BLOCK), 1)
        live = jnp.where(column < length, 1.0, 0.0)
        live_values = (values.astype(F32) * live).astype(BF16)
        for head in range(heads):
            vone_ref[head, :size, where] = live_values[head * size : (head + 1) * size]
            vone_ref[head, size:, where] = jnp.broadcast_to(live, (16, BLOCK)).astype(BF16)
        split_pairs(query, q_ref, where)
        split_pairs(keys, k_ref, where)
        split_pairs(values, v_ref, where)
        traffic.give(block, 0, 1, 2, 3, 4)
        return carry

    lax.fori_loop(0, blocks, project, 0)

    longest = jnp.max(bound_ref[...], axis=1, keepdims=True)
    safe = jnp.max(longest[:heads] * longest[heads : 2 * heads]) * scaling**2 <= SAFE_EXPONENT**2

    def scores(pair, half, where, n):
        return nn(k_ref[pair, : n * BLOCK, :], pad_rows(qt_ref[2 * pair + half, :, where], half, 2))

    def mix(head, where, n, grown, top):
        mixed = nn(vone_ref[head, :, : n * BLOCK], grown)
        total = mixed[size : size + 1]
        ot_ref[head, :, where] = mixed[:size] * (1.0 / total)
        lse_ref[head, :, where] = jnp.broadcast_to(top + jnp.log2(total), (8, BLOCK))

    def fast(n):
        def step(block, carry):
            where = lanes(block)
            pipeline(
                heads,
                lambda head: scores(head // 2, head % 2, where, n),
                lambda head, score: jnp.exp2(score).astype(BF16),
                lambda head, grown: mix(head, where, n, grown, 0.0),
            )
            traffic.give(block, 5, 6)
            return carry

        lax.fori_loop(0, n, step, 0)

    def slow():
        most = rows // BLOCK
        clear_dead(blocks, rows, vone_ref)

        def step(index, carry):
            block, pair = index // (heads // 2), index % (heads // 2)
            where = lanes(block)
            for half in range(2):
                score = mask_tail(scores(pair, half, where, most), most, length, 0)
                top = jnp.max(score, axis=0, keepdims=True)
                mix(2 * pair + half, where, most, jnp.exp2(score - top).astype(BF16), top)
            pl.when(pair == heads // 2 - 1)(lambda: traffic.give(block, 5, 6))
            return carry

        lax.fori_loop(0, blocks * (heads // 2), step, 0)

    for_size(blocks, rows // BLOCK, safe, fast, slow)

    def output(block, carry):
        where = lanes(block)
        mixed = ot_ref[:, :, where].reshape(flat, BLOCK).astype(BF16)
        at_ref[:, where] = nn(weight_ref[:, 3 * flat :], mixed).astype(BF16)
        traffic.give(block, 7)
        return carry

    lax.fori_loop(0, blocks, output, 0)


def first_norm(xt, own, other, vec_ref):
    resid = xt.astype(F32) + (own.astype(F32) + other.astype(F32)) + vec_ref[:, 2:3]
    return norm_forward(resid)


def feed_kernel(traffic, len_ref, xt_ref, own_ref, other_ref, in_ref, out_ref, vec_ref, ht_ref, zt_ref, slope_ref, ft_ref):
    def first(block):
        where = lanes(block)
        traffic.take(block)
        normed, _ = first_norm(xt_ref[:, where], own_ref[:, where], other_ref[:, where], vec_ref)
        hidden = normed * vec_ref[:, 3:4] + vec_ref[:, 4:5]
        ht_ref[:, where] = hidden
        return tn(in_ref[...], hidden.astype(BF16))

    def second(block, pre):
        where = lanes(block)
        cdf = 0.5 + 0.5 * lax.erf(pre * (0.5**0.5))
        pdf = jnp.exp2(pre * pre * (-0.5 * LOG2_E)) * 0.3989422804014327
        active = (pre * cdf).astype(BF16)
        zt_ref[:, where] = active
        slope_ref[:, where] = (cdf + pre * pdf).astype(BF16)
        ft_ref[:, where] = nn(out_ref[...], active).astype(BF16)
        traffic.give(block, 0, 1, 2, 3)

    staged(live_blocks(len_ref), first, second)


def second_norm(ht, own, other, vec_ref):
    resid = ht + (own.astype(F32) + other.astype(F32)) + vec_ref[:, 5:6]
    return norm_forward(resid)


def relation_kernel(
    chained, traffic, len_ref, weight_ref, ht_ref, own_ref, other_ref, rel_ref, vec_ref, tqt_ref, tk_ref, tvt_ref, tv_ref,
    tbound_ref, *refs,
):
    earlier_ref, refs = (refs[0], refs[1:]) if chained else (None, refs)
    grad_out_ref, dt_ref, refs = refs[0], refs[1], refs[2:]
    grad_ref, refs = refs[0], refs[1:]
    relation_body(
        traffic, len_ref, weight_ref, ht_ref, own_ref, other_ref, rel_ref, vec_ref, tqt_ref, tk_ref, tvt_ref, tv_ref,
        tbound_ref, grad_ref, dt_ref, *refs,
    )
    traffic.take_last()
    grad = grad_ref[...] + earlier_ref[...] if chained else grad_ref[...]
    grad_out_ref[...] = grad.astype(grad_out_ref.dtype)


def relation_body(
    traffic, len_ref, weight_ref, ht_ref, own_ref, other_ref, rel_ref, vec_ref, tqt_ref, tk_ref, tvt_ref, tv_ref,
    tbound_ref, grad_ref, dt_ref,
    h2_ref, qt_ref, kt_ref, vt_ref, st_ref, q_ref, k_ref, v_ref, dqt_ref, dvt_ref, dk_ref, dv_ref, bound_ref,
):
    heads, size, rows = qt_ref.shape
    teacher_size = tqt_ref.shape[1]
    flat = heads * size
    plain = size ** (-0.5)
    scaling = LOG2_E * plain
    teacher_scaling = LOG2_E * teacher_size ** (-0.5)
    blocks = live_blocks(len_ref)
    length = len_ref[0]
    weight = weight_ref[0]
    bound_ref[...] = jnp.zeros(bound_ref.shape, F32)

    def project(block, carry):
        where = lanes(block)
        traffic.take(block)
        normed, _ = second_norm(ht_ref[:, where], own_ref[:, where], other_ref[:, where], vec_ref)
        hidden = (normed * vec_ref[:, 6:7] + vec_ref[:, 7:8]).astype(BF16)
        h2_ref[:, where] = hidden
        projected = tn(rel_ref[...], hidden)
        split_heads((projected[:flat] * scaling).astype(BF16), qt_ref, where, size)
        split_heads((projected[2 * flat :] * scaling).astype(BF16), st_ref, where, size)
        projected = projected.astype(BF16)
        bound_ref[...] = jnp.maximum(bound_ref[...], squared_lengths(projected, size))
        split_heads(projected[flat : 2 * flat], kt_ref, where, size)
        split_heads(projected[2 * flat :], vt_ref, where, size)
        split_pairs(projected[:flat], q_ref, where)
        split_pairs(projected[flat : 2 * flat], k_ref, where)
        split_pairs(projected[2 * flat :], v_ref, where)
        for pair in range(heads // 2):
            dk_ref[pair, where, :] = jnp.zeros((BLOCK, 2 * size), F32)
            dv_ref[pair, where, :] = jnp.zeros((BLOCK, 2 * size), F32)
        return carry

    lax.fori_loop(0, blocks, project, 0)

    traffic.take_rest()

    def exponents(ref, attention_scale, relation_scale):
        longest = jnp.max(ref[...], axis=1, keepdims=True)
        attention = jnp.max(longest[:heads] * longest[heads : 2 * heads]) * attention_scale**2
        relation = jnp.max(longest[2 * heads : 3 * heads]) * relation_scale
        return jnp.logical_and(attention <= SAFE_EXPONENT**2, relation <= SAFE_EXPONENT)

    safe = jnp.logical_and(
        exponents(bound_ref, scaling, scaling), exponents(tbound_ref, 1.0, 1.0 / teacher_scaling)
    )
    pairs = heads // 2
    attention = (k_ref, qt_ref, q_ref, tk_ref, tqt_ref, kt_ref, dqt_ref, dk_ref)
    relation = (v_ref, st_ref, v_ref, tv_ref, tvt_ref, vt_ref, dvt_ref, dv_ref)
    tasks = [(half, refs) for refs in (attention, relation) for half in range(2)]

    def steps(n, pair, where, mask, grow):
        column = where.start + lax.broadcasted_iota(jnp.int32, (1, BLOCK), 1)
        live = jnp.where(column < length, weight, 0.0)
        kept = {}

        def first(t):
            half, (left, rightt, _, teacher_left, teacher_rightt, _, _, _) = tasks[t]
            head = 2 * pair + half
            student = nn(left[pair, : n * BLOCK, :], pad_rows(rightt[head, :, where], half, 2))
            teacher = nn(teacher_left[pair, : n * BLOCK, :], pad_rows(teacher_rightt[head, :, where], half, 2))
            return student, teacher

        def second(t, scores):
            student, teacher = grow(mask(scores[0])), grow(mask(scores[1]))
            student_part = live / jnp.sum(student, axis=0, keepdims=True)
            teacher_part = live / jnp.sum(teacher, axis=0, keepdims=True)
            return (student * student_part - teacher * teacher_part).astype(BF16)

        def third(t, grad):
            half, (_, _, right, _, _, leftt, own_ref, running_ref) = tasks[t]
            head = 2 * pair + half
            own_ref[head, :, where] = (nn(leftt[head, :, : n * BLOCK], grad) * plain).astype(own_ref.dtype)
            kept[half] = grad
            if half == 1:
                queries = right[pair, where, :]
                stacked = jnp.concatenate([pad_lanes(queries, i, size) for i in range(2)], axis=0)
                running_ref[pair, : n * BLOCK, :] += nn(jnp.concatenate([kept[0], kept[1]], axis=1), stacked)

        return first, second, third

    def fast(n):
        def step(index, carry):
            stages = steps(
                n, index % pairs, lanes(index // pairs), lambda score: mask_tail(score, n, length), jnp.exp2
            )
            pipeline(len(tasks), *stages)
            return carry

        lax.fori_loop(0, n * pairs, step, 0)

    def slow():
        most = rows // BLOCK
        clear_dead(blocks, rows, kt_ref, vt_ref)

        def grow(score):
            return jnp.exp2(score - jnp.max(score, axis=0, keepdims=True))

        def step(index, carry):
            first, second, third = steps(
                most, index % pairs, lanes(index // pairs), lambda score: mask_tail(score, most, length, 0), grow
            )
            for t in range(len(tasks)):
                third(t, second(t, first(t)))
            return carry

        lax.fori_loop(0, blocks * pairs, step, 0)

    for_size(blocks, rows // BLOCK, safe, fast, slow)
    grad_ref[...] = jnp.zeros(grad_ref.shape, F32)

    def finish(block, carry):
        where = lanes(block)
        queries = dqt_ref[:, :, where].reshape(flat, BLOCK)
        keys = jnp.concatenate([dk_ref[pair, where, :].T for pair in range(heads // 2)], axis=0) * plain
        values = jnp.concatenate([dv_ref[pair, where, :].T for pair in range(heads // 2)], axis=0) * plain
        values = values + dvt_ref[:, :, where].reshape(flat, BLOCK)
        grads = jnp.concatenate([queries, keys.astype(BF16), values.astype(BF16)], axis=0)
        grad_ref[...] += nt(h2_ref[:, where], grads)
        dt_ref[:, where] = nn(rel_ref[...], grads).astype(BF16)
        traffic.give(block, 1)
        return carry

    lax.fori_loop(0, blocks, finish, 0)


def feed_back_kernel(
    chained, traffic, len_ref, ht_ref, own_ref, other_ref, down_own_ref, down_other_ref, zt_ref, slope_ref, in_ref, out_ref, vec_ref, *refs,
):
    earlier, refs = (refs[:2], refs[2:]) if chained else (None, refs)
    total_ref, sums_out_ref, resid_ref, up_ref, refs = *refs[:4], refs[4:]
    grad_ref, sums_ref = refs
    hidden_units = in_ref.shape[1]
    grad_ref[...] = jnp.zeros(grad_ref.shape, F32)
    sums_ref[...] = jnp.zeros(sums_ref.shape, F32)

    def first(block):
        where = lanes(block)
        traffic.take(block)
        normed, inverse = second_norm(ht_ref[:, where], own_ref[:, where], other_ref[:, where], vec_ref)
        grad = down_own_ref[:, where].astype(F32) + down_other_ref[:, where].astype(F32)
        resid = norm_backward(grad * vec_ref[:, 6:7], normed, inverse)
        resid_ref[:, where] = resid
        sums_ref[:, 0:1] += jnp.sum(resid, axis=1, keepdims=True)
        sums_ref[:, 1:2] += jnp.sum(grad * normed, axis=1, keepdims=True)
        sums_ref[:, 2:3] += jnp.sum(grad, axis=1, keepdims=True)
        return resid.astype(BF16)

    def second(block, branch):
        where = lanes(block)
        grad_ref[:, hidden_units:] += nt(branch, zt_ref[:, where])
        pre_grad = (tn(out_ref[...], branch) * slope_ref[:, where].astype(F32)).astype(BF16)
        grad_ref[:, :hidden_units] += nt(ht_ref[:, where].astype(BF16), pre_grad)
        up_ref[:, where] = nn(in_ref[...], pre_grad).astype(BF16)
        traffic.give(block, 2, 3)

    staged(live_blocks(len_ref), first, second)
    traffic.take_last()
    grad, sums = grad_ref[...], sums_ref[...]
    if chained:
        grad, sums = grad + earlier[0][...], sums + earlier[1][...]
    total_ref[...] = grad.astype(total_ref.dtype)
    sums_out_ref[...] = sums


def attend_back_kernel(
    chained, last, traffic, len_ref, core_ref, xt_ref, own_ref, other_ref, resid_ref, up_own_ref, up_other_ref, weight_ref, vec_ref,
    qt_ref, kt_ref, q_ref, k_ref, v_ref, ot_ref, lse_ref, *refs,
):
    back_sums_ref, refs = (refs[0], refs[1:]) if last else (None, refs)
    earlier, refs = (refs[:3], refs[3:]) if chained else (None, refs)
    outs, refs = (refs[:1], refs[1:]) if last else (refs[:3], refs[3:])
    running, refs = refs[:3], refs[3:]
    grad_ref, sums_ref, head_sums_ref = running
    for ref in running:
        ref[...] = jnp.zeros(ref.shape, F32)
    attend_back_body(
        traffic, len_ref, xt_ref, own_ref, other_ref, resid_ref, up_own_ref, up_other_ref, weight_ref, vec_ref,
        qt_ref, kt_ref, q_ref, k_ref, v_ref, ot_ref, lse_ref, grad_ref, sums_ref, head_sums_ref, *refs,
    )
    traffic.take_last()
    if chained:
        for ref, value in zip(running, earlier):
            ref[...] += value[...]
    if not last:
        for ref, value in zip(outs, running):
            ref[...] = value[...]
        return
    total_ref = outs[0]
    columns, flat = grad_ref.shape[1], head_sums_ref.shape[0]
    total_ref[:, :columns] = grad_ref[...].astype(BF16)
    biases = head_sums_ref[:, 0:2].astype(BF16)
    total_ref[:, columns : columns + 2] = jnp.zeros((total_ref.shape[0], 2), BF16)
    for core in range(total_ref.shape[0] // flat):

        @pl.when(core_ref[0] == core)
        def _(core=core):
            total_ref[core * flat : (core + 1) * flat, columns : columns + 2] = biases

    total_ref[:, columns + 2 : columns + 5] = sums_ref[:, 0:3].astype(BF16)
    total_ref[:, columns + 5 : columns + 8] = back_sums_ref[:, 0:3].astype(BF16)


def attend_back_body(
    traffic, len_ref, xt_ref, own_ref, other_ref, resid_ref, up_own_ref, up_other_ref, weight_ref, vec_ref,
    qt_ref, kt_ref, q_ref, k_ref, v_ref, ot_ref, lse_ref, grad_ref, sums_ref, head_sums_ref,
    dot_ref, do_ref, inner_ref, dqt_ref, dk_ref, dv_ref,
):
    heads, size, rows = qt_ref.shape
    flat = heads * size
    plain = size ** (-0.5)
    scaling = LOG2_E * plain
    blocks = live_blocks(len_ref)
    length = len_ref[0]

    def start(block, carry):
        where = lanes(block)
        traffic.take(block)
        normed, inverse = first_norm(xt_ref[:, where], own_ref[:, where], other_ref[:, where], vec_ref)
        grad = resid_ref[:, where] + (up_own_ref[:, where].astype(F32) + up_other_ref[:, where].astype(F32))
        branch = norm_backward(grad * vec_ref[:, 3:4], normed, inverse).astype(BF16)
        sums_ref[:, 0:1] += jnp.sum(branch.astype(F32), axis=1, keepdims=True)
        sums_ref[:, 1:2] += jnp.sum(grad * normed, axis=1, keepdims=True)
        sums_ref[:, 2:3] += jnp.sum(grad, axis=1, keepdims=True)
        mixed = ot_ref[:, :, where]
        grad_ref[:, 3 * flat :] += nt(branch, mixed.reshape(flat, BLOCK).astype(BF16))
        mixed_grad = tn(weight_ref[:, 3 * flat :], branch).astype(BF16)
        split_heads(mixed_grad, dot_ref, where, size)
        split_pairs(mixed_grad, do_ref, where)
        for head in range(heads):
            product = mixed_grad[head * size : (head + 1) * size].astype(F32) * mixed[head]
            inner_ref[head, :, where] = jnp.broadcast_to(jnp.sum(product, axis=0, keepdims=True), (8, BLOCK))
        for pair in range(heads // 2):
            dk_ref[pair, where, :] = jnp.zeros((BLOCK, 2 * size), F32)
            dv_ref[pair, where, :] = jnp.zeros((BLOCK, 2 * size), F32)
        return carry

    lax.fori_loop(0, blocks, start, 0)
    traffic.take_rest()

    def attend(n):
        def step(block, carry):
            where = lanes(block)
            kept = {}

            def first(head):
                pair, half = head // 2, head % 2
                scores = nn(k_ref[pair, : n * BLOCK, :], pad_rows(qt_ref[head, :, where], half, 2))
                prob_grad = nn(v_ref[pair, : n * BLOCK, :], pad_rows(dot_ref[head, :, where], half, 2))
                return scores, prob_grad

            def second(head, parts):
                scores, prob_grad = parts
                prob = jnp.exp2(mask_tail(scores, n, length) - lse_ref[head, 0:1, where])
                grad = (prob * (prob_grad - inner_ref[head, 0:1, where])).astype(BF16)
                return prob.astype(BF16), grad

            def third(head, parts):
                pair = head // 2
                dqt_ref[head, :, where] = (nn(kt_ref[head, :, : n * BLOCK], parts[1]) * plain).astype(BF16)
                kept[head % 2] = parts
                if head % 2 == 1:
                    for index, right, running in ((1, q_ref, dk_ref), (0, do_ref, dv_ref)):
                        queries = right[pair, where, :]
                        stacked = jnp.concatenate([pad_lanes(queries, half, size) for half in range(2)], axis=0)
                        running[pair, : n * BLOCK, :] += nn(
                            jnp.concatenate([kept[0][index], kept[1][index]], axis=1), stacked
                        )

            pipeline(heads, first, second, third)
            return carry

        lax.fori_loop(0, n, step, 0)

    for n in range(1, rows // BLOCK + 1):
        pl.when(blocks == n)(functools.partial(attend, n))

    def finish(block, carry):
        where = lanes(block)
        queries = dqt_ref[:, :, where].reshape(flat, BLOCK)
        keys = jnp.concatenate([dk_ref[pair, where, :].T for pair in range(heads // 2)], axis=0) * plain
        values = jnp.concatenate([dv_ref[pair, where, :].T for pair in range(heads // 2)], axis=0).astype(BF16)
        head_sums_ref[:, 0:1] += jnp.sum(queries.astype(F32), axis=1, keepdims=True)
        head_sums_ref[:, 1:2] += jnp.sum(values.astype(F32), axis=1, keepdims=True)
        grads = jnp.concatenate([queries, keys.astype(BF16), values], axis=0)
        grad_ref[:, : 3 * flat] += nt(xt_ref[:, where], grads)
        return carry

    lax.fori_loop(0, blocks, finish, 0)


class Traffic:
    def __init__(self, blocks, ins, outs, in_sems, out_sems):
        self.blocks, self.ins, self.outs, self.in_sems, self.out_sems = blocks, ins, outs, in_sems, out_sems

    def part(self, ref, axis, block):
        return ref if axis is None else ref.at[(slice(None),) * axis + (lanes(block),)]

    def inward(self, index, block):
        source, target, axis, _, first = self.ins[index]
        if axis is None:
            if first:
                source = source.at[:, first[0] : first[0] + first[1]]
            return pltpu.make_async_copy(source, target, self.in_sems.at[index, 0])
        return pltpu.make_async_copy(
            self.part(source, axis, first + block), self.part(target, axis, block), self.in_sems.at[index, block]
        )

    def outward(self, index, block):
        target, source, axis = self.outs[index]
        return pltpu.make_async_copy(
            self.part(source, axis, block), self.part(target, axis, block), self.out_sems.at[index, block]
        )

    def chosen(self, group, whole=False):
        return [i for i, entry in enumerate(self.ins) if (entry[2] is None) == whole and entry[3] == group]

    def start(self):
        for index in self.chosen(0, whole=True):
            self.inward(index, 0).start()
        for group in (0, 1):
            indices = self.chosen(group)

            def step(block, carry):
                for index in indices:
                    self.inward(index, block).start()
                return carry

            if indices:
                lax.fori_loop(0, self.blocks, step, 0)
        for index in self.chosen(1, whole=True):
            self.inward(index, 0).start()
        for index in self.chosen(0, whole=True):
            self.inward(index, 0).wait()

    def take(self, block):
        for index in self.chosen(0):
            self.inward(index, block).wait()

    def take_rest(self):
        def step(block, carry):
            for index in self.chosen(1):
                self.inward(index, block).wait()
            return carry

        lax.fori_loop(0, self.blocks, step, 0)

    def take_last(self):
        for index in self.chosen(1, whole=True):
            self.inward(index, 0).wait()

    def give(self, block, *indices):
        for index in indices:
            if self.outs[index][2] != HELD:
                self.outward(index, block).start()

    def finish(self):
        whole = [i for i, entry in enumerate(self.outs) if entry[2] is None]
        parts = [i for i, entry in enumerate(self.outs) if entry[2] not in (None, HELD)]
        for index in whole:
            self.outward(index, 0).start()

        def step(block, carry):
            for index in parts:
                self.outward(index, block).wait()
            return carry

        if parts:
            lax.fori_loop(0, self.blocks, step, 0)
        for index in whole:
            self.outward(index, 0).wait()


def call(blocks, kernel, name, scalars, arrays, outs, scratch=(), flops=0):
    smem = pl.BlockSpec(memory_space=pltpu.SMEM)
    hbm = pl.BlockSpec(memory_space=pltpu.HBM)
    vmem = pl.BlockSpec(memory_space=pltpu.VMEM)
    arrays = [entry if len(entry) == 4 else (*entry, 0) for entry in arrays]

    def held(array, axis, group, first):
        shape = list(array.shape)
        if axis is not None:
            shape[axis] = blocks * BLOCK
        elif first:
            shape[1] = first[1]
        return pltpu.VMEM(tuple(shape), array.dtype)

    count, ins, results = len(scalars), len(arrays), len(outs)
    copied = [i for i in range(ins) if arrays[i][2] != HELD]
    filled = [i for i in range(results) if outs[i][2] != HELD]

    def view(ref, axis, group, first):
        if group != HELD or not first:
            return ref
        if axis is None:
            return ref.at[:, first[0] : first[0] + first[1]]
        return ref.at[(slice(None),) * axis + (slice(first * BLOCK, (first + blocks) * BLOCK),)]

    def body(*refs):
        scalar_refs, refs = refs[:count], refs[count:]
        in_refs, refs = refs[:ins], refs[ins:]
        out_refs, refs = refs[:results], refs[results:]
        in_copies = [view(ref, *entry[1:]) for ref, entry in zip(in_refs, arrays)]
        for index, ref in zip(copied, refs):
            in_copies[index] = ref
        refs = refs[len(copied) :]
        out_copies = list(out_refs)
        for index, ref in zip(filled, refs):
            out_copies[index] = ref
        refs = refs[len(filled) :]
        in_sems, out_sems, refs = refs[0], refs[1], refs[2:]
        traffic = Traffic(
            live_blocks(scalar_refs[0]),
            [(in_refs[i], in_copies[i], *arrays[i][1:]) for i in copied],
            [(ref, copy, axis) for ref, copy, (_, _, axis) in zip(out_refs, out_copies, outs)],
            in_sems,
            out_sems,
        )
        traffic.start()
        kernel(traffic, *scalar_refs, *in_copies, *out_copies, *refs)
        traffic.finish()

    return pl.pallas_call(
        body,
        name=name,
        out_shape=tuple(
            (pltpu.VMEM if axis == HELD else pltpu.HBM)(shape, dtype) for shape, dtype, axis in outs
        ),
        in_specs=[smem] * count
        + [vmem if group == HELD else hbm for _, _, group, _ in arrays],
        out_specs=tuple(vmem if axis == HELD else hbm for _, _, axis in outs),
        scratch_shapes=[held(*arrays[i]) for i in copied]
        + [pltpu.VMEM(*outs[i][:2]) for i in filled]
        + [pltpu.SemaphoreType.DMA((ins, blocks)), pltpu.SemaphoreType.DMA((results, blocks))]
        + [pltpu.VMEM(shape, dtype) for shape, dtype in scratch],
        compiler_params=pltpu.CompilerParams(vmem_limit_bytes=VMEM_BYTES),
        cost_estimate=pl.CostEstimate(flops=flops, bytes_accessed=4 << 20, transcendentals=0),
    )(
        *scalars,
        *(
            pltpu.with_memory_space_constraint(array, pltpu.VMEM if group == HELD else pltpu.HBM)
            for array, _, group, _ in arrays
        ),
    )


def exchange(part):
    return swap(part, "ffn", 0)


def swap(value, axis, bit):
    count = lax.axis_size(axis)
    return lax.ppermute(value, axis, [(i, i ^ (1 << bit)) for i in range(count)])


def bit_of(axis, bit):
    return (lax.axis_index(axis) >> bit) & 1


def dp_bits():
    return lax.axis_size("dp").bit_length() - 1


def after(value, *others):
    return lax.optimization_barrier((value, *others))[0]


def gather_step(whole, other, bit):
    dim = dp_bits() - 1 - bit
    upper = bit_of("dp", bit) == 1
    return jnp.where(upper, jnp.concatenate([other, whole], axis=dim), jnp.concatenate([whole, other], axis=dim))


def gather_direct(shard, *tokens):
    count = lax.axis_size("dp")
    spread = after(jnp.broadcast_to(shard[None], (count,) + shard.shape), *tokens)
    return lax.all_to_all(spread, "dp", 0, 0, tiled=True).reshape((-1,) + shard.shape[1:])


def collect_kernel(shared_columns, shared_weight, squares_ref, spread_ref, own_ref, message_ref):
    own = spread_ref[0].astype(F32)
    for source in range(1, spread_ref.shape[0]):
        own = own + spread_ref[source].astype(F32)
    own_ref[...] = own
    column = lax.broadcasted_iota(jnp.int32, own.shape, 1)
    weights = jnp.where(column < own.shape[1] - shared_columns, 1.0, shared_weight)
    squares = jnp.sum(jnp.sum(own * own * weights, axis=0, keepdims=True), axis=1, keepdims=True)
    message_ref[...] = jnp.broadcast_to(squares + squares_ref[0], message_ref.shape)


def collect(spread, squares, shared_columns, shared_weight):
    vmem = pl.BlockSpec(memory_space=pltpu.VMEM)
    count = lax.axis_size("dp") * lax.axis_size("ffn")
    return pl.pallas_call(
        functools.partial(collect_kernel, shared_columns, shared_weight),
        name="collect",
        out_shape=(pltpu.VMEM(spread.shape[1:], F32), pltpu.VMEM((count, 128), F32)),
        in_specs=[pl.BlockSpec(memory_space=pltpu.SMEM), vmem],
        out_specs=(vmem, vmem),
    )(squares.reshape(1), pltpu.with_memory_space_constraint(spread, pltpu.VMEM))


def send_owner(value):
    count = lax.axis_size("dp")
    rows = value.shape[0] // count
    return lax.all_to_all(value.astype(BF16).reshape((count, rows) + value.shape[1:]), "dp", 0, 0, tiled=True)


def add_parts(spread):
    return jnp.sum(spread.astype(F32), axis=0)


def adam_update(weight, gradient, first, second, clipped, rate, decay):
    scaled = gradient * clipped
    first_new = BETA_ONE * first + (1.0 - BETA_ONE) * scaled
    second_new = BETA_TWO * second + (1.0 - BETA_TWO) * scaled * scaled
    ratio = (
        first_new
        / (1.0 - BETA_ONE**STEP)
        / (jnp.sqrt(second_new / (1.0 - BETA_TWO**STEP)) + ADAM_EPSILON)
    )
    return (weight - rate * (ratio + decay * weight), first_new, second_new)


def per_device(
    states, teacher_states, lengths, domain_ids, domain_weight, teacher_qkv,
    attn_a, ffn_in, ffn_out, attn_b, vec_d,
    mom1_attn_a, mom1_ffn_in, mom1_ffn_out, mom1_attn_b, mom1_vec_d,
    mom2_attn_a, mom2_ffn_in, mom2_ffn_out, mom2_attn_b, mom2_vec_d,
):
    cores = lax.axis_size("ffn")
    core = lax.axis_index("ffn")
    replicas = lax.axis_size("dp")
    replica = lax.axis_index("dp")
    sequences = lengths.shape[0]
    rows = states.shape[0] // sequences
    features = states.shape[1]
    heads = HEADS // cores
    flat = features // cores
    size = flat // heads
    pairs = heads // 2
    hidden = ffn_in.shape[1]
    teacher_flat = teacher_qkv.shape[2]
    teacher_size = teacher_flat // heads
    shard = attn_a.shape[0]
    matched = domain_ids[:, None] == jnp.arange(domain_weight.shape[0])[None, :]
    sequence_weight = jnp.sum(jnp.where(matched, domain_weight[None, :], 0.0), axis=1) / HEADS

    teacher_w = teacher_qkv.transpose(1, 0, 2)
    statest = states.T
    live = [lengths[i : i + 1] for i in range(sequences)]
    weights = [sequence_weight[i : i + 1] for i in range(sequences)]
    each = range(sequences)
    launch = functools.partial(call, rows // BLOCK)
    act = ((features, rows), BF16)
    wide = ((features, rows), F32)
    head_t = ((heads, size, rows), BF16)
    pair_rows = ((pairs, rows, 2 * size), BF16)

    bound_rows = -(-3 * heads // 8) * 8

    def project_teacher(i, token):
        return launch(
            teacher_kernel, "teacher", (live[i],),
            ((after(teacher_states, *token), 0, 0, i * rows // BLOCK), (teacher_w, None, 0)),
            (
                ((heads, teacher_size, rows), BF16, 2),
                ((pairs, rows, 2 * teacher_size), BF16, 1),
                ((heads, teacher_size, rows), BF16, 2),
                ((pairs, rows, 2 * teacher_size), BF16, 1),
                ((bound_rows, BLOCK), F32, None),
            ),
            flops=2 * rows * 768 * 1152,
        )

    attn_own = [lax.dynamic_slice_in_dim(attn_a, start + core * flat, flat, 1) for start in range(0, 4 * features, features)]
    early = gather_direct(jnp.concatenate([*attn_own, vec_d], axis=1).astype(BF16))
    teacher = [project_teacher(i, (statest,)) for i in each]
    late_feed = gather_direct(jnp.concatenate([ffn_in, ffn_out], axis=1).astype(BF16), *teacher[0], *teacher[1])
    early = after(early, *teacher[0], *teacher[1])
    vec_full = early[:, 4 * flat :].astype(F32)
    vec_own = lax.dynamic_slice_in_dim(vec_full, core * flat, flat, 0)
    attn_full = (early, None, 0, (0, 4 * flat))

    attended = [
        launch(
            attend_kernel, "attend", (live[i],),
            ((statest, 1, 0, i * rows // BLOCK), attn_full, (vec_own, None, 0)),
            ((*head_t, 2), (*head_t, 2), (*pair_rows, 1), (*pair_rows, 1), (*pair_rows, 1),
             ((heads, size, rows), F32, 2), ((heads, 8, rows), F32, 2), (*act, 1)),
            scratch=(((heads, size + 16, rows), BF16), ((-(-2 * heads // 8) * 8, BLOCK), F32)),
            flops=6 * 10**9,
        )
        for i in each
    ]
    in_full, out_full = (late_feed, None, 0, (0, hidden)), (late_feed, None, 0, (hidden, hidden))
    late_rel = gather_direct(after(attn_b.reshape(shard, 3 * flat).astype(BF16), *attended[0]))
    rel_full = (late_rel, None, 0)
    mixed_other = [exchange(attended[i][7]) for i in each]
    fed = [
        launch(
            feed_kernel, "feed", (live[i],),
            ((statest, 1, 0, i * rows // BLOCK), (attended[i][7], 1, 0), (mixed_other[i], 1, HELD), in_full,
             out_full, (vec_full, None, 0)),
            ((*wide, 1), ((hidden, rows), BF16, 1), ((hidden, rows), BF16, 1), (*act, 1)),
            flops=3 * 10**9,
        )
        for i in each
    ]
    fed_other = [exchange(fed[i][3]) for i in each]

    def relate(i, earlier):
        last = i + 1 == sequences
        return launch(
            functools.partial(relation_kernel, bool(earlier)), "relation", (live[i], weights[i]),
            ((fed[i][0], 1, 0), (fed[i][3], 1, 0), (fed_other[i], 1, HELD), rel_full,
             (vec_full, None, 0), (teacher[i][0], 2, 1), (teacher[i][1], 1, 1), (teacher[i][2], 2, 1),
             (teacher[i][3], 1, 1), (teacher[i][4], None, 0), *((value, None, HELD) for value in earlier)),
            (((features, 3 * flat), BF16 if last else F32, HELD), (*act, 1)),
            scratch=(
                ((features, 3 * flat), F32), act, head_t, head_t, head_t, head_t, pair_rows, pair_rows, pair_rows,
                head_t, ((heads, size, rows), F32),
                ((pairs, rows, 2 * size), F32), ((pairs, rows, 2 * size), F32), ((bound_rows, BLOCK), F32),
            ),
            flops=30 * 10**9,
        )

    def feed_back(i, earlier):
        last = i + 1 == sequences
        sums = ((features, 8), F32)
        return launch(
            functools.partial(feed_back_kernel, bool(earlier)), "feed_back", (live[i],),
            ((fed[i][0], 1, 0), (fed[i][3], 1, 0), (fed_other[i], 1, 0), (related[i][1], 1, 0),
             (down_other[i], None, HELD), (fed[i][1], 1, 0), (fed[i][2], 1, 0), in_full,
             out_full, (vec_full, None, 0), *((value, None, HELD) for value in earlier)),
            (((features, 2 * hidden), BF16 if last else F32, HELD), (*sums, HELD), (*wide, 1), (*act, HELD)),
            scratch=(((features, 2 * hidden), F32), sums),
            flops=4 * 10**9,
        )

    def attend_back(i, earlier):
        last = i + 1 == sequences
        running = (((features, 4 * flat), F32), ((features, 8), F32), ((flat, 8), F32))
        return launch(
            functools.partial(attend_back_kernel, bool(earlier), last), "attend_back",
            (live[i], core.reshape(1).astype(jnp.int32)),
            ((statest, 1, 0, i * rows // BLOCK), (attended[i][7], 1, 0), (mixed_other[i], 1, 0), (fed_back[i][2], 1, 0),
             (fed_back[i][3], 1, HELD), (up_other[i], None, HELD), attn_full, (vec_full, None, 0),
             (attended[i][0], 2, 1), (attended[i][1], 2, 1), (attended[i][2], 1, 1), (attended[i][3], 1, 1),
             (attended[i][4], 1, 1), (attended[i][5], 2, 0), (attended[i][6], 2, 1),
             *([(fed_back[i][1], None, HELD)] if last else []), *((value, None, HELD) for value in earlier)),
            (((features, 4 * flat + 8), BF16, HELD),) if last else tuple((*spec, HELD) for spec in running),
            scratch=running + (
                head_t, pair_rows, ((heads, 8, rows), F32), head_t,
                ((pairs, rows, 2 * size), F32), ((pairs, rows, 2 * size), F32),
            ),
            flops=15 * 10**9,
        )

    related, down_other = [], []
    for i in each:
        related.append(relate(i, related[-1][:1] if related else ()))
        down_other.append(exchange(related[i][1]))
    sent_rel = send_owner(related[-1][0])
    fed_back, up_other = [], []
    for i in each:
        fed_back.append(feed_back(i, fed_back[-1][:2] if fed_back else ()))
        up_other.append(exchange(fed_back[i][3]))
    sent_feed = send_owner(fed_back[-1][0])
    attended_back = []
    for i in each:
        attended_back.append(attend_back(i, attended_back[-1] if attended_back else ()))
    sent_attn = send_owner(after(attended_back[-1][0], sent_rel, sent_feed))
    shard_rel, shard_feed = add_parts(sent_rel), add_parts(sent_feed)
    shard_in, shard_out = shard_feed[:, :hidden], shard_feed[:, hidden:]
    own, message = collect(sent_attn, jnp.sum(shard_feed * shard_feed) + jnp.sum(shard_rel * shard_rel), 6, 1.0 / cores)
    grad_norm = jnp.sqrt(jnp.sum(lax.all_to_all(message, ("dp", "ffn"), 0, 0, tiled=True)[:, 0]))
    other = swap(own, "ffn", 0)
    grad_rel = shard_rel.reshape(attn_b.shape)
    upper = core == 1
    low, high = jnp.where(upper, other, own), jnp.where(upper, own, other)
    columns = [
        half[:, start : start + flat] for start in range(0, 4 * flat, flat) for half in (low, high)
    ]
    grad_attn = jnp.concatenate(columns, axis=1)
    grad_vec = jnp.concatenate([(low + high)[:, 4 * flat : 4 * flat + 2], own[:, 4 * flat + 2 :]], axis=1)
    gradients = (grad_attn, shard_in, shard_out, grad_rel, grad_vec)
    clipped = jnp.minimum(1.0, CLIP_NORM / grad_norm)
    masters = (attn_a, ffn_in, ffn_out, attn_b, vec_d)
    firsts = (mom1_attn_a, mom1_ffn_in, mom1_ffn_out, mom1_attn_b, mom1_vec_d)
    seconds = (mom2_attn_a, mom2_ffn_in, mom2_ffn_out, mom2_attn_b, mom2_vec_d)
    rates = (RATE_MATRIX, RATE_MATRIX, RATE_MATRIX, RATE_MATRIX, RATE_VECTOR)
    decays = (DECAY_RATE, DECAY_RATE, DECAY_RATE, DECAY_RATE, 0.0)
    news = [
        adam_update(masters[i], gradients[i], firsts[i], seconds[i], clipped, rates[i], decays[i])
        for i in range(5)
    ]
    return (grad_norm, *(new[0] for new in news), *(new[1] for new in news), *(new[2] for new in news))


def solution(mesh):
    matrix = P("dp", None)
    halved = P("dp", "ffn")
    cube = P("dp", None, "ffn")
    trained = (matrix, halved, halved, cube, matrix)
    in_specs = (matrix, matrix, P("dp"), P("dp"), P(), P(None, None, "ffn")) + trained * 3
    out_specs = (P(),) + trained * 3
    return jax.shard_map(per_device, mesh=mesh, in_specs=in_specs, out_specs=out_specs, check_vma=False)
```

```python
import functools

import jax
import jax.numpy as jnp
from jax import lax
from jax.experimental import pallas as pl
from jax.experimental.pallas import tpu as pltpu
from jax.sharding import PartitionSpec as P

HEADS = 12
STEP = 10

NORM_EPSILON = 1e-12
CLIP_NORM = 1.0
BETA_ONE = 0.9
BETA_TWO = 0.999
ADAM_EPSILON = 1e-08
RATE_MATRIX = 0.04
RATE_VECTOR = 0.2
DECAY_RATE = 0.01
MASK_VALUE = -1e30
LOG2_E = 1.4426950408889634
BLOCK = 256
SAFE_EXPONENT = 100.0
HELD = -1
VMEM_BYTES = 24 * 2**20
F32 = jnp.float32
BF16 = jnp.bfloat16


def nn(left, right):
    return lax.dot_general(left, right, (((1,), (0,)), ((), ())), preferred_element_type=F32)


def nt(left, right):
    return lax.dot_general(left, right, (((1,), (1,)), ((), ())), preferred_element_type=F32)


def tn(left, right):
    return lax.dot_general(left, right, (((0,), (0,)), ((), ())), preferred_element_type=F32)


def lanes(block):
    return pl.ds(pl.multiple_of(block * BLOCK, BLOCK), BLOCK)


def live_blocks(len_ref):
    return (len_ref[0] + BLOCK - 1) // BLOCK


def for_keys(length, most, safe, body, spare=BLOCK // 2):
    sizes = [n * BLOCK for n in range(1, most)] + ([most * BLOCK - spare] if spare else []) + [most * BLOCK]
    for lower, keys in zip([0] + sizes, sizes):
        fits = jnp.logical_and(length > lower, length <= keys)
        pl.when(jnp.logical_and(safe, fits))(functools.partial(body, keys))


def for_size(length, most, safe, fast, slow, spare=BLOCK // 2):
    for_keys(length, most, safe, fast, spare)
    pl.when(jnp.logical_not(safe))(slow)


def pipeline(count, first, second, third):
    firsts, seconds = {}, {}
    for t in range(count + 2):
        if t < count:
            firsts[t] = first(t)
        if 0 <= t - 1 < count:
            seconds[t - 1] = second(t - 1, firsts.pop(t - 1))
        if 0 <= t - 2 < count:
            third(t - 2, seconds.pop(t - 2))


def staged(blocks, first, second):
    def step(block, held):
        ahead = first(block)
        second(block - 1, held)
        return ahead

    second(blocks - 1, lax.fori_loop(1, blocks, step, first(jnp.int32(0))))


def squared_lengths(flat, size):
    features = flat.shape[0]
    groups = -(-features // size // 8) * 8
    row = lax.broadcasted_iota(jnp.int32, (groups, features), 0)
    column = lax.broadcasted_iota(jnp.int32, (groups, features), 1)
    ones = jnp.where((column >= row * size) & (column < (row + 1) * size), 1.0, 0.0).astype(BF16)
    return nn(ones, flat * flat)


def clear_dead(blocks, rows, *refs):
    def step(block, carry):
        for ref in refs:
            ref[:, :, lanes(block)] = jnp.zeros(ref.shape[:2] + (BLOCK,), ref.dtype)
        return carry

    lax.fori_loop(blocks, rows // BLOCK, step, 0)


def norm_forward(resid):
    features = resid.shape[0]
    centred = resid - jnp.sum(resid, axis=0, keepdims=True) * (1.0 / features)
    variance = jnp.sum(centred * centred, axis=0, keepdims=True) * (1.0 / features)
    inverse = lax.rsqrt(variance + NORM_EPSILON)
    return centred * inverse, inverse


def norm_backward(scaled, normed, inverse):
    features = scaled.shape[0]
    mean = jnp.sum(scaled, axis=0, keepdims=True) * (1.0 / features)
    slope = jnp.sum(scaled * normed, axis=0, keepdims=True) * (1.0 / features)
    return inverse * (scaled - mean - normed * slope)


def mask_tail(scores, length, start=None):
    keys = scores.shape[0]
    start = keys - BLOCK if start is None else start
    rows = start + lax.broadcasted_iota(jnp.int32, (keys - start, scores.shape[1]), 0)
    tail = jnp.where(rows < length, scores[start:], MASK_VALUE)
    if start == 0:
        return tail
    return jnp.concatenate([scores[:start], tail], axis=0)


def pad_rows(part, index, count):
    zeros = jnp.zeros_like(part)
    return jnp.concatenate([part if i == index else zeros for i in range(count)], axis=0)


def pad_half(part, half):
    zeros = jnp.zeros_like(part)
    return jnp.concatenate([jnp.where(half == 0, part, zeros), jnp.where(half == 0, zeros, part)], axis=0)


def pad_lanes(pair, index, size):
    lane = lax.broadcasted_iota(jnp.int32, pair.shape, 1)
    return jnp.where((lane >= index * size) & (lane < (index + 1) * size), pair, jnp.zeros_like(pair))


def split_heads(flat, ref, columns, size):
    heads = flat.shape[0] // size
    for head in range(heads):
        ref[head, :, columns] = flat[head * size : (head + 1) * size]


def split_pairs(flat, ref, rows):
    pairs, width = ref.shape[0], ref.shape[2]
    for pair in range(pairs):
        ref[pair, rows, :] = flat[pair * width : (pair + 1) * width].T


def teacher_kernel(traffic, len_ref, rows_ref, weight_ref, qt_ref, k_ref, vt_ref, v_ref, bound_ref):
    size = qt_ref.shape[1]
    scaling = LOG2_E * size ** (-0.5)
    bound_ref[...] = jnp.zeros(bound_ref.shape, F32)

    def step(block, carry):
        where = lanes(block)
        traffic.take(block)
        rows = rows_ref[where, :]
        queries, keys, values = [nn(rows, weight_ref[index]) for index in range(3)]
        scaled = [(part * scaling).astype(BF16).T for part in (queries, values)]
        queries, keys, values = queries.astype(BF16), keys.astype(BF16), values.astype(BF16)
        columns = [scaled[0], keys.T, scaled[1]]
        bound_ref[...] = jnp.maximum(bound_ref[...], squared_lengths(jnp.concatenate(columns, axis=0), size))
        split_heads(columns[0], qt_ref, where, size)
        split_heads(columns[2], vt_ref, where, size)
        for pair in range(k_ref.shape[0]):
            k_ref[pair, where, :] = keys[:, 2 * size * pair : 2 * size * (pair + 1)]
            v_ref[pair, where, :] = values[:, 2 * size * pair : 2 * size * (pair + 1)]
        traffic.give(block, 0, 1, 2, 3)
        return carry

    lax.fori_loop(0, live_blocks(len_ref), step, 0)


def attend_kernel(
    traffic, len_ref, xt_ref, weight_ref, vec_ref, qt_ref, kt_ref, q_ref, k_ref, v_ref, ot_ref, lse_ref, at_ref,
    vone_ref, bound_ref,
):
    heads, size, rows = qt_ref.shape
    flat = heads * size
    scaling = LOG2_E * size ** (-0.5)
    blocks = live_blocks(len_ref)
    length = len_ref[0]
    bound_ref[...] = jnp.zeros(bound_ref.shape, F32)

    def project(block, carry):
        where = lanes(block)
        traffic.take(block)
        xt = xt_ref[:, where]
        projected = tn(weight_ref[:, : 3 * flat], xt)
        query = projected[:flat] + vec_ref[:, 0:1]
        scaled = (query * scaling).astype(BF16)
        query = query.astype(BF16)
        keys = projected[flat : 2 * flat].astype(BF16)
        values = (projected[2 * flat :] + vec_ref[:, 1:2]).astype(BF16)
        split_heads(scaled, qt_ref, where, size)
        split_heads(keys, kt_ref, where, size)
        bound_ref[...] = jnp.maximum(
            bound_ref[...], squared_lengths(jnp.concatenate([query, keys], axis=0), size)
        )
        column = block * BLOCK + lax.broadcasted_iota(jnp.int32, (1, BLOCK), 1)
        live = jnp.where(column < length, 1.0, 0.0)
        live_values = (values.astype(F32) * live).astype(BF16)
        for head in range(heads):
            vone_ref[head, :size, where] = live_values[head * size : (head + 1) * size]
            vone_ref[head, size:, where] = jnp.broadcast_to(live, (16, BLOCK)).astype(BF16)
        split_pairs(query, q_ref, where)
        split_pairs(keys, k_ref, where)
        split_pairs(values, v_ref, where)
        traffic.give(block, 0, 1, 2, 3, 4)
        return carry

    lax.fori_loop(0, blocks, project, 0)

    longest = jnp.max(bound_ref[...], axis=1, keepdims=True)
    safe = jnp.max(longest[:heads] * longest[heads : 2 * heads]) * scaling**2 <= SAFE_EXPONENT**2

    def scores(pair, half, where, keys):
        return nn(k_ref[pair, :keys, :], pad_rows(qt_ref[2 * pair + half, :, where], half, 2))

    def mix(head, where, keys, grown, top):
        mixed = nn(vone_ref[head, :, :keys], grown)
        total = mixed[size : size + 1]
        ot_ref[head, :, where] = mixed[:size] * (1.0 / total)
        lse_ref[head, :, where] = jnp.broadcast_to(top + jnp.log2(total), (8, BLOCK))

    def fast(keys):
        def step(block, carry):
            where = lanes(block)
            pipeline(
                heads,
                lambda head: scores(head // 2, head % 2, where, keys),
                lambda head, score: jnp.exp2(score).astype(BF16),
                lambda head, grown: mix(head, where, keys, grown, 0.0),
            )
            traffic.give(block, 5, 6)
            return carry

        lax.fori_loop(0, blocks, step, 0)

    def slow():
        clear_dead(blocks, rows, vone_ref)

        def step(index, carry):
            block, head = index // heads, index % heads
            where = lanes(block)
            score = nn(k_ref[head // 2], pad_half(qt_ref[head, :, where], head % 2))
            score = mask_tail(score, length, 0)
            top = jnp.max(score, axis=0, keepdims=True)
            mix(head, where, rows, jnp.exp2(score - top).astype(BF16), top)
            pl.when(head == heads - 1)(lambda: traffic.give(block, 5, 6))
            return carry

        lax.fori_loop(0, blocks * heads, step, 0)

    for_size(length, rows // BLOCK, safe, fast, slow)

    def output(block, carry):
        where = lanes(block)
        mixed = ot_ref[:, :, where].reshape(flat, BLOCK).astype(BF16)
        at_ref[:, where] = nn(weight_ref[:, 3 * flat :], mixed).astype(BF16)
        traffic.give(block, 7)
        return carry

    lax.fori_loop(0, blocks, output, 0)


def first_norm(xt, own, other, vec_ref):
    resid = xt.astype(F32) + (own.astype(F32) + other.astype(F32)) + vec_ref[:, 2:3]
    return norm_forward(resid)


def feed_kernel(traffic, len_ref, xt_ref, own_ref, other_ref, in_ref, out_ref, vec_ref, ht_ref, zt_ref, slope_ref, ft_ref):
    def first(block):
        where = lanes(block)
        traffic.take(block)
        normed, _ = first_norm(xt_ref[:, where], own_ref[:, where], other_ref[:, where], vec_ref)
        hidden = normed * vec_ref[:, 3:4] + vec_ref[:, 4:5]
        ht_ref[:, where] = hidden
        return tn(in_ref[...], hidden.astype(BF16))

    def second(block, pre):
        where = lanes(block)
        cdf = 0.5 + 0.5 * lax.erf(pre * (0.5**0.5))
        pdf = jnp.exp2(pre * pre * (-0.5 * LOG2_E)) * 0.3989422804014327
        active = (pre * cdf).astype(BF16)
        zt_ref[:, where] = active
        slope_ref[:, where] = (cdf + pre * pdf).astype(BF16)
        ft_ref[:, where] = nn(out_ref[...], active).astype(BF16)
        traffic.give(block, 0, 1, 2, 3)

    staged(live_blocks(len_ref), first, second)


def second_norm(ht, own, other, vec_ref):
    resid = ht + (own.astype(F32) + other.astype(F32)) + vec_ref[:, 5:6]
    return norm_forward(resid)


def relation_kernel(
    chained, traffic, len_ref, weight_ref, ht_ref, own_ref, other_ref, rel_ref, vec_ref, tqt_ref, tk_ref, tvt_ref, tv_ref,
    tbound_ref, *refs,
):
    earlier_ref, refs = (refs[0], refs[1:]) if chained else (None, refs)
    grad_out_ref, dt_ref, refs = refs[0], refs[1], refs[2:]
    grad_ref, refs = refs[0], refs[1:]
    relation_body(
        traffic, len_ref, weight_ref, ht_ref, own_ref, other_ref, rel_ref, vec_ref, tqt_ref, tk_ref, tvt_ref, tv_ref,
        tbound_ref, grad_ref, dt_ref, *refs,
    )
    traffic.take_last()
    grad = grad_ref[...] + earlier_ref[...] if chained else grad_ref[...]
    grad_out_ref[...] = grad.astype(grad_out_ref.dtype)


def relation_body(
    traffic, len_ref, weight_ref, ht_ref, own_ref, other_ref, rel_ref, vec_ref, tqt_ref, tk_ref, tvt_ref, tv_ref,
    tbound_ref, grad_ref, dt_ref,
    h2_ref, qt_ref, kt_ref, vt_ref, st_ref, q_ref, k_ref, v_ref, dqt_ref, dvt_ref, dk_ref, dv_ref, bound_ref,
):
    heads, size, rows = qt_ref.shape
    teacher_size = tqt_ref.shape[1]
    flat = heads * size
    plain = size ** (-0.5)
    scaling = LOG2_E * plain
    teacher_scaling = LOG2_E * teacher_size ** (-0.5)
    blocks = live_blocks(len_ref)
    length = len_ref[0]
    weight = weight_ref[0]
    bound_ref[...] = jnp.zeros(bound_ref.shape, F32)

    def project(block, carry):
        where = lanes(block)
        traffic.take(block)
        normed, _ = second_norm(ht_ref[:, where], own_ref[:, where], other_ref[:, where], vec_ref)
        hidden = (normed * vec_ref[:, 6:7] + vec_ref[:, 7:8]).astype(BF16)
        h2_ref[:, where] = hidden
        projected = tn(rel_ref[...], hidden)
        split_heads((projected[:flat] * scaling).astype(BF16), qt_ref, where, size)
        split_heads((projected[2 * flat :] * scaling).astype(BF16), st_ref, where, size)
        projected = projected.astype(BF16)
        bound_ref[...] = jnp.maximum(bound_ref[...], squared_lengths(projected, size))
        split_heads(projected[flat : 2 * flat], kt_ref, where, size)
        split_heads(projected[2 * flat :], vt_ref, where, size)
        split_pairs(projected[:flat], q_ref, where)
        split_pairs(projected[flat : 2 * flat], k_ref, where)
        split_pairs(projected[2 * flat :], v_ref, where)
        for pair in range(heads // 2):
            dk_ref[pair, where, :] = jnp.zeros((BLOCK, 2 * size), F32)
            dv_ref[pair, where, :] = jnp.zeros((BLOCK, 2 * size), F32)
        return carry

    lax.fori_loop(0, blocks, project, 0)

    traffic.take_rest()

    def exponents(ref, attention_scale, relation_scale):
        longest = jnp.max(ref[...], axis=1, keepdims=True)
        attention = jnp.max(longest[:heads] * longest[heads : 2 * heads]) * attention_scale**2
        relation = jnp.max(longest[2 * heads : 3 * heads]) * relation_scale
        return jnp.logical_and(attention <= SAFE_EXPONENT**2, relation <= SAFE_EXPONENT)

    safe = jnp.logical_and(
        exponents(bound_ref, scaling, scaling), exponents(tbound_ref, 1.0, 1.0 / teacher_scaling)
    )
    pairs = heads // 2
    attention = (k_ref, qt_ref, q_ref, tk_ref, tqt_ref, kt_ref, dqt_ref, dk_ref)
    relation = (v_ref, st_ref, v_ref, tv_ref, tvt_ref, vt_ref, dvt_ref, dv_ref)
    tasks = [(half, refs) for refs in (attention, relation) for half in range(2)]

    def live_weight(where):
        column = where.start + lax.broadcasted_iota(jnp.int32, (1, BLOCK), 1)
        return jnp.where(column < length, weight, 0.0)

    def steps(keys, pair, where):
        live = live_weight(where)
        kept = {}

        def first(t):
            half, (left, rightt, _, teacher_left, teacher_rightt, _, _, _) = tasks[t]
            head = 2 * pair + half
            student = nn(left[pair, :keys, :], pad_rows(rightt[head, :, where], half, 2))
            teacher = nn(teacher_left[pair, :keys, :], pad_rows(teacher_rightt[head, :, where], half, 2))
            return student, teacher

        def second(t, scores):
            student, teacher = [jnp.exp2(mask_tail(score, length)) for score in scores]
            student_part = live / jnp.sum(student, axis=0, keepdims=True)
            teacher_part = live / jnp.sum(teacher, axis=0, keepdims=True)
            return (student * student_part - teacher * teacher_part).astype(BF16)

        def third(t, grad):
            half, (_, _, right, _, _, leftt, own_ref, running_ref) = tasks[t]
            head = 2 * pair + half
            own_ref[head, :, where] = (nn(leftt[head, :, :keys], grad) * plain).astype(own_ref.dtype)
            kept[half] = grad
            if half == 1:
                queries = right[pair, where, :]
                stacked = jnp.concatenate([pad_lanes(queries, i, size) for i in range(2)], axis=0)
                running_ref[pair, :keys, :] += nn(jnp.concatenate([kept[0], kept[1]], axis=1), stacked)

        return first, second, third

    def fast(keys):
        def step(index, carry):
            stages = steps(keys, index % pairs, lanes(index // pairs))
            pipeline(len(tasks), *stages)
            return carry

        lax.fori_loop(0, blocks * pairs, step, 0)

    def slow():
        clear_dead(blocks, rows, kt_ref, vt_ref)

        def step(index, carry):
            half, pair, where = index % 2, index // 2 % pairs, lanes(index // 2 // pairs)
            head = 2 * pair + half
            live = live_weight(where)
            for left, rightt, right, teacher_left, teacher_rightt, leftt, own_ref, running_ref in (attention, relation):
                parts = []
                for keys, queries in ((left, rightt), (teacher_left, teacher_rightt)):
                    score = mask_tail(nn(keys[pair], pad_half(queries[head, :, where], half)), length, 0)
                    grown = jnp.exp2(score - jnp.max(score, axis=0, keepdims=True))
                    parts.append(grown * (live / jnp.sum(grown, axis=0, keepdims=True)))
                grad = (parts[0] - parts[1]).astype(BF16)
                own_ref[head, :, where] = (nn(leftt[head], grad) * plain).astype(own_ref.dtype)
                running_ref[pair] += nn(grad, pad_lanes(right[pair, where, :], half, size))
            return carry

        lax.fori_loop(0, blocks * heads, step, 0)

    for_size(length, rows // BLOCK, safe, fast, slow)
    grad_ref[...] = jnp.zeros(grad_ref.shape, F32)

    def finish(block, carry):
        where = lanes(block)
        queries = dqt_ref[:, :, where].reshape(flat, BLOCK)
        keys = jnp.concatenate([dk_ref[pair, where, :].T for pair in range(heads // 2)], axis=0) * plain
        values = jnp.concatenate([dv_ref[pair, where, :].T for pair in range(heads // 2)], axis=0) * plain
        values = values + dvt_ref[:, :, where].reshape(flat, BLOCK)
        grads = jnp.concatenate([queries, keys.astype(BF16), values.astype(BF16)], axis=0)
        grad_ref[...] += nt(h2_ref[:, where], grads)
        dt_ref[:, where] = nn(rel_ref[...], grads).astype(BF16)
        traffic.give(block, 1)
        return carry

    lax.fori_loop(0, blocks, finish, 0)


def feed_back_kernel(
    chained, traffic, len_ref, ht_ref, own_ref, other_ref, down_own_ref, down_other_ref, zt_ref, slope_ref, in_ref, out_ref, vec_ref, *refs,
):
    earlier, refs = (refs[:2], refs[2:]) if chained else (None, refs)
    total_ref, sums_out_ref, resid_ref, up_ref, refs = *refs[:4], refs[4:]
    grad_ref, sums_ref = refs
    hidden_units = in_ref.shape[1]
    grad_ref[...] = jnp.zeros(grad_ref.shape, F32)
    sums_ref[...] = jnp.zeros(sums_ref.shape, F32)

    def first(block):
        where = lanes(block)
        traffic.take(block)
        normed, inverse = second_norm(ht_ref[:, where], own_ref[:, where], other_ref[:, where], vec_ref)
        grad = down_own_ref[:, where].astype(F32) + down_other_ref[:, where].astype(F32)
        resid = norm_backward(grad * vec_ref[:, 6:7], normed, inverse)
        resid_ref[:, where] = resid
        sums_ref[:, 0:1] += jnp.sum(resid, axis=1, keepdims=True)
        sums_ref[:, 1:2] += jnp.sum(grad * normed, axis=1, keepdims=True)
        sums_ref[:, 2:3] += jnp.sum(grad, axis=1, keepdims=True)
        return resid.astype(BF16)

    def second(block, branch):
        where = lanes(block)
        grad_ref[:, hidden_units:] += nt(branch, zt_ref[:, where])
        pre_grad = (tn(out_ref[...], branch) * slope_ref[:, where].astype(F32)).astype(BF16)
        grad_ref[:, :hidden_units] += nt(ht_ref[:, where].astype(BF16), pre_grad)
        up_ref[:, where] = nn(in_ref[...], pre_grad).astype(BF16)
        traffic.give(block, 2, 3)

    staged(live_blocks(len_ref), first, second)
    traffic.take_last()
    grad, sums = grad_ref[...], sums_ref[...]
    if chained:
        grad, sums = grad + earlier[0][...], sums + earlier[1][...]
    total_ref[...] = grad.astype(total_ref.dtype)
    sums_out_ref[...] = sums


def attend_back_kernel(
    chained, last, traffic, len_ref, core_ref, xt_ref, own_ref, other_ref, resid_ref, up_own_ref, up_other_ref, weight_ref, vec_ref,
    qt_ref, kt_ref, q_ref, k_ref, v_ref, ot_ref, lse_ref, *refs,
):
    back_sums_ref, refs = (refs[0], refs[1:]) if last else (None, refs)
    earlier, refs = (refs[:3], refs[3:]) if chained else (None, refs)
    outs, refs = (refs[:1], refs[1:]) if last else (refs[:3], refs[3:])
    running, refs = refs[:3], refs[3:]
    grad_ref, sums_ref, head_sums_ref = running
    for ref in running:
        ref[...] = jnp.zeros(ref.shape, F32)
    attend_back_body(
        traffic, len_ref, xt_ref, own_ref, other_ref, resid_ref, up_own_ref, up_other_ref, weight_ref, vec_ref,
        qt_ref, kt_ref, q_ref, k_ref, v_ref, ot_ref, lse_ref, grad_ref, sums_ref, head_sums_ref, *refs,
    )
    traffic.take_last()
    if chained:
        for ref, value in zip(running, earlier):
            ref[...] += value[...]
    if not last:
        for ref, value in zip(outs, running):
            ref[...] = value[...]
        return
    total_ref = outs[0]
    columns, flat = grad_ref.shape[1], head_sums_ref.shape[0]
    total_ref[:, :columns] = grad_ref[...].astype(BF16)
    biases = head_sums_ref[:, 0:2].astype(BF16)
    total_ref[:, columns : columns + 2] = jnp.zeros((total_ref.shape[0], 2), BF16)
    for core in range(total_ref.shape[0] // flat):

        @pl.when(core_ref[0] == core)
        def _(core=core):
            total_ref[core * flat : (core + 1) * flat, columns : columns + 2] = biases

    total_ref[:, columns + 2 : columns + 5] = sums_ref[:, 0:3].astype(BF16)
    total_ref[:, columns + 5 : columns + 8] = back_sums_ref[:, 0:3].astype(BF16)


def attend_back_body(
    traffic, len_ref, xt_ref, own_ref, other_ref, resid_ref, up_own_ref, up_other_ref, weight_ref, vec_ref,
    qt_ref, kt_ref, q_ref, k_ref, v_ref, ot_ref, lse_ref, grad_ref, sums_ref, head_sums_ref,
    dot_ref, do_ref, inner_ref, dqt_ref, dk_ref, dv_ref,
):
    heads, size, rows = qt_ref.shape
    flat = heads * size
    plain = size ** (-0.5)
    scaling = LOG2_E * plain
    blocks = live_blocks(len_ref)
    length = len_ref[0]

    def start(block, carry):
        where = lanes(block)
        traffic.take(block)
        normed, inverse = first_norm(xt_ref[:, where], own_ref[:, where], other_ref[:, where], vec_ref)
        grad = resid_ref[:, where] + (up_own_ref[:, where].astype(F32) + up_other_ref[:, where].astype(F32))
        branch = norm_backward(grad * vec_ref[:, 3:4], normed, inverse).astype(BF16)
        sums_ref[:, 0:1] += jnp.sum(branch.astype(F32), axis=1, keepdims=True)
        sums_ref[:, 1:2] += jnp.sum(grad * normed, axis=1, keepdims=True)
        sums_ref[:, 2:3] += jnp.sum(grad, axis=1, keepdims=True)
        mixed = ot_ref[:, :, where]
        grad_ref[:, 3 * flat :] += nt(branch, mixed.reshape(flat, BLOCK).astype(BF16))
        mixed_grad = tn(weight_ref[:, 3 * flat :], branch).astype(BF16)
        split_heads(mixed_grad, dot_ref, where, size)
        split_pairs(mixed_grad, do_ref, where)
        for head in range(heads):
            product = mixed_grad[head * size : (head + 1) * size].astype(F32) * mixed[head]
            inner_ref[head, :, where] = jnp.broadcast_to(jnp.sum(product, axis=0, keepdims=True), (8, BLOCK))
        for pair in range(heads // 2):
            dk_ref[pair, where, :] = jnp.zeros((BLOCK, 2 * size), F32)
            dv_ref[pair, where, :] = jnp.zeros((BLOCK, 2 * size), F32)
        return carry

    lax.fori_loop(0, blocks, start, 0)
    traffic.take_rest()

    def attend(keys):
        def step(block, carry):
            where = lanes(block)
            kept = {}

            def first(head):
                pair, half = head // 2, head % 2
                scores = nn(k_ref[pair, :keys, :], pad_rows(qt_ref[head, :, where], half, 2))
                prob_grad = nn(v_ref[pair, :keys, :], pad_rows(dot_ref[head, :, where], half, 2))
                return scores, prob_grad

            def second(head, parts):
                scores, prob_grad = parts
                prob = jnp.exp2(mask_tail(scores, length) - lse_ref[head, 0:1, where])
                grad = (prob * (prob_grad - inner_ref[head, 0:1, where])).astype(BF16)
                return prob.astype(BF16), grad

            def third(head, parts):
                pair = head // 2
                dqt_ref[head, :, where] = (nn(kt_ref[head, :, :keys], parts[1]) * plain).astype(BF16)
                kept[head % 2] = parts
                if head % 2 == 1:
                    for index, right, running in ((1, q_ref, dk_ref), (0, do_ref, dv_ref)):
                        queries = right[pair, where, :]
                        stacked = jnp.concatenate([pad_lanes(queries, half, size) for half in range(2)], axis=0)
                        running[pair, :keys, :] += nn(
                            jnp.concatenate([kept[0][index], kept[1][index]], axis=1), stacked
                        )

            pipeline(heads, first, second, third)
            return carry

        lax.fori_loop(0, blocks, step, 0)

    for_keys(length, rows // BLOCK, True, attend, 0)

    def finish(block, carry):
        where = lanes(block)
        queries = dqt_ref[:, :, where].reshape(flat, BLOCK)
        keys = jnp.concatenate([dk_ref[pair, where, :].T for pair in range(heads // 2)], axis=0) * plain
        values = jnp.concatenate([dv_ref[pair, where, :].T for pair in range(heads // 2)], axis=0).astype(BF16)
        head_sums_ref[:, 0:1] += jnp.sum(queries.astype(F32), axis=1, keepdims=True)
        head_sums_ref[:, 1:2] += jnp.sum(values.astype(F32), axis=1, keepdims=True)
        grads = jnp.concatenate([queries, keys.astype(BF16), values], axis=0)
        grad_ref[:, : 3 * flat] += nt(xt_ref[:, where], grads)
        return carry

    lax.fori_loop(0, blocks, finish, 0)


class Traffic:
    def __init__(self, blocks, ins, outs, in_sems, out_sems):
        self.blocks, self.ins, self.outs, self.in_sems, self.out_sems = blocks, ins, outs, in_sems, out_sems

    def part(self, ref, axis, block):
        return ref if axis is None else ref.at[(slice(None),) * axis + (lanes(block),)]

    def inward(self, index, block):
        source, target, axis, _, first = self.ins[index]
        if axis is None:
            if first:
                source = source.at[:, first[0] : first[0] + first[1]]
            return pltpu.make_async_copy(source, target, self.in_sems.at[index, 0])
        return pltpu.make_async_copy(
            self.part(source, axis, first + block), self.part(target, axis, block), self.in_sems.at[index, block]
        )

    def outward(self, index, block):
        target, source, axis = self.outs[index]
        return pltpu.make_async_copy(
            self.part(source, axis, block), self.part(target, axis, block), self.out_sems.at[index, block]
        )

    def chosen(self, group, whole=False):
        return [i for i, entry in enumerate(self.ins) if (entry[2] is None) == whole and entry[3] == group]

    def start(self):
        for index in self.chosen(0, whole=True):
            self.inward(index, 0).start()
        for group in (0, 1):
            indices = self.chosen(group)

            def step(block, carry):
                for index in indices:
                    self.inward(index, block).start()
                return carry

            if indices:
                lax.fori_loop(0, self.blocks, step, 0)
        for index in self.chosen(1, whole=True):
            self.inward(index, 0).start()
        for index in self.chosen(0, whole=True):
            self.inward(index, 0).wait()

    def take(self, block):
        for index in self.chosen(0):
            self.inward(index, block).wait()

    def take_rest(self):
        def step(block, carry):
            for index in self.chosen(1):
                self.inward(index, block).wait()
            return carry

        lax.fori_loop(0, self.blocks, step, 0)

    def take_last(self):
        for index in self.chosen(1, whole=True):
            self.inward(index, 0).wait()

    def give(self, block, *indices):
        for index in indices:
            if self.outs[index][2] != HELD:
                self.outward(index, block).start()

    def finish(self):
        whole = [i for i, entry in enumerate(self.outs) if entry[2] is None]
        parts = [i for i, entry in enumerate(self.outs) if entry[2] not in (None, HELD)]
        for index in whole:
            self.outward(index, 0).start()

        def step(block, carry):
            for index in parts:
                self.outward(index, block).wait()
            return carry

        if parts:
            lax.fori_loop(0, self.blocks, step, 0)
        for index in whole:
            self.outward(index, 0).wait()


def call(blocks, kernel, name, scalars, arrays, outs, scratch=(), flops=0):
    smem = pl.BlockSpec(memory_space=pltpu.SMEM)
    hbm = pl.BlockSpec(memory_space=pltpu.HBM)
    vmem = pl.BlockSpec(memory_space=pltpu.VMEM)
    arrays = [entry if len(entry) == 4 else (*entry, 0) for entry in arrays]

    def held(array, axis, group, first):
        shape = list(array.shape)
        if axis is not None:
            shape[axis] = blocks * BLOCK
        elif first:
            shape[1] = first[1]
        return pltpu.VMEM(tuple(shape), array.dtype)

    count, ins, results = len(scalars), len(arrays), len(outs)
    copied = [i for i in range(ins) if arrays[i][2] != HELD]
    filled = [i for i in range(results) if outs[i][2] != HELD]

    def view(ref, axis, group, first):
        if group != HELD or not first:
            return ref
        if axis is None:
            return ref.at[:, first[0] : first[0] + first[1]]
        return ref.at[(slice(None),) * axis + (slice(first * BLOCK, (first + blocks) * BLOCK),)]

    def body(*refs):
        scalar_refs, refs = refs[:count], refs[count:]
        in_refs, refs = refs[:ins], refs[ins:]
        out_refs, refs = refs[:results], refs[results:]
        in_copies = [view(ref, *entry[1:]) for ref, entry in zip(in_refs, arrays)]
        for index, ref in zip(copied, refs):
            in_copies[index] = ref
        refs = refs[len(copied) :]
        out_copies = list(out_refs)
        for index, ref in zip(filled, refs):
            out_copies[index] = ref
        refs = refs[len(filled) :]
        in_sems, out_sems, refs = refs[0], refs[1], refs[2:]
        traffic = Traffic(
            live_blocks(scalar_refs[0]),
            [(in_refs[i], in_copies[i], *arrays[i][1:]) for i in copied],
            [(ref, copy, axis) for ref, copy, (_, _, axis) in zip(out_refs, out_copies, outs)],
            in_sems,
            out_sems,
        )
        traffic.start()
        kernel(traffic, *scalar_refs, *in_copies, *out_copies, *refs)
        traffic.finish()

    return pl.pallas_call(
        body,
        name=name,
        out_shape=tuple(
            (pltpu.VMEM if axis == HELD else pltpu.HBM)(shape, dtype) for shape, dtype, axis in outs
        ),
        in_specs=[smem] * count
        + [vmem if group == HELD else hbm for _, _, group, _ in arrays],
        out_specs=tuple(vmem if axis == HELD else hbm for _, _, axis in outs),
        scratch_shapes=[held(*arrays[i]) for i in copied]
        + [pltpu.VMEM(*outs[i][:2]) for i in filled]
        + [pltpu.SemaphoreType.DMA((ins, blocks)), pltpu.SemaphoreType.DMA((results, blocks))]
        + [pltpu.VMEM(shape, dtype) for shape, dtype in scratch],
        compiler_params=pltpu.CompilerParams(vmem_limit_bytes=VMEM_BYTES),
        cost_estimate=pl.CostEstimate(flops=flops, bytes_accessed=4 << 20, transcendentals=0),
    )(
        *scalars,
        *(
            pltpu.with_memory_space_constraint(array, pltpu.VMEM if group == HELD else pltpu.HBM)
            for array, _, group, _ in arrays
        ),
    )


def exchange(part):
    return swap(part, "ffn", 0)


def swap(value, axis, bit):
    count = lax.axis_size(axis)
    return lax.ppermute(value, axis, [(i, i ^ (1 << bit)) for i in range(count)])


def bit_of(axis, bit):
    return (lax.axis_index(axis) >> bit) & 1


def dp_bits():
    return lax.axis_size("dp").bit_length() - 1


def after(value, *others):
    return lax.optimization_barrier((value, *others))[0]


def gather_step(whole, other, bit):
    dim = dp_bits() - 1 - bit
    upper = bit_of("dp", bit) == 1
    return jnp.where(upper, jnp.concatenate([other, whole], axis=dim), jnp.concatenate([whole, other], axis=dim))


def gather_direct(shard, *tokens):
    count = lax.axis_size("dp")
    spread = after(jnp.broadcast_to(shard[None], (count,) + shard.shape), *tokens)
    return lax.all_to_all(spread, "dp", 0, 0, tiled=True).reshape((-1,) + shard.shape[1:])


def collect_kernel(shared_columns, shared_weight, squares_ref, spread_ref, own_ref, message_ref):
    own = spread_ref[0].astype(F32)
    for source in range(1, spread_ref.shape[0]):
        own = own + spread_ref[source].astype(F32)
    own_ref[...] = own
    column = lax.broadcasted_iota(jnp.int32, own.shape, 1)
    weights = jnp.where(column < own.shape[1] - shared_columns, 1.0, shared_weight)
    squares = jnp.sum(jnp.sum(own * own * weights, axis=0, keepdims=True), axis=1, keepdims=True)
    message_ref[...] = jnp.broadcast_to(squares + squares_ref[0], message_ref.shape)


def collect(spread, squares, shared_columns, shared_weight):
    vmem = pl.BlockSpec(memory_space=pltpu.VMEM)
    count = lax.axis_size("dp") * lax.axis_size("ffn")
    return pl.pallas_call(
        functools.partial(collect_kernel, shared_columns, shared_weight),
        name="collect",
        out_shape=(pltpu.VMEM(spread.shape[1:], F32), pltpu.VMEM((count, 128), F32)),
        in_specs=[pl.BlockSpec(memory_space=pltpu.SMEM), vmem],
        out_specs=(vmem, vmem),
    )(squares.reshape(1), pltpu.with_memory_space_constraint(spread, pltpu.VMEM))


def send_owner(value):
    count = lax.axis_size("dp")
    rows = value.shape[0] // count
    return lax.all_to_all(value.astype(BF16).reshape((count, rows) + value.shape[1:]), "dp", 0, 0, tiled=True)


def add_parts(spread):
    return jnp.sum(spread.astype(F32), axis=0)


def adam_update(weight, gradient, first, second, clipped, rate, decay):
    scaled = gradient * clipped
    first_new = BETA_ONE * first + (1.0 - BETA_ONE) * scaled
    second_new = BETA_TWO * second + (1.0 - BETA_TWO) * scaled * scaled
    ratio = (
        first_new
        / (1.0 - BETA_ONE**STEP)
        / (jnp.sqrt(second_new / (1.0 - BETA_TWO**STEP)) + ADAM_EPSILON)
    )
    return (weight - rate * (ratio + decay * weight), first_new, second_new)


def per_device(
    states, teacher_states, lengths, domain_ids, domain_weight, teacher_qkv,
    attn_a, ffn_in, ffn_out, attn_b, vec_d,
    mom1_attn_a, mom1_ffn_in, mom1_ffn_out, mom1_attn_b, mom1_vec_d,
    mom2_attn_a, mom2_ffn_in, mom2_ffn_out, mom2_attn_b, mom2_vec_d,
):
    cores = lax.axis_size("ffn")
    core = lax.axis_index("ffn")
    replicas = lax.axis_size("dp")
    replica = lax.axis_index("dp")
    sequences = lengths.shape[0]
    rows = states.shape[0] // sequences
    features = states.shape[1]
    heads = HEADS // cores
    flat = features // cores
    size = flat // heads
    pairs = heads // 2
    hidden = ffn_in.shape[1]
    teacher_flat = teacher_qkv.shape[2]
    teacher_size = teacher_flat // heads
    shard = attn_a.shape[0]
    matched = domain_ids[:, None] == jnp.arange(domain_weight.shape[0])[None, :]
    sequence_weight = jnp.sum(jnp.where(matched, domain_weight[None, :], 0.0), axis=1) / HEADS

    teacher_w = teacher_qkv.transpose(1, 0, 2)
    statest = states.T
    live = [lengths[i : i + 1] for i in range(sequences)]
    weights = [sequence_weight[i : i + 1] for i in range(sequences)]
    each = range(sequences)
    launch = functools.partial(call, rows // BLOCK)
    act = ((features, rows), BF16)
    wide = ((features, rows), F32)
    head_t = ((heads, size, rows), BF16)
    pair_rows = ((pairs, rows, 2 * size), BF16)

    bound_rows = -(-3 * heads // 8) * 8

    def project_teacher(i, token):
        return launch(
            teacher_kernel, "teacher", (live[i],),
            ((after(teacher_states, *token), 0, 0, i * rows // BLOCK), (teacher_w, None, 0)),
            (
                ((heads, teacher_size, rows), BF16, 2),
                ((pairs, rows, 2 * teacher_size), BF16, 1),
                ((heads, teacher_size, rows), BF16, 2),
                ((pairs, rows, 2 * teacher_size), BF16, 1),
                ((bound_rows, BLOCK), F32, None),
            ),
            flops=2 * rows * 768 * 1152,
        )

    attn_own = [lax.dynamic_slice_in_dim(attn_a, start + core * flat, flat, 1) for start in range(0, 4 * features, features)]
    early = gather_direct(jnp.concatenate([*attn_own, vec_d], axis=1).astype(BF16))
    teacher = [project_teacher(i, (statest,)) for i in each]
    late_feed = gather_direct(jnp.concatenate([ffn_in, ffn_out], axis=1).astype(BF16), *teacher[0], *teacher[1])
    early = after(early, *teacher[0], *teacher[1])
    vec_full = early[:, 4 * flat :].astype(F32)
    vec_own = lax.dynamic_slice_in_dim(vec_full, core * flat, flat, 0)
    attn_full = (early, None, 0, (0, 4 * flat))

    attended = [
        launch(
            attend_kernel, "attend", (live[i],),
            ((statest, 1, 0, i * rows // BLOCK), attn_full, (vec_own, None, 0)),
            ((*head_t, 2), (*head_t, 2), (*pair_rows, 1), (*pair_rows, 1), (*pair_rows, 1),
             ((heads, size, rows), F32, 2), ((heads, 8, rows), F32, 2), (*act, 1)),
            scratch=(((heads, size + 16, rows), BF16), ((-(-2 * heads // 8) * 8, BLOCK), F32)),
            flops=6 * 10**9,
        )
        for i in each
    ]
    in_full, out_full = (late_feed, None, 0, (0, hidden)), (late_feed, None, 0, (hidden, hidden))
    late_rel = gather_direct(after(attn_b.reshape(shard, 3 * flat).astype(BF16), *attended[0]))
    rel_full = (late_rel, None, 0)
    mixed_other = [exchange(attended[i][7]) for i in each]
    fed = [
        launch(
            feed_kernel, "feed", (live[i],),
            ((statest, 1, 0, i * rows // BLOCK), (attended[i][7], 1, 0), (mixed_other[i], 1, HELD), in_full,
             out_full, (vec_full, None, 0)),
            ((*wide, 1), ((hidden, rows), BF16, 1), ((hidden, rows), BF16, 1), (*act, 1)),
            flops=3 * 10**9,
        )
        for i in each
    ]
    fed_other = [exchange(fed[i][3]) for i in each]

    def relate(i, earlier):
        last = i + 1 == sequences
        return launch(
            functools.partial(relation_kernel, bool(earlier)), "relation", (live[i], weights[i]),
            ((fed[i][0], 1, 0), (fed[i][3], 1, 0), (fed_other[i], 1, HELD), rel_full,
             (vec_full, None, 0), (teacher[i][0], 2, 1), (teacher[i][1], 1, 1), (teacher[i][2], 2, 1),
             (teacher[i][3], 1, 1), (teacher[i][4], None, 0), *((value, None, HELD) for value in earlier)),
            (((features, 3 * flat), BF16 if last else F32, HELD), (*act, 1)),
            scratch=(
                ((features, 3 * flat), F32), act, head_t, head_t, head_t, head_t, pair_rows, pair_rows, pair_rows,
                head_t, ((heads, size, rows), F32),
                ((pairs, rows, 2 * size), F32), ((pairs, rows, 2 * size), F32), ((bound_rows, BLOCK), F32),
            ),
            flops=30 * 10**9,
        )

    def feed_back(i, earlier):
        last = i + 1 == sequences
        sums = ((features, 8), F32)
        return launch(
            functools.partial(feed_back_kernel, bool(earlier)), "feed_back", (live[i],),
            ((fed[i][0], 1, 0), (fed[i][3], 1, 0), (fed_other[i], 1, 0), (related[i][1], 1, 0),
             (down_other[i], None, HELD), (fed[i][1], 1, 0), (fed[i][2], 1, 0), in_full,
             out_full, (vec_full, None, 0), *((value, None, HELD) for value in earlier)),
            (((features, 2 * hidden), BF16 if last else F32, HELD), (*sums, HELD), (*wide, 1), (*act, HELD)),
            scratch=(((features, 2 * hidden), F32), sums),
            flops=4 * 10**9,
        )

    def attend_back(i, earlier):
        last = i + 1 == sequences
        running = (((features, 4 * flat), F32), ((features, 8), F32), ((flat, 8), F32))
        return launch(
            functools.partial(attend_back_kernel, bool(earlier), last), "attend_back",
            (live[i], core.reshape(1).astype(jnp.int32)),
            ((statest, 1, 0, i * rows // BLOCK), (attended[i][7], 1, 0), (mixed_other[i], 1, 0), (fed_back[i][2], 1, 0),
             (fed_back[i][3], 1, HELD), (up_other[i], None, HELD), attn_full, (vec_full, None, 0),
             (attended[i][0], 2, 1), (attended[i][1], 2, 1), (attended[i][2], 1, 1), (attended[i][3], 1, 1),
             (attended[i][4], 1, 1), (attended[i][5], 2, 0), (attended[i][6], 2, 1),
             *([(fed_back[i][1], None, HELD)] if last else []), *((value, None, HELD) for value in earlier)),
            (((features, 4 * flat + 8), BF16, HELD),) if last else tuple((*spec, HELD) for spec in running),
            scratch=running + (
                head_t, pair_rows, ((heads, 8, rows), F32), head_t,
                ((pairs, rows, 2 * size), F32), ((pairs, rows, 2 * size), F32),
            ),
            flops=15 * 10**9,
        )

    related, down_other = [], []
    for i in each:
        related.append(relate(i, related[-1][:1] if related else ()))
        down_other.append(exchange(related[i][1]))
    sent_rel = send_owner(related[-1][0])
    fed_back, up_other = [], []
    for i in each:
        fed_back.append(feed_back(i, fed_back[-1][:2] if fed_back else ()))
        up_other.append(exchange(fed_back[i][3]))
    sent_feed = send_owner(fed_back[-1][0])
    attended_back = []
    for i in each:
        attended_back.append(attend_back(i, attended_back[-1] if attended_back else ()))
    sent_attn = send_owner(after(attended_back[-1][0], sent_rel, sent_feed))
    shard_rel, shard_feed = add_parts(sent_rel), add_parts(sent_feed)
    shard_in, shard_out = shard_feed[:, :hidden], shard_feed[:, hidden:]
    own, message = collect(sent_attn, jnp.sum(shard_feed * shard_feed) + jnp.sum(shard_rel * shard_rel), 6, 1.0 / cores)
    grad_norm = jnp.sqrt(jnp.sum(lax.all_to_all(message, ("dp", "ffn"), 0, 0, tiled=True)[:, 0]))
    other = swap(own, "ffn", 0)
    grad_rel = shard_rel.reshape(attn_b.shape)
    upper = core == 1
    low, high = jnp.where(upper, other, own), jnp.where(upper, own, other)
    columns = [
        half[:, start : start + flat] for start in range(0, 4 * flat, flat) for half in (low, high)
    ]
    grad_attn = jnp.concatenate(columns, axis=1)
    grad_vec = jnp.concatenate([(low + high)[:, 4 * flat : 4 * flat + 2], own[:, 4 * flat + 2 :]], axis=1)
    gradients = (grad_attn, shard_in, shard_out, grad_rel, grad_vec)
    clipped = jnp.minimum(1.0, CLIP_NORM / grad_norm)
    masters = (attn_a, ffn_in, ffn_out, attn_b, vec_d)
    firsts = (mom1_attn_a, mom1_ffn_in, mom1_ffn_out, mom1_attn_b, mom1_vec_d)
    seconds = (mom2_attn_a, mom2_ffn_in, mom2_ffn_out, mom2_attn_b, mom2_vec_d)
    rates = (RATE_MATRIX, RATE_MATRIX, RATE_MATRIX, RATE_MATRIX, RATE_VECTOR)
    decays = (DECAY_RATE, DECAY_RATE, DECAY_RATE, DECAY_RATE, 0.0)
    news = [
        adam_update(masters[i], gradients[i], firsts[i], seconds[i], clipped, rates[i], decays[i])
        for i in range(5)
    ]
    return (grad_norm, *(new[0] for new in news), *(new[1] for new in news), *(new[2] for new in news))


def solution(mesh):
    matrix = P("dp", None)
    halved = P("dp", "ffn")
    cube = P("dp", None, "ffn")
    trained = (matrix, halved, halved, cube, matrix)
    in_specs = (matrix, matrix, P("dp"), P("dp"), P(), P(None, None, "ffn")) + trained * 3
    out_specs = (P(),) + trained * 3
    return jax.shard_map(per_device, mesh=mesh, in_specs=in_specs, out_specs=out_specs, check_vma=False)
```

```python
import functools

import jax
import jax.numpy as jnp
from jax import lax
from jax.experimental import pallas as pl
from jax.experimental.pallas import tpu as pltpu
from jax.sharding import PartitionSpec as P

HEADS = 12
STEP = 10

NORM_EPSILON = 1e-12
CLIP_NORM = 1.0
BETA_ONE = 0.9
BETA_TWO = 0.999
ADAM_EPSILON = 1e-08
RATE_MATRIX = 0.04
RATE_VECTOR = 0.2
DECAY_RATE = 0.01
MASK_VALUE = -1e30
LOG2_E = 1.4426950408889634
BLOCK = 256
SAFE_EXPONENT = 100.0
HELD = -1
VMEM_BYTES = 24 * 2**20
F32 = jnp.float32
BF16 = jnp.bfloat16


def nn(left, right):
    return lax.dot_general(left, right, (((1,), (0,)), ((), ())), preferred_element_type=F32)


def nt(left, right):
    return lax.dot_general(left, right, (((1,), (1,)), ((), ())), preferred_element_type=F32)


def tn(left, right):
    return lax.dot_general(left, right, (((0,), (0,)), ((), ())), preferred_element_type=F32)


def lanes(block):
    return pl.ds(pl.multiple_of(block * BLOCK, BLOCK), BLOCK)


def live_blocks(len_ref):
    return (len_ref[0] + BLOCK - 1) // BLOCK


def for_keys(length, most, safe, body, spare=BLOCK // 2):
    sizes = [n * BLOCK for n in range(1, most)] + ([most * BLOCK - spare] if spare else []) + [most * BLOCK]
    for lower, keys in zip([0] + sizes, sizes):
        fits = jnp.logical_and(length > lower, length <= keys)
        pl.when(jnp.logical_and(safe, fits))(functools.partial(body, keys))


def for_size(length, most, safe, fast, slow, spare=BLOCK // 2):
    for_keys(length, most, safe, fast, spare)
    pl.when(jnp.logical_not(safe))(slow)


def pipeline(count, first, second, third):
    firsts, seconds = {}, {}
    for t in range(count + 2):
        if t < count:
            firsts[t] = first(t)
        if 0 <= t - 1 < count:
            seconds[t - 1] = second(t - 1, firsts.pop(t - 1))
        if 0 <= t - 2 < count:
            third(t - 2, seconds.pop(t - 2))


def staged(blocks, first, second):
    def step(block, held):
        ahead = first(block)
        second(block - 1, held)
        return ahead

    second(blocks - 1, lax.fori_loop(1, blocks, step, first(jnp.int32(0))))


def squared_lengths(flat, size):
    features = flat.shape[0]
    groups = -(-features // size // 8) * 8
    row = lax.broadcasted_iota(jnp.int32, (groups, features), 0)
    column = lax.broadcasted_iota(jnp.int32, (groups, features), 1)
    ones = jnp.where((column >= row * size) & (column < (row + 1) * size), 1.0, 0.0).astype(BF16)
    return nn(ones, flat * flat)


def clear_dead(blocks, rows, *refs):
    def step(block, carry):
        for ref in refs:
            ref[:, :, lanes(block)] = jnp.zeros(ref.shape[:2] + (BLOCK,), ref.dtype)
        return carry

    lax.fori_loop(blocks, rows // BLOCK, step, 0)


def norm_forward(resid):
    features = resid.shape[0]
    centred = resid - jnp.sum(resid, axis=0, keepdims=True) * (1.0 / features)
    variance = jnp.sum(centred * centred, axis=0, keepdims=True) * (1.0 / features)
    inverse = lax.rsqrt(variance + NORM_EPSILON)
    return centred * inverse, inverse


def norm_backward(scaled, normed, inverse):
    features = scaled.shape[0]
    mean = jnp.sum(scaled, axis=0, keepdims=True) * (1.0 / features)
    slope = jnp.sum(scaled * normed, axis=0, keepdims=True) * (1.0 / features)
    return inverse * (scaled - mean - normed * slope)


def mask_tail(scores, length, start=None):
    keys = scores.shape[0]
    start = keys - BLOCK if start is None else start
    rows = start + lax.broadcasted_iota(jnp.int32, (keys - start, scores.shape[1]), 0)
    tail = jnp.where(rows < length, scores[start:], MASK_VALUE)
    if start == 0:
        return tail
    return jnp.concatenate([scores[:start], tail], axis=0)


def pad_rows(part, index, count):
    zeros = jnp.zeros_like(part)
    return jnp.concatenate([part if i == index else zeros for i in range(count)], axis=0)


def pad_half(part, half):
    zeros = jnp.zeros_like(part)
    return jnp.concatenate([jnp.where(half == 0, part, zeros), jnp.where(half == 0, zeros, part)], axis=0)


def pad_lanes(pair, index, size):
    lane = lax.broadcasted_iota(jnp.int32, pair.shape, 1)
    return jnp.where((lane >= index * size) & (lane < (index + 1) * size), pair, jnp.zeros_like(pair))


def split_heads(flat, ref, columns, size):
    heads = flat.shape[0] // size
    for head in range(heads):
        ref[head, :, columns] = flat[head * size : (head + 1) * size]


def split_pairs(flat, ref, rows):
    pairs, width = ref.shape[0], ref.shape[2]
    for pair in range(pairs):
        ref[pair, rows, :] = flat[pair * width : (pair + 1) * width].T


def teacher_kernel(traffic, len_ref, rows_ref, weight_ref, qt_ref, k_ref, vt_ref, v_ref, bound_ref):
    size = qt_ref.shape[1]
    scaling = LOG2_E * size ** (-0.5)
    bound_ref[...] = jnp.zeros(bound_ref.shape, F32)

    def step(block, carry):
        where = lanes(block)
        traffic.take(block)
        rows = rows_ref[where, :]
        queries, keys, values = [nn(rows, weight_ref[index]) for index in range(3)]
        scaled = [(part * scaling).astype(BF16).T for part in (queries, values)]
        queries, keys, values = queries.astype(BF16), keys.astype(BF16), values.astype(BF16)
        columns = [scaled[0], keys.T, scaled[1]]
        bound_ref[...] = jnp.maximum(bound_ref[...], squared_lengths(jnp.concatenate(columns, axis=0), size))
        split_heads(columns[0], qt_ref, where, size)
        split_heads(columns[2], vt_ref, where, size)
        for pair in range(k_ref.shape[0]):
            k_ref[pair, where, :] = keys[:, 2 * size * pair : 2 * size * (pair + 1)]
            v_ref[pair, where, :] = values[:, 2 * size * pair : 2 * size * (pair + 1)]
        traffic.give(block, 0, 1, 2, 3)
        return carry

    lax.fori_loop(0, live_blocks(len_ref), step, 0)


def attend_kernel(
    traffic, len_ref, xt_ref, weight_ref, vec_ref, qt_ref, kt_ref, q_ref, k_ref, v_ref, ot_ref, lse_ref, at_ref,
    vone_ref, bound_ref,
):
    heads, size, rows = qt_ref.shape
    flat = heads * size
    scaling = LOG2_E * size ** (-0.5)
    blocks = live_blocks(len_ref)
    length = len_ref[0]
    bound_ref[...] = jnp.zeros(bound_ref.shape, F32)

    def project(block, carry):
        where = lanes(block)
        traffic.take(block)
        xt = xt_ref[:, where]
        projected = tn(weight_ref[:, : 3 * flat], xt)
        query = projected[:flat] + vec_ref[:, 0:1]
        scaled = (query * scaling).astype(BF16)
        query = query.astype(BF16)
        keys = projected[flat : 2 * flat].astype(BF16)
        values = (projected[2 * flat :] + vec_ref[:, 1:2]).astype(BF16)
        split_heads(scaled, qt_ref, where, size)
        split_heads(keys, kt_ref, where, size)
        bound_ref[...] = jnp.maximum(
            bound_ref[...], squared_lengths(jnp.concatenate([query, keys], axis=0), size)
        )
        column = block * BLOCK + lax.broadcasted_iota(jnp.int32, (1, BLOCK), 1)
        live = jnp.where(column < length, 1.0, 0.0)
        live_values = (values.astype(F32) * live).astype(BF16)
        for head in range(heads):
            vone_ref[head, :size, where] = live_values[head * size : (head + 1) * size]
            vone_ref[head, size:, where] = jnp.broadcast_to(live, (16, BLOCK)).astype(BF16)
        split_pairs(query, q_ref, where)
        split_pairs(keys, k_ref, where)
        split_pairs(values, v_ref, where)
        traffic.give(block, 0, 1, 2, 3, 4)
        return carry

    lax.fori_loop(0, blocks, project, 0)

    longest = jnp.max(bound_ref[...], axis=1, keepdims=True)
    safe = jnp.max(longest[:heads] * longest[heads : 2 * heads]) * scaling**2 <= SAFE_EXPONENT**2

    def scores(pair, half, where, keys):
        return nn(k_ref[pair, :keys, :], pad_rows(qt_ref[2 * pair + half, :, where], half, 2))

    def mix(head, where, keys, grown, top):
        mixed = nn(vone_ref[head, :, :keys], grown)
        total = mixed[size : size + 1]
        ot_ref[head, :, where] = mixed[:size] * (1.0 / total)
        lse_ref[head, :, where] = jnp.broadcast_to(top + jnp.log2(total), (8, BLOCK))

    def fast(keys):
        def step(block, carry):
            where = lanes(block)
            pipeline(
                heads,
                lambda head: scores(head // 2, head % 2, where, keys),
                lambda head, score: jnp.exp2(score).astype(BF16),
                lambda head, grown: mix(head, where, keys, grown, 0.0),
            )
            traffic.give(block, 5, 6)
            return carry

        lax.fori_loop(0, blocks, step, 0)

    def slow():
        clear_dead(blocks, rows, vone_ref)

        def step(index, carry):
            block, head = index // heads, index % heads
            where = lanes(block)
            score = nn(k_ref[head // 2], pad_half(qt_ref[head, :, where], head % 2))
            score = mask_tail(score, length, 0)
            top = jnp.max(score, axis=0, keepdims=True)
            mix(head, where, rows, jnp.exp2(score - top).astype(BF16), top)
            pl.when(head == heads - 1)(lambda: traffic.give(block, 5, 6))
            return carry

        lax.fori_loop(0, blocks * heads, step, 0)

    for_size(length, rows // BLOCK, safe, fast, slow)

    def output(block, carry):
        where = lanes(block)
        mixed = ot_ref[:, :, where].reshape(flat, BLOCK).astype(BF16)
        at_ref[:, where] = nn(weight_ref[:, 3 * flat :], mixed).astype(BF16)
        traffic.give(block, 7)
        return carry

    lax.fori_loop(0, blocks, output, 0)


def first_norm(xt, own, other, vec_ref):
    resid = xt.astype(F32) + (own.astype(F32) + other.astype(F32)) + vec_ref[:, 2:3]
    return norm_forward(resid)


def feed_kernel(traffic, len_ref, xt_ref, own_ref, other_ref, in_ref, out_ref, vec_ref, ht_ref, zt_ref, slope_ref, ft_ref):
    def first(block):
        where = lanes(block)
        traffic.take(block)
        normed, _ = first_norm(xt_ref[:, where], own_ref[:, where], other_ref[:, where], vec_ref)
        hidden = normed * vec_ref[:, 3:4] + vec_ref[:, 4:5]
        hidden = hidden.astype(BF16)
        ht_ref[:, where] = hidden
        return tn(in_ref[...], hidden)

    def second(block, pre):
        where = lanes(block)
        cdf = 0.5 + 0.5 * lax.erf(pre * (0.5**0.5))
        pdf = jnp.exp2(pre * pre * (-0.5 * LOG2_E)) * 0.3989422804014327
        active = (pre * cdf).astype(BF16)
        zt_ref[:, where] = active
        slope_ref[:, where] = (cdf + pre * pdf).astype(BF16)
        ft_ref[:, where] = nn(out_ref[...], active).astype(BF16)
        traffic.give(block, 0, 1, 2, 3)

    staged(live_blocks(len_ref), first, second)


def second_norm(ht, own, other, vec_ref):
    resid = ht.astype(F32) + (own.astype(F32) + other.astype(F32)) + vec_ref[:, 5:6]
    return norm_forward(resid)


def relation_kernel(
    chained, traffic, len_ref, weight_ref, ht_ref, own_ref, other_ref, rel_ref, vec_ref, tqt_ref, tk_ref, tvt_ref, tv_ref,
    tbound_ref, *refs,
):
    earlier_ref, refs = (refs[0], refs[1:]) if chained else (None, refs)
    grad_out_ref, dt_ref, refs = refs[0], refs[1], refs[2:]
    grad_ref, refs = refs[0], refs[1:]
    relation_body(
        traffic, len_ref, weight_ref, ht_ref, own_ref, other_ref, rel_ref, vec_ref, tqt_ref, tk_ref, tvt_ref, tv_ref,
        tbound_ref, grad_ref, dt_ref, *refs,
    )
    traffic.take_last()
    grad = grad_ref[...] + earlier_ref[...] if chained else grad_ref[...]
    grad_out_ref[...] = grad.astype(grad_out_ref.dtype)


def relation_body(
    traffic, len_ref, weight_ref, ht_ref, own_ref, other_ref, rel_ref, vec_ref, tqt_ref, tk_ref, tvt_ref, tv_ref,
    tbound_ref, grad_ref, dt_ref,
    h2_ref, qt_ref, kt_ref, vt_ref, st_ref, q_ref, k_ref, v_ref, dqt_ref, dvt_ref, dk_ref, dv_ref, bound_ref,
):
    heads, size, rows = qt_ref.shape
    teacher_size = tqt_ref.shape[1]
    flat = heads * size
    plain = size ** (-0.5)
    scaling = LOG2_E * plain
    teacher_scaling = LOG2_E * teacher_size ** (-0.5)
    blocks = live_blocks(len_ref)
    length = len_ref[0]
    weight = weight_ref[0]
    bound_ref[...] = jnp.zeros(bound_ref.shape, F32)

    def project(block, carry):
        where = lanes(block)
        traffic.take(block)
        normed, _ = second_norm(ht_ref[:, where], own_ref[:, where], other_ref[:, where], vec_ref)
        hidden = (normed * vec_ref[:, 6:7] + vec_ref[:, 7:8]).astype(BF16)
        h2_ref[:, where] = hidden
        projected = tn(rel_ref[...], hidden)
        split_heads((projected[:flat] * scaling).astype(BF16), qt_ref, where, size)
        split_heads((projected[2 * flat :] * scaling).astype(BF16), st_ref, where, size)
        projected = projected.astype(BF16)
        bound_ref[...] = jnp.maximum(bound_ref[...], squared_lengths(projected, size))
        split_heads(projected[flat : 2 * flat], kt_ref, where, size)
        split_heads(projected[2 * flat :], vt_ref, where, size)
        split_pairs(projected[:flat], q_ref, where)
        split_pairs(projected[flat : 2 * flat], k_ref, where)
        split_pairs(projected[2 * flat :], v_ref, where)
        for pair in range(heads // 2):
            dk_ref[pair, where, :] = jnp.zeros((BLOCK, 2 * size), F32)
            dv_ref[pair, where, :] = jnp.zeros((BLOCK, 2 * size), F32)
        return carry

    lax.fori_loop(0, blocks, project, 0)

    traffic.take_rest()

    def exponents(ref, attention_scale, relation_scale):
        longest = jnp.max(ref[...], axis=1, keepdims=True)
        attention = jnp.max(longest[:heads] * longest[heads : 2 * heads]) * attention_scale**2
        relation = jnp.max(longest[2 * heads : 3 * heads]) * relation_scale
        return jnp.logical_and(attention <= SAFE_EXPONENT**2, relation <= SAFE_EXPONENT)

    safe = jnp.logical_and(
        exponents(bound_ref, scaling, scaling), exponents(tbound_ref, 1.0, 1.0 / teacher_scaling)
    )
    pairs = heads // 2
    attention = (k_ref, qt_ref, q_ref, tk_ref, tqt_ref, kt_ref, dqt_ref, dk_ref)
    relation = (v_ref, st_ref, v_ref, tv_ref, tvt_ref, vt_ref, dvt_ref, dv_ref)
    tasks = [(half, refs) for refs in (attention, relation) for half in range(2)]

    def live_weight(where):
        column = where.start + lax.broadcasted_iota(jnp.int32, (1, BLOCK), 1)
        return jnp.where(column < length, weight, 0.0)

    def steps(keys, pair, where):
        live = live_weight(where)
        kept = {}

        def first(t):
            half, (left, rightt, _, teacher_left, teacher_rightt, _, _, _) = tasks[t]
            head = 2 * pair + half
            student = nn(left[pair, :keys, :], pad_rows(rightt[head, :, where], half, 2))
            teacher = nn(teacher_left[pair, :keys, :], pad_rows(teacher_rightt[head, :, where], half, 2))
            return student, teacher

        def second(t, scores):
            student, teacher = [jnp.exp2(mask_tail(score, length)) for score in scores]
            student_part = live / jnp.sum(student, axis=0, keepdims=True)
            teacher_part = live / jnp.sum(teacher, axis=0, keepdims=True)
            return (student * student_part - teacher * teacher_part).astype(BF16)

        def third(t, grad):
            half, (_, _, right, _, _, leftt, own_ref, running_ref) = tasks[t]
            head = 2 * pair + half
            own_ref[head, :, where] = (nn(leftt[head, :, :keys], grad) * plain).astype(own_ref.dtype)
            kept[half] = grad
            if half == 1:
                queries = right[pair, where, :]
                stacked = jnp.concatenate([pad_lanes(queries, i, size) for i in range(2)], axis=0)
                running_ref[pair, :keys, :] += nn(jnp.concatenate([kept[0], kept[1]], axis=1), stacked)

        return first, second, third

    def fast(keys):
        def step(index, carry):
            stages = steps(keys, index % pairs, lanes(index // pairs))
            pipeline(len(tasks), *stages)
            return carry

        lax.fori_loop(0, blocks * pairs, step, 0)

    def slow():
        clear_dead(blocks, rows, kt_ref, vt_ref)

        def step(index, carry):
            half, pair, where = index % 2, index // 2 % pairs, lanes(index // 2 // pairs)
            head = 2 * pair + half
            live = live_weight(where)
            for left, rightt, right, teacher_left, teacher_rightt, leftt, own_ref, running_ref in (attention, relation):
                parts = []
                for keys, queries in ((left, rightt), (teacher_left, teacher_rightt)):
                    score = mask_tail(nn(keys[pair], pad_half(queries[head, :, where], half)), length, 0)
                    grown = jnp.exp2(score - jnp.max(score, axis=0, keepdims=True))
                    parts.append(grown * (live / jnp.sum(grown, axis=0, keepdims=True)))
                grad = (parts[0] - parts[1]).astype(BF16)
                own_ref[head, :, where] = (nn(leftt[head], grad) * plain).astype(own_ref.dtype)
                running_ref[pair] += nn(grad, pad_lanes(right[pair, where, :], half, size))
            return carry

        lax.fori_loop(0, blocks * heads, step, 0)

    for_size(length, rows // BLOCK, safe, fast, slow)
    grad_ref[...] = jnp.zeros(grad_ref.shape, F32)

    def finish(block, carry):
        where = lanes(block)
        queries = dqt_ref[:, :, where].reshape(flat, BLOCK)
        keys = jnp.concatenate([dk_ref[pair, where, :].T for pair in range(heads // 2)], axis=0) * plain
        values = jnp.concatenate([dv_ref[pair, where, :].T for pair in range(heads // 2)], axis=0) * plain
        values = values + dvt_ref[:, :, where].reshape(flat, BLOCK)
        grads = jnp.concatenate([queries, keys.astype(BF16), values.astype(BF16)], axis=0)
        grad_ref[...] += nt(h2_ref[:, where], grads)
        dt_ref[:, where] = nn(rel_ref[...], grads).astype(BF16)
        traffic.give(block, 1)
        return carry

    lax.fori_loop(0, blocks, finish, 0)


def feed_back_kernel(
    chained, traffic, len_ref, ht_ref, own_ref, other_ref, down_own_ref, down_other_ref, zt_ref, slope_ref, in_ref, out_ref, vec_ref, *refs,
):
    earlier, refs = (refs[:2], refs[2:]) if chained else (None, refs)
    total_ref, sums_out_ref, resid_ref, up_ref, refs = *refs[:4], refs[4:]
    grad_ref, sums_ref = refs
    hidden_units = in_ref.shape[1]
    grad_ref[...] = jnp.zeros(grad_ref.shape, F32)
    sums_ref[...] = jnp.zeros(sums_ref.shape, F32)

    def first(block):
        where = lanes(block)
        traffic.take(block)
        normed, inverse = second_norm(ht_ref[:, where], own_ref[:, where], other_ref[:, where], vec_ref)
        grad = down_own_ref[:, where].astype(F32) + down_other_ref[:, where].astype(F32)
        resid = norm_backward(grad * vec_ref[:, 6:7], normed, inverse)
        resid_ref[:, where] = resid.astype(BF16)
        sums_ref[:, 0:1] += jnp.sum(resid, axis=1, keepdims=True)
        sums_ref[:, 1:2] += jnp.sum(grad * normed, axis=1, keepdims=True)
        sums_ref[:, 2:3] += jnp.sum(grad, axis=1, keepdims=True)
        return resid.astype(BF16)

    def second(block, branch):
        where = lanes(block)
        grad_ref[:, hidden_units:] += nt(branch, zt_ref[:, where])
        pre_grad = (tn(out_ref[...], branch) * slope_ref[:, where].astype(F32)).astype(BF16)
        grad_ref[:, :hidden_units] += nt(ht_ref[:, where], pre_grad)
        up_ref[:, where] = nn(in_ref[...], pre_grad).astype(BF16)
        traffic.give(block, 2, 3)

    staged(live_blocks(len_ref), first, second)
    traffic.take_last()
    grad, sums = grad_ref[...], sums_ref[...]
    if chained:
        grad, sums = grad + earlier[0][...], sums + earlier[1][...]
    total_ref[...] = grad.astype(total_ref.dtype)
    sums_out_ref[...] = sums


def attend_back_kernel(
    chained, last, traffic, len_ref, core_ref, xt_ref, own_ref, other_ref, resid_ref, up_own_ref, up_other_ref, weight_ref, vec_ref,
    qt_ref, kt_ref, q_ref, k_ref, v_ref, ot_ref, lse_ref, *refs,
):
    back_sums_ref, refs = (refs[0], refs[1:]) if last else (None, refs)
    earlier, refs = (refs[:3], refs[3:]) if chained else (None, refs)
    outs, refs = (refs[:1], refs[1:]) if last else (refs[:3], refs[3:])
    running, refs = refs[:3], refs[3:]
    grad_ref, sums_ref, head_sums_ref = running
    for ref in running:
        ref[...] = jnp.zeros(ref.shape, F32)
    attend_back_body(
        traffic, len_ref, xt_ref, own_ref, other_ref, resid_ref, up_own_ref, up_other_ref, weight_ref, vec_ref,
        qt_ref, kt_ref, q_ref, k_ref, v_ref, ot_ref, lse_ref, grad_ref, sums_ref, head_sums_ref, *refs,
    )
    traffic.take_last()
    if chained:
        for ref, value in zip(running, earlier):
            ref[...] += value[...]
    if not last:
        for ref, value in zip(outs, running):
            ref[...] = value[...]
        return
    total_ref = outs[0]
    columns, flat = grad_ref.shape[1], head_sums_ref.shape[0]
    total_ref[:, :columns] = grad_ref[...].astype(BF16)
    biases = head_sums_ref[:, 0:2].astype(BF16)
    total_ref[:, columns : columns + 2] = jnp.zeros((total_ref.shape[0], 2), BF16)
    for core in range(total_ref.shape[0] // flat):

        @pl.when(core_ref[0] == core)
        def _(core=core):
            total_ref[core * flat : (core + 1) * flat, columns : columns + 2] = biases

    total_ref[:, columns + 2 : columns + 5] = sums_ref[:, 0:3].astype(BF16)
    total_ref[:, columns + 5 : columns + 8] = back_sums_ref[:, 0:3].astype(BF16)


def attend_back_body(
    traffic, len_ref, xt_ref, own_ref, other_ref, resid_ref, up_own_ref, up_other_ref, weight_ref, vec_ref,
    qt_ref, kt_ref, q_ref, k_ref, v_ref, ot_ref, lse_ref, grad_ref, sums_ref, head_sums_ref,
    dot_ref, do_ref, inner_ref, dqt_ref, dk_ref, dv_ref,
):
    heads, size, rows = qt_ref.shape
    flat = heads * size
    plain = size ** (-0.5)
    scaling = LOG2_E * plain
    blocks = live_blocks(len_ref)
    length = len_ref[0]

    def start(block, carry):
        where = lanes(block)
        traffic.take(block)
        normed, inverse = first_norm(xt_ref[:, where], own_ref[:, where], other_ref[:, where], vec_ref)
        grad = resid_ref[:, where].astype(F32) + (up_own_ref[:, where].astype(F32) + up_other_ref[:, where].astype(F32))
        branch = norm_backward(grad * vec_ref[:, 3:4], normed, inverse).astype(BF16)
        sums_ref[:, 0:1] += jnp.sum(branch.astype(F32), axis=1, keepdims=True)
        sums_ref[:, 1:2] += jnp.sum(grad * normed, axis=1, keepdims=True)
        sums_ref[:, 2:3] += jnp.sum(grad, axis=1, keepdims=True)
        mixed = ot_ref[:, :, where]
        grad_ref[:, 3 * flat :] += nt(branch, mixed.reshape(flat, BLOCK).astype(BF16))
        mixed_grad = tn(weight_ref[:, 3 * flat :], branch).astype(BF16)
        split_heads(mixed_grad, dot_ref, where, size)
        split_pairs(mixed_grad, do_ref, where)
        for head in range(heads):
            product = mixed_grad[head * size : (head + 1) * size].astype(F32) * mixed[head]
            inner_ref[head, :, where] = jnp.broadcast_to(jnp.sum(product, axis=0, keepdims=True), (8, BLOCK))
        for pair in range(heads // 2):
            dk_ref[pair, where, :] = jnp.zeros((BLOCK, 2 * size), F32)
            dv_ref[pair, where, :] = jnp.zeros((BLOCK, 2 * size), F32)
        return carry

    lax.fori_loop(0, blocks, start, 0)
    traffic.take_rest()

    def attend(keys):
        def step(block, carry):
            where = lanes(block)
            kept = {}

            def first(head):
                pair, half = head // 2, head % 2
                scores = nn(k_ref[pair, :keys, :], pad_rows(qt_ref[head, :, where], half, 2))
                prob_grad = nn(v_ref[pair, :keys, :], pad_rows(dot_ref[head, :, where], half, 2))
                return scores, prob_grad

            def second(head, parts):
                scores, prob_grad = parts
                prob = jnp.exp2(mask_tail(scores, length) - lse_ref[head, 0:1, where])
                grad = (prob * (prob_grad - inner_ref[head, 0:1, where])).astype(BF16)
                return prob.astype(BF16), grad

            def third(head, parts):
                pair = head // 2
                dqt_ref[head, :, where] = (nn(kt_ref[head, :, :keys], parts[1]) * plain).astype(BF16)
                kept[head % 2] = parts
                if head % 2 == 1:
                    for index, right, running in ((1, q_ref, dk_ref), (0, do_ref, dv_ref)):
                        queries = right[pair, where, :]
                        stacked = jnp.concatenate([pad_lanes(queries, half, size) for half in range(2)], axis=0)
                        running[pair, :keys, :] += nn(
                            jnp.concatenate([kept[0][index], kept[1][index]], axis=1), stacked
                        )

            pipeline(heads, first, second, third)
            return carry

        lax.fori_loop(0, blocks, step, 0)

    for_keys(length, rows // BLOCK, True, attend, 0)

    def finish(block, carry):
        where = lanes(block)
        queries = dqt_ref[:, :, where].reshape(flat, BLOCK)
        keys = jnp.concatenate([dk_ref[pair, where, :].T for pair in range(heads // 2)], axis=0) * plain
        values = jnp.concatenate([dv_ref[pair, where, :].T for pair in range(heads // 2)], axis=0).astype(BF16)
        head_sums_ref[:, 0:1] += jnp.sum(queries.astype(F32), axis=1, keepdims=True)
        head_sums_ref[:, 1:2] += jnp.sum(values.astype(F32), axis=1, keepdims=True)
        grads = jnp.concatenate([queries, keys.astype(BF16), values], axis=0)
        grad_ref[:, : 3 * flat] += nt(xt_ref[:, where], grads)
        return carry

    lax.fori_loop(0, blocks, finish, 0)


class Traffic:
    def __init__(self, blocks, ins, outs, in_sems, out_sems):
        self.blocks, self.ins, self.outs, self.in_sems, self.out_sems = blocks, ins, outs, in_sems, out_sems

    def part(self, ref, axis, block):
        return ref if axis is None else ref.at[(slice(None),) * axis + (lanes(block),)]

    def inward(self, index, block):
        source, target, axis, _, first = self.ins[index]
        if axis is None:
            if first:
                source = source.at[:, first[0] : first[0] + first[1]]
            return pltpu.make_async_copy(source, target, self.in_sems.at[index, 0])
        return pltpu.make_async_copy(
            self.part(source, axis, first + block), self.part(target, axis, block), self.in_sems.at[index, block]
        )

    def outward(self, index, block):
        target, source, axis = self.outs[index]
        return pltpu.make_async_copy(
            self.part(source, axis, block), self.part(target, axis, block), self.out_sems.at[index, block]
        )

    def chosen(self, group, whole=False):
        return [i for i, entry in enumerate(self.ins) if (entry[2] is None) == whole and entry[3] == group]

    def start(self):
        for index in self.chosen(0, whole=True):
            self.inward(index, 0).start()
        for group in (0, 1):
            indices = self.chosen(group)

            def step(block, carry):
                for index in indices:
                    self.inward(index, block).start()
                return carry

            if indices:
                lax.fori_loop(0, self.blocks, step, 0)
        for index in self.chosen(1, whole=True):
            self.inward(index, 0).start()
        for index in self.chosen(0, whole=True):
            self.inward(index, 0).wait()

    def take(self, block):
        for index in self.chosen(0):
            self.inward(index, block).wait()

    def take_rest(self):
        def step(block, carry):
            for index in self.chosen(1):
                self.inward(index, block).wait()
            return carry

        lax.fori_loop(0, self.blocks, step, 0)

    def take_last(self):
        for index in self.chosen(1, whole=True):
            self.inward(index, 0).wait()

    def give(self, block, *indices):
        for index in indices:
            if self.outs[index][2] != HELD:
                self.outward(index, block).start()

    def finish(self):
        whole = [i for i, entry in enumerate(self.outs) if entry[2] is None]
        parts = [i for i, entry in enumerate(self.outs) if entry[2] not in (None, HELD)]
        for index in whole:
            self.outward(index, 0).start()

        def step(block, carry):
            for index in parts:
                self.outward(index, block).wait()
            return carry

        if parts:
            lax.fori_loop(0, self.blocks, step, 0)
        for index in whole:
            self.outward(index, 0).wait()


def call(blocks, kernel, name, scalars, arrays, outs, scratch=(), flops=0):
    smem = pl.BlockSpec(memory_space=pltpu.SMEM)
    hbm = pl.BlockSpec(memory_space=pltpu.HBM)
    vmem = pl.BlockSpec(memory_space=pltpu.VMEM)
    arrays = [entry if len(entry) == 4 else (*entry, 0) for entry in arrays]

    def held(array, axis, group, first):
        shape = list(array.shape)
        if axis is not None:
            shape[axis] = blocks * BLOCK
        elif first:
            shape[1] = first[1]
        return pltpu.VMEM(tuple(shape), array.dtype)

    count, ins, results = len(scalars), len(arrays), len(outs)
    copied = [i for i in range(ins) if arrays[i][2] != HELD]
    filled = [i for i in range(results) if outs[i][2] != HELD]

    def view(ref, axis, group, first):
        if group != HELD or not first:
            return ref
        if axis is None:
            return ref.at[:, first[0] : first[0] + first[1]]
        return ref.at[(slice(None),) * axis + (slice(first * BLOCK, (first + blocks) * BLOCK),)]

    def body(*refs):
        scalar_refs, refs = refs[:count], refs[count:]
        in_refs, refs = refs[:ins], refs[ins:]
        out_refs, refs = refs[:results], refs[results:]
        in_copies = [view(ref, *entry[1:]) for ref, entry in zip(in_refs, arrays)]
        for index, ref in zip(copied, refs):
            in_copies[index] = ref
        refs = refs[len(copied) :]
        out_copies = list(out_refs)
        for index, ref in zip(filled, refs):
            out_copies[index] = ref
        refs = refs[len(filled) :]
        in_sems, out_sems, refs = refs[0], refs[1], refs[2:]
        traffic = Traffic(
            live_blocks(scalar_refs[0]),
            [(in_refs[i], in_copies[i], *arrays[i][1:]) for i in copied],
            [(ref, copy, axis) for ref, copy, (_, _, axis) in zip(out_refs, out_copies, outs)],
            in_sems,
            out_sems,
        )
        traffic.start()
        kernel(traffic, *scalar_refs, *in_copies, *out_copies, *refs)
        traffic.finish()

    return pl.pallas_call(
        body,
        name=name,
        out_shape=tuple(
            (pltpu.VMEM if axis == HELD else pltpu.HBM)(shape, dtype) for shape, dtype, axis in outs
        ),
        in_specs=[smem] * count
        + [vmem if group == HELD else hbm for _, _, group, _ in arrays],
        out_specs=tuple(vmem if axis == HELD else hbm for _, _, axis in outs),
        scratch_shapes=[held(*arrays[i]) for i in copied]
        + [pltpu.VMEM(*outs[i][:2]) for i in filled]
        + [pltpu.SemaphoreType.DMA((ins, blocks)), pltpu.SemaphoreType.DMA((results, blocks))]
        + [pltpu.VMEM(shape, dtype) for shape, dtype in scratch],
        compiler_params=pltpu.CompilerParams(vmem_limit_bytes=VMEM_BYTES),
        cost_estimate=pl.CostEstimate(flops=flops, bytes_accessed=4 << 20, transcendentals=0),
    )(
        *scalars,
        *(
            pltpu.with_memory_space_constraint(array, pltpu.VMEM if group == HELD else pltpu.HBM)
            for array, _, group, _ in arrays
        ),
    )


def exchange(part):
    return swap(part, "ffn", 0)


def swap(value, axis, bit):
    count = lax.axis_size(axis)
    return lax.ppermute(value, axis, [(i, i ^ (1 << bit)) for i in range(count)])


def bit_of(axis, bit):
    return (lax.axis_index(axis) >> bit) & 1


def dp_bits():
    return lax.axis_size("dp").bit_length() - 1


def after(value, *others):
    return lax.optimization_barrier((value, *others))[0]


def gather_step(whole, other, bit):
    dim = dp_bits() - 1 - bit
    upper = bit_of("dp", bit) == 1
    return jnp.where(upper, jnp.concatenate([other, whole], axis=dim), jnp.concatenate([whole, other], axis=dim))


def gather_direct(shard, *tokens):
    count = lax.axis_size("dp")
    spread = after(jnp.broadcast_to(shard[None], (count,) + shard.shape), *tokens)
    return lax.all_to_all(spread, "dp", 0, 0, tiled=True).reshape((-1,) + shard.shape[1:])


def collect_kernel(shared_columns, shared_weight, squares_ref, spread_ref, own_ref, message_ref):
    own = spread_ref[0].astype(F32)
    for source in range(1, spread_ref.shape[0]):
        own = own + spread_ref[source].astype(F32)
    own_ref[...] = own
    column = lax.broadcasted_iota(jnp.int32, own.shape, 1)
    weights = jnp.where(column < own.shape[1] - shared_columns, 1.0, shared_weight)
    squares = jnp.sum(jnp.sum(own * own * weights, axis=0, keepdims=True), axis=1, keepdims=True)
    message_ref[...] = jnp.broadcast_to(squares + squares_ref[0], message_ref.shape)


def collect(spread, squares, shared_columns, shared_weight):
    vmem = pl.BlockSpec(memory_space=pltpu.VMEM)
    count = lax.axis_size("dp") * lax.axis_size("ffn")
    return pl.pallas_call(
        functools.partial(collect_kernel, shared_columns, shared_weight),
        name="collect",
        out_shape=(pltpu.VMEM(spread.shape[1:], F32), pltpu.VMEM((count, 128), F32)),
        in_specs=[pl.BlockSpec(memory_space=pltpu.SMEM), vmem],
        out_specs=(vmem, vmem),
    )(squares.reshape(1), pltpu.with_memory_space_constraint(spread, pltpu.VMEM))


def send_owner(value):
    count = lax.axis_size("dp")
    rows = value.shape[0] // count
    return lax.all_to_all(value.astype(BF16).reshape((count, rows) + value.shape[1:]), "dp", 0, 0, tiled=True)


def add_parts(spread):
    return jnp.sum(spread.astype(F32), axis=0)


def adam_update(weight, gradient, first, second, clipped, rate, decay):
    scaled = gradient * clipped
    first_new = BETA_ONE * first + (1.0 - BETA_ONE) * scaled
    second_new = BETA_TWO * second + (1.0 - BETA_TWO) * scaled * scaled
    ratio = (
        first_new
        / (1.0 - BETA_ONE**STEP)
        / (jnp.sqrt(second_new / (1.0 - BETA_TWO**STEP)) + ADAM_EPSILON)
    )
    return (weight - rate * (ratio + decay * weight), first_new, second_new)


def per_device(
    states, teacher_states, lengths, domain_ids, domain_weight, teacher_qkv,
    attn_a, ffn_in, ffn_out, attn_b, vec_d,
    mom1_attn_a, mom1_ffn_in, mom1_ffn_out, mom1_attn_b, mom1_vec_d,
    mom2_attn_a, mom2_ffn_in, mom2_ffn_out, mom2_attn_b, mom2_vec_d,
):
    cores = lax.axis_size("ffn")
    core = lax.axis_index("ffn")
    replicas = lax.axis_size("dp")
    replica = lax.axis_index("dp")
    sequences = lengths.shape[0]
    rows = states.shape[0] // sequences
    features = states.shape[1]
    heads = HEADS // cores
    flat = features // cores
    size = flat // heads
    pairs = heads // 2
    hidden = ffn_in.shape[1]
    teacher_flat = teacher_qkv.shape[2]
    teacher_size = teacher_flat // heads
    shard = attn_a.shape[0]
    matched = domain_ids[:, None] == jnp.arange(domain_weight.shape[0])[None, :]
    sequence_weight = jnp.sum(jnp.where(matched, domain_weight[None, :], 0.0), axis=1) / HEADS

    teacher_w = teacher_qkv.transpose(1, 0, 2)
    statest = states.T
    live = [lengths[i : i + 1] for i in range(sequences)]
    weights = [sequence_weight[i : i + 1] for i in range(sequences)]
    each = range(sequences)
    launch = functools.partial(call, rows // BLOCK)
    act = ((features, rows), BF16)
    head_t = ((heads, size, rows), BF16)
    pair_rows = ((pairs, rows, 2 * size), BF16)

    bound_rows = -(-3 * heads // 8) * 8

    def project_teacher(i, token):
        return launch(
            teacher_kernel, "teacher", (live[i],),
            ((after(teacher_states, *token), 0, 0, i * rows // BLOCK), (teacher_w, None, 0)),
            (
                ((heads, teacher_size, rows), BF16, 2),
                ((pairs, rows, 2 * teacher_size), BF16, 1),
                ((heads, teacher_size, rows), BF16, 2),
                ((pairs, rows, 2 * teacher_size), BF16, 1),
                ((bound_rows, BLOCK), F32, None),
            ),
            flops=2 * rows * 768 * 1152,
        )

    attn_own = [lax.dynamic_slice_in_dim(attn_a, start + core * flat, flat, 1) for start in range(0, 4 * features, features)]
    early = gather_direct(jnp.concatenate([*attn_own, vec_d], axis=1).astype(BF16))
    teacher = [project_teacher(i, (statest,)) for i in each]
    late_feed = gather_direct(jnp.concatenate([ffn_in, ffn_out], axis=1).astype(BF16), *teacher[0], *teacher[1])
    early = after(early, *teacher[0], *teacher[1])
    vec_full = early[:, 4 * flat :].astype(F32)
    vec_own = lax.dynamic_slice_in_dim(vec_full, core * flat, flat, 0)
    attn_full = (early, None, 0, (0, 4 * flat))

    attended = [
        launch(
            attend_kernel, "attend", (live[i],),
            ((statest, 1, 0, i * rows // BLOCK), attn_full, (vec_own, None, 0)),
            ((*head_t, 2), (*head_t, 2), (*pair_rows, 1), (*pair_rows, 1), (*pair_rows, 1),
             ((heads, size, rows), F32, 2), ((heads, 8, rows), F32, 2), (*act, 1)),
            scratch=(((heads, size + 16, rows), BF16), ((-(-2 * heads // 8) * 8, BLOCK), F32)),
            flops=6 * 10**9,
        )
        for i in each
    ]
    in_full, out_full = (late_feed, None, 0, (0, hidden)), (late_feed, None, 0, (hidden, hidden))
    late_rel = gather_direct(after(attn_b.reshape(shard, 3 * flat).astype(BF16), *attended[0]))
    rel_full = (late_rel, None, 0)
    mixed_other = [exchange(attended[i][7]) for i in each]
    fed = [
        launch(
            feed_kernel, "feed", (live[i],),
            ((statest, 1, 0, i * rows // BLOCK), (attended[i][7], 1, 0), (mixed_other[i], 1, HELD), in_full,
             out_full, (vec_full, None, 0)),
            ((*act, 1), ((hidden, rows), BF16, 1), ((hidden, rows), BF16, 1), (*act, 1)),
            flops=3 * 10**9,
        )
        for i in each
    ]
    fed_other = [exchange(fed[i][3]) for i in each]

    def relate(i, earlier):
        last = i + 1 == sequences
        return launch(
            functools.partial(relation_kernel, bool(earlier)), "relation", (live[i], weights[i]),
            ((fed[i][0], 1, 0), (fed[i][3], 1, 0), (fed_other[i], 1, HELD), rel_full,
             (vec_full, None, 0), (teacher[i][0], 2, 1), (teacher[i][1], 1, 1), (teacher[i][2], 2, 1),
             (teacher[i][3], 1, 1), (teacher[i][4], None, 0), *((value, None, HELD) for value in earlier)),
            (((features, 3 * flat), BF16 if last else F32, HELD), (*act, 1)),
            scratch=(
                ((features, 3 * flat), F32), act, head_t, head_t, head_t, head_t, pair_rows, pair_rows, pair_rows,
                head_t, ((heads, size, rows), F32),
                ((pairs, rows, 2 * size), F32), ((pairs, rows, 2 * size), F32), ((bound_rows, BLOCK), F32),
            ),
            flops=30 * 10**9,
        )

    def feed_back(i, earlier):
        last = i + 1 == sequences
        sums = ((features, 8), F32)
        return launch(
            functools.partial(feed_back_kernel, bool(earlier)), "feed_back", (live[i],),
            ((fed[i][0], 1, 0), (fed[i][3], 1, 0), (fed_other[i], 1, 0), (related[i][1], 1, 0),
             (down_other[i], None, HELD), (fed[i][1], 1, 0), (fed[i][2], 1, 0), in_full,
             out_full, (vec_full, None, 0), *((value, None, HELD) for value in earlier)),
            (((features, 2 * hidden), BF16 if last else F32, HELD), (*sums, HELD), (*act, HELD), (*act, HELD)),
            scratch=(((features, 2 * hidden), F32), sums),
            flops=4 * 10**9,
        )

    def attend_back(i, earlier):
        last = i + 1 == sequences
        running = (((features, 4 * flat), F32), ((features, 8), F32), ((flat, 8), F32))
        return launch(
            functools.partial(attend_back_kernel, bool(earlier), last), "attend_back",
            (live[i], core.reshape(1).astype(jnp.int32)),
            ((statest, 1, 0, i * rows // BLOCK), (attended[i][7], 1, 0), (mixed_other[i], 1, 0), (fed_back[i][2], 1, HELD),
             (fed_back[i][3], 1, HELD), (up_other[i], None, HELD), attn_full, (vec_full, None, 0),
             (attended[i][0], 2, 1), (attended[i][1], 2, 1), (attended[i][2], 1, 1), (attended[i][3], 1, 1),
             (attended[i][4], 1, 1), (attended[i][5], 2, 0), (attended[i][6], 2, 1),
             *([(fed_back[i][1], None, HELD)] if last else []), *((value, None, HELD) for value in earlier)),
            (((features, 4 * flat + 8), BF16, HELD),) if last else tuple((*spec, HELD) for spec in running),
            scratch=running + (
                head_t, pair_rows, ((heads, 8, rows), F32), head_t,
                ((pairs, rows, 2 * size), F32), ((pairs, rows, 2 * size), F32),
            ),
            flops=15 * 10**9,
        )

    related, down_other = [], []
    for i in each:
        related.append(relate(i, related[-1][:1] if related else ()))
        down_other.append(exchange(related[i][1]))
    sent_rel = send_owner(related[-1][0])
    fed_back, up_other = [], []
    for i in each:
        fed_back.append(feed_back(i, fed_back[-1][:2] if fed_back else ()))
        up_other.append(exchange(fed_back[i][3]))
    sent_feed = send_owner(fed_back[-1][0])
    attended_back = []
    for i in each:
        attended_back.append(attend_back(i, attended_back[-1] if attended_back else ()))
    sent_attn = send_owner(after(attended_back[-1][0], sent_rel, sent_feed))
    shard_rel, shard_feed = add_parts(sent_rel), add_parts(sent_feed)
    shard_in, shard_out = shard_feed[:, :hidden], shard_feed[:, hidden:]
    own, message = collect(sent_attn, jnp.sum(shard_feed * shard_feed) + jnp.sum(shard_rel * shard_rel), 6, 1.0 / cores)
    grad_norm = jnp.sqrt(jnp.sum(lax.all_to_all(message, ("dp", "ffn"), 0, 0, tiled=True)[:, 0]))
    other = swap(own, "ffn", 0)
    grad_rel = shard_rel.reshape(attn_b.shape)
    upper = core == 1
    low, high = jnp.where(upper, other, own), jnp.where(upper, own, other)
    columns = [
        half[:, start : start + flat] for start in range(0, 4 * flat, flat) for half in (low, high)
    ]
    grad_attn = jnp.concatenate(columns, axis=1)
    grad_vec = jnp.concatenate([(low + high)[:, 4 * flat : 4 * flat + 2], own[:, 4 * flat + 2 :]], axis=1)
    gradients = (grad_attn, shard_in, shard_out, grad_rel, grad_vec)
    clipped = jnp.minimum(1.0, CLIP_NORM / grad_norm)
    masters = (attn_a, ffn_in, ffn_out, attn_b, vec_d)
    firsts = (mom1_attn_a, mom1_ffn_in, mom1_ffn_out, mom1_attn_b, mom1_vec_d)
    seconds = (mom2_attn_a, mom2_ffn_in, mom2_ffn_out, mom2_attn_b, mom2_vec_d)
    rates = (RATE_MATRIX, RATE_MATRIX, RATE_MATRIX, RATE_MATRIX, RATE_VECTOR)
    decays = (DECAY_RATE, DECAY_RATE, DECAY_RATE, DECAY_RATE, 0.0)
    news = [
        adam_update(masters[i], gradients[i], firsts[i], seconds[i], clipped, rates[i], decays[i])
        for i in range(5)
    ]
    return (grad_norm, *(new[0] for new in news), *(new[1] for new in news), *(new[2] for new in news))


def solution(mesh):
    matrix = P("dp", None)
    halved = P("dp", "ffn")
    cube = P("dp", None, "ffn")
    trained = (matrix, halved, halved, cube, matrix)
    in_specs = (matrix, matrix, P("dp"), P("dp"), P(), P(None, None, "ffn")) + trained * 3
    out_specs = (P(),) + trained * 3
    return jax.shard_map(per_device, mesh=mesh, in_specs=in_specs, out_specs=out_specs, check_vma=False)
```
